128 devices in a mesh: blk: 32 (over x, z, core), hd: 4 (over y).
Axes of the slice: x: 4, y: 4, z: 4, core: 2. Of those that a mesh axis runs over, the one named last changes fastest.
Arguments:
- tokens: bfloat16 [16384, 768], P(('blk', 'hd')), may hold values from -6 to 6
- attn_gain: bfloat16 [768], P(('blk', 'hd')), may hold values from 0.099609375 to 1.8984375
- w_query: bfloat16 [768, 768], P(('blk', 'hd')), may hold values from -0.21875 to 0.21875
- w_key: bfloat16 [768, 768], P(('blk', 'hd')), may hold values from -0.21875 to 0.21875
- w_value: bfloat16 [768, 768], P(('blk', 'hd')), may hold values from -0.21875 to 0.21875
- w_out: bfloat16 [768, 768], P(('blk', 'hd')), may hold values from -0.875 to 0.875
- mlp_gain: bfloat16 [768], P(('blk', 'hd')), may hold values from 0.099609375 to 1.8984375
- w_gate: bfloat16 [768, 2048], P(('blk', 'hd')), may hold values from -0.21875 to 0.21875
- w_up: bfloat16 [768, 2048], P(('blk', 'hd')), may hold values from -0.21875 to 0.21875
- w_down: bfloat16 [2048, 768], P(('blk', 'hd')), may hold values from -0.125 to 0.125
- segments: int32 [16384], replicated, may hold values from 0 to 24, as said below
- teacher: bfloat16 [16384, 768], P(('blk', 'hd')), may hold values from -6 to 6
Outputs:
- output: bfloat16 [16384, 768], P(('blk', 'hd'))
- grad_tokens: bfloat16 [16384, 768], P(('blk', 'hd'))
- mean_loss: float32 [], replicated
- grad_attn_gain: float32 [768], P(('blk', 'hd'))
- grad_query: float32 [768, 768], P(('blk', 'hd'))
- grad_key: float32 [768, 768], P(('blk', 'hd'))
- grad_value: float32 [768, 768], P(('blk', 'hd'))
- grad_out: float32 [768, 768], P(('blk', 'hd'))
- grad_mlp_gain: float32 [768], P(('blk', 'hd'))
- grad_gate: float32 [768, 2048], P(('blk', 'hd'))
- grad_up: float32 [768, 2048], P(('blk', 'hd'))
- grad_down: float32 [2048, 768], P(('blk', 'hd'))
The draws below stay inside these ranges and needn't reach their ends.
Inputs may be any that keep to these rules, and one draw needn't show every extreme that they name: `segments`: along the tokens the segment numbers are 1, 2, ..., 24 in this order, each over a run of one or more tokens, followed by a run of one or more zeros that ends the sequence.
All inputs are finite; a program needn't handle non-finite values.
Results may differ from the reference program's by a relative error of at most 0.019.
Values may be sent and summed in bfloat16 or wider, within the bound.
No kernel may reach another device: no remote copies, remote signals or barrier semaphores. Data moves between devices by JAX's collectives and lax.ppermute only.
A program may use at most 192 MiB of HBM per device.

```python
import math
import jax
import jax.numpy as jnp
from jax import lax

D = 768
HEADS = 12
KV_HEADS = 12
HEAD_SIZE = 64
FF = 2048
DOCS = 24
BLOCK = 512
TOKENS = 16384


def draw_segments(key, part):
    key = jax.random.fold_in(key, 11)
    split_keys = jax.random.split(key, 5)
    exponents = jax.random.randint(split_keys[0], (DOCS,), 0, 10)
    lowest = jnp.left_shift(jnp.ones((DOCS,), jnp.int32), exponents.astype(jnp.int32))
    doc_weights = jax.random.randint(split_keys[1], (DOCS,), lowest, 2 * lowest).astype(jnp.int32)
    long_index = jax.random.randint(split_keys[2], (), 0, DOCS)
    is_long = jnp.arange(DOCS, dtype=jnp.int32) == long_index
    others = jnp.sum(jnp.where(is_long, 0, doc_weights)).astype(jnp.int32)
    extra = jax.random.randint(split_keys[3], (), others // 2, others + 1).astype(jnp.int32)
    doc_weights = jnp.where(is_long, others + extra, doc_weights).astype(jnp.int32)
    padding = jax.random.randint(split_keys[4], (), 1, BLOCK // 2 + 1).astype(jnp.int32)
    filled = TOKENS - padding
    spare = filled - DOCS
    weight_total = jnp.sum(doc_weights).astype(jnp.int32)
    lengths = (1 + doc_weights * spare // weight_total).astype(jnp.int32)
    lengths = lengths + jnp.where(is_long, filled - jnp.sum(lengths), 0).astype(jnp.int32)
    ends = jnp.cumsum(lengths).astype(jnp.int32)
    position = jnp.arange(TOKENS, dtype=jnp.int32)
    labels = 1 + jnp.sum((ends[None, :] <= position[:, None]).astype(jnp.int32), axis=1)
    labels = jnp.where(position < filled, labels, 0)
    return labels.astype(jnp.int32)


def levels(own_key, dims, shards, low, top_value):
    gain = 1.0
    for axis_at, blocks in shards:
        draws = jax.random.uniform(jax.random.fold_in(jax.random.fold_in(own_key, 6), axis_at), (blocks,), jnp.float32, low / len(shards), top_value / len(shards))
        gain = gain * jnp.repeat(jnp.exp(draws), dims[axis_at] // blocks).reshape((-1,) + (1,) * (len(dims) - 1 - axis_at))
    return gain


def normal_values(stream_key, shape, spread, bound, cuts=(), kind=jnp.bfloat16):
    loudness = levels(stream_key, shape, cuts, -0.22, 0.18) if cuts else 1.0
    drawn = jax.random.normal(stream_key, shape, jnp.float32) * spread * loudness
    return jnp.minimum(jnp.maximum(drawn, -bound), bound).astype(kind)


def setup_inputs(seed: int = 0) -> dict:
    streams_of = jax.random.split(jax.random.key(seed), 13)
    return {
        "tokens": normal_values(streams_of[0], (TOKENS, D), 1.0, 6.0, ((0, 128),)),
        "attn_gain": jnp.clip(1.0 + 0.18 * jax.random.normal(streams_of[1], (D,), jnp.float32), 0.099609375, 1.8984375).astype(jnp.bfloat16),
        "w_query": normal_values(streams_of[2], (D, HEADS * HEAD_SIZE), D ** -0.5, 0.21875, ((0, 128),)),
        "w_key": normal_values(streams_of[3], (D, KV_HEADS * HEAD_SIZE), D ** -0.5, 0.21875, ((0, 128),)),
        "w_value": normal_values(streams_of[4], (D, KV_HEADS * HEAD_SIZE), D ** -0.5, 0.21875, ((0, 128),)),
        "w_out": normal_values(streams_of[5], (HEADS * HEAD_SIZE, D), (max(16, HEADS * HEAD_SIZE // 16)) ** -0.5, 0.875, ((0, 128),)),
        "mlp_gain": jnp.clip(1.0 + 0.18 * jax.random.normal(streams_of[6], (D,), jnp.float32), 0.099609375, 1.8984375).astype(jnp.bfloat16),
        "w_gate": normal_values(streams_of[7], (D, FF), D ** -0.5, 0.21875, ((0, 128),)),
        "w_up": normal_values(streams_of[8], (D, FF), D ** -0.5, 0.21875, ((0, 128),)),
        "w_down": normal_values(streams_of[9], (FF, D), FF ** -0.5, 0.125, ((0, 128),)),
        "segments": draw_segments(jax.random.fold_in(streams_of[12], 71), 0),
        "teacher": normal_values(streams_of[11], (TOKENS, D), 1.0, 6.0, ((0, 128),)),
    }


@jax.custom_vjp
def low(v):
    return lax.optimization_barrier(v.astype(jnp.bfloat16)).astype(jnp.float32)

@jax.custom_vjp
def low_back(v):
    return v

def low_keep(v):
    return (low(v), None)

def low_pass(kept, grad):
    return (grad,)

def back_keep(v):
    return (v, None)

def back_low(kept, grad):
    return (low(grad),)
low.defvjp(low_keep, low_pass)
low_back.defvjp(back_keep, back_low)
EPSILON = 1e-05
ROPE_BASE = 10000.0
MASKED_SCORE = -1e+30

def root_norm(inputs, norm_gain):
    return inputs * lax.rsqrt(lax.optimization_barrier(jnp.mean(inputs * inputs, axis=-1, keepdims=True)) + EPSILON) * norm_gain

def rotate(vectors, positions):
    head_width = vectors.shape[-1]
    half_width = head_width // 2
    exponents = jnp.arange(half_width, dtype=jnp.float32) * (-2.0 / head_width)
    frequency = ROPE_BASE ** exponents
    angles = positions.astype(jnp.float32)[:, None] * frequency[None, :]
    cosine = jnp.cos(angles)[:, None, :]
    sine_part = jnp.sin(angles)[:, None, :]
    first_half = vectors[..., :half_width]
    second_half = vectors[..., half_width:]
    return jnp.concatenate([first_half * cosine - second_half * sine_part, second_half * cosine + first_half * sine_part], axis=-1)

def matmul(left_side, right_side):
    return jnp.dot(left_side, right_side, precision=lax.Precision.HIGHEST, preferred_element_type=jnp.float32)

def attention(queries, keys, values, segments):
    query_rows = math.gcd(TOKENS, 512)
    block_count = TOKENS // query_rows
    group_size = HEADS // KV_HEADS
    scale_factor = HEAD_SIZE ** (-0.5)
    positions = jnp.arange(TOKENS, dtype=jnp.int32)
    grouped = queries.reshape(TOKENS, KV_HEADS, group_size, HEAD_SIZE).transpose(1, 0, 2, 3)
    grouped = grouped.reshape(KV_HEADS, block_count, query_rows, group_size, HEAD_SIZE)
    key_heads = keys.transpose(1, 0, 2)
    value_heads = values.transpose(1, 0, 2)

    def one_head(carried):
        query_blocks, head_keys, head_values = carried

        def one_block(block_item):
            query_block, block_index = block_item
            starting = block_index * query_rows
            query_places = starting + jnp.arange(query_rows, dtype=jnp.int32)
            query_segments = lax.dynamic_slice_in_dim(segments, starting, query_rows, 0)
            raw_scores = jnp.einsum('qgd,sd->gqs', query_block, head_keys, precision=lax.Precision.HIGHEST)
            scores = low_back(raw_scores * scale_factor)
            allowed = (query_segments[:, None] == segments[None, :]) & (positions[None, :] <= query_places[:, None])
            masked = jnp.where(allowed, scores, MASKED_SCORE)
            highest = lax.optimization_barrier(jnp.max(masked, axis=-1, keepdims=True))
            weights = jnp.where(allowed, jnp.exp(masked - highest), 0.0)
            probabilities = weights / lax.optimization_barrier(jnp.sum(weights, axis=-1, keepdims=True))
            return jnp.einsum('gqs,sd->qgd', low(probabilities), head_values, precision=lax.Precision.HIGHEST)
        return lax.map(jax.checkpoint(one_block), (query_blocks, jnp.arange(block_count, dtype=jnp.int32)))
    mixed = lax.map(one_head, (grouped, key_heads, value_heads))
    return mixed.transpose(1, 2, 0, 3, 4).reshape(TOKENS, HEADS * HEAD_SIZE)

def layer_forward(tokens, attn_gain, w_query, w_key, w_value, w_out, mlp_gain, w_gate, w_up, w_down, segments, teacher):
    positions = jnp.arange(TOKENS, dtype=jnp.int32)
    normed = low(root_norm(tokens, attn_gain))
    query_linear = low_back(matmul(normed, w_query))
    key_linear = low_back(matmul(normed, w_key))
    value_linear = matmul(normed, w_value)
    queries = low_back(low(rotate(query_linear.reshape(TOKENS, HEADS, HEAD_SIZE), positions)))
    keys = low_back(low(rotate(key_linear.reshape(TOKENS, KV_HEADS, HEAD_SIZE), positions)))
    values = low_back(low(value_linear.reshape(TOKENS, KV_HEADS, HEAD_SIZE)))
    mixed = low_back(low(attention(queries, keys, values, segments)))
    middle = tokens + low_back(matmul(mixed, w_out))
    normed_mid = low(root_norm(middle, mlp_gain))
    gate_pre = low_back(matmul(normed_mid, w_gate))
    upward = low_back(matmul(normed_mid, w_up))
    hidden = low(jax.nn.silu(gate_pre) * upward)
    output = middle + low_back(matmul(hidden, w_down))
    valid_mask = (segments != 0).astype(jnp.float32)
    counted = jnp.sum(valid_mask)
    squared_error = jnp.sum(valid_mask[:, None] * (output - teacher) ** 2)
    mean_loss = squared_error / (counted * D)
    return (mean_loss * (TOKENS * D * 0.5), (output, mean_loss))

def reference(tokens, attn_gain, w_query, w_key, w_value, w_out, mlp_gain, w_gate, w_up, w_down, segments, teacher):
    floats = tuple((argument.astype(jnp.float32) for argument in (tokens, attn_gain, w_query, w_key, w_value, w_out, mlp_gain, w_gate, w_up, w_down)))
    target = teacher.astype(jnp.float32)

    def objective(params):
        return layer_forward(*params, segments, target)
    scaled, pullback, extras = jax.vjp(objective, floats, has_aux=True)
    gradients, = pullback(jnp.ones_like(scaled))
    output, mean_loss = extras
    return (output.astype(jnp.bfloat16), gradients[0].astype(jnp.bfloat16), mean_loss, gradients[1], gradients[2], gradients[3], gradients[4], gradients[5], gradients[6], gradients[7], gradients[8], gradients[9])
```

```python
import jax
import jax.numpy as jnp
from jax import lax
from jax.experimental import pallas as pl
from jax.experimental.pallas import tpu as pltpu
from jax.sharding import Mesh
from jax.sharding import PartitionSpec as P

HEADS = 12
HEAD_SIZE = 64
D = 768
FF = 2048
EPSILON = 1e-05
ROPE_BASE = 10000.0
X, Z, C, Y = "blk_0", "blk_1", "blk_2", "hd"
BLK = (X, Z, C)
BLK_HD = (X, Z, C, Y)
WIDE = 640

BF = jnp.bfloat16
F32 = jnp.float32
NEG = -1e30
LABEL_LANE = 72
LABELS = 25
NT = (((1,), (1,)), ((), ()))
TN = (((0,), (0,)), ((), ()))
NN = (((1,), (0,)), ((), ()))
LIMIT = 70.0


def mm(a, b, dims=NN):
    return lax.dot_general(a, b, dims, preferred_element_type=F32)


def lanes(rows):
    return lax.broadcasted_iota(jnp.int32, (rows, 128), 1)


def rows_of(rows):
    return lax.broadcasted_iota(jnp.int32, (rows, 128), 0)


def lane_masks():
    lane = lanes(128)
    low = (lane < 64).astype(F32)
    head = rows_of(128) // 64
    first = (head == lane).astype(F32).astype(BF)
    second = ((head == 0) & (lane == 2)).astype(F32).astype(BF)
    return low.astype(BF), (1.0 - low).astype(BF), first, second


def one_lane(n):
    return (lanes(128) == n).astype(F32).astype(BF)


def stage_keys(meta, lab, own, oth, kaug, other):
    ix, iz, ic, iy = (meta[k] for k in range(4))
    lane = lanes(128)
    row = rows_of(128)
    first, last = lab[0:1, :], lab[1:2, :]
    one = ((lane >= 64) & (lane < 66)).astype(F32)
    low, _, _, _ = lane_masks()

    def place(i, _):
        for j in range(4):
            ki = ((ix - i) & 3) * 4 + ((iz - j) & 3)
            for ref, core in ((own[j], ic), (oth[j], 1 - ic)):
                at = pl.multiple_of(ki * 256 + core * 128, 128)
                k0, k1, v1 = (ref[i, :, 128 * n : 128 * n + 128] for n in range(3))
                place_at = ki * 1024 + core * 512 + iy * 128 + row
                outside = (place_at < first) | (place_at >= last)
                half = k1 * low
                kaug[pl.ds(at, 128), 0:128] = k0
                kaug[pl.ds(at, 128), 128:256] = half + jnp.where(outside, NEG, one).astype(BF)
                other(at, k0, half, k1, v1)
        return 0

    lax.fori_loop(0, 4, place, 0)


def split_two(x):
    hi = x.astype(BF).astype(F32)
    return hi, x - hi


def fwd_kernel(meta, lab, *refs):
    q_refs, kv_own, kv_oth = refs[0:4], refs[4:8], refs[8:12]
    out_ref, kaug, vbd, qm, acc = refs[12:]
    ix, iz, ic, iy = (meta[k] for k in range(4))
    lane = lanes(128)
    first, last = lab[0:1, :], lab[1:2, :]
    is_label = (lane >= LABEL_LANE) & (lane < LABEL_LANE + LABELS)
    zeros = jnp.zeros((128, 128), BF)
    low, high, by_head0, by_head1 = lane_masks()
    ones = [one_lane(h) for h in range(3)]

    def value_rows(at, k0, half, k1, v1):
        t = at // 256
        inner = pl.multiple_of(at % 256, 128)
        rows = [pl.ds(256 * h + inner, 128) for h in range(3)]
        vbd[t, rows[0], 0:128] = k1 * high + ones[0]
        vbd[t, rows[0], 128:256] = zeros
        vbd[t, rows[1], 0:128] = ones[1]
        vbd[t, rows[1], 128:256] = v1 * low
        vbd[t, rows[2], 0:128] = ones[2]
        vbd[t, rows[2], 128:256] = v1 * high

    stage_keys(meta, lab, kv_own, kv_oth, kaug, value_rows)
    key_norms = query_norms = jnp.zeros((1, 128), F32)
    for n in range(4):
        for ref, at in ((kaug, pl.ds(1024 * n, 1024)), (q_refs[n], slice(None))):
            whole = ref[at].reshape(-1, 256)
            v0, v1 = whole[:, 0:128], whole[:, 128:256] * low[0:1, :]
            norms = mm(v0 * v0, by_head0) + mm(v1 * v1, by_head1)
            norms = jnp.max(norms, axis=0, keepdims=True)
            if ref is kaug:
                key_norms = jnp.maximum(key_norms, norms)
            else:
                query_norms = jnp.maximum(query_norms, norms)
    bound = key_norms * query_norms
    small = jnp.max(bound) < LIMIT * LIMIT

    def one_run(xr, _):
        i = (ix - xr) & 3
        begin = xr * 4096 + iz * 1024 + ic * 512
        for j in range(4):
            yq = (iy - j) & 3
            q0, q1 = q_refs[j][i, :, 0:128], q_refs[j][i, :, 128:256]
            place = begin + yq * 128 + rows_of(128)
            mine = is_label & (place >= first) & (place < last)
            label = jnp.where(mine, 1.0, 0.0).astype(BF)
            at = [pl.ds(pl.multiple_of(512 * h + yq * 128, 128), 128) for h in range(3)]
            qm[at[0], 0:128] = q0 * low
            qm[at[0], 128:256] = label
            qm[at[1], 0:128] = q0 * high
            qm[at[1], 128:256] = label
            qm[at[2], 0:128] = zeros
            qm[at[2], 128:256] = q1 * low + label
        start = meta[4 + xr]
        end = xr * 4 + iz

        def allowed_keys(t):
            key_row = lax.broadcasted_iota(jnp.int32, (256, 512), 0)
            key_place = t * 1024 + iy * 128 + key_row + jnp.where(key_row >= 128, 512 - 128, 0)
            return key_place <= begin + lax.broadcasted_iota(jnp.int32, (256, 512), 1)

        acc[...] = jnp.zeros((512, 256), F32)

        def fast(tiles, diagonal):
            probs = []
            for t in tiles:
                s = mm(qm[...], kaug[pl.ds(pl.multiple_of(t * 256, 256), 256), :], NT)
                if diagonal:
                    key_lane = lax.broadcasted_iota(jnp.int32, (512, 256), 1)
                    key_place = t * 1024 + iy * 128 + key_lane + jnp.where(key_lane >= 128, 512 - 128, 0)
                    allowed = key_place <= begin + lax.broadcasted_iota(jnp.int32, (512, 256), 0)
                for h in range(3):
                    part = s[512 * h : 512 * h + 512]
                    if diagonal:
                        part = jnp.where(allowed, part, NEG)
                    probs.append(jnp.exp(part).astype(BF))
            probs = jnp.concatenate(probs, axis=1)
            values = vbd[pl.ds(tiles[0], len(tiles))].reshape(768 * len(tiles), 256)
            acc[...] += mm(probs, values)

        def finish(highest):
            a0, a1 = acc[:, 0:128], acc[:, 128:256]
            lane5 = lanes(512)
            some = a0 > 0.0
            mass = jnp.where(some, a0, 1.0)
            inverse = jnp.where(some, 1.0 / mass, 0.0)
            log_mass = jnp.where(some, jnp.log(mass) + highest, NEG)
            hi, lo = split_two(log_mass)
            extra = jnp.where(lane5 < 3, hi, pltpu.roll(lo, 3, 1))
            scaled = [inverse[:, h : h + 1] for h in range(3)]
            o0 = jnp.where(lane5 >= 64, a0 * scaled[0], jnp.where(lane5 < 6, extra, 0.0)).astype(BF)
            o1 = (a1 * jnp.where(lane5 < 64, scaled[1], scaled[2])).astype(BF)
            for yq in range(4):
                at = slice(yq * 128, yq * 128 + 128)
                out_ref[xr, yq, :, 0:128] = o0[at]
                out_ref[xr, yq, :, 128:256] = o1[at]

        @pl.when(small)
        def _():
            def step(t, _):
                fast((start + 2 * t, start + 2 * t + 1), False)
                return 0

            lax.fori_loop(0, (end - start) // 2, step, 0)

            @pl.when(((end - start) & 1) == 1)
            def _():
                fast((end - 1,), False)

            fast((end,), True)
            finish(0.0)

        @pl.when(jnp.logical_not(small))
        def _():
            lane5 = lanes(512)

            def step(t, highs):
                at = pl.ds(pl.multiple_of(t * 256, 256), 256)
                keys = kaug[at, :]
                allowed = allowed_keys(t)
                a0, a1 = acc[:, 0:128], acc[:, 128:256]
                total, fresh, scales = None, [], []
                for h in range(3):
                    s = jnp.where(allowed, mm(keys, qm[512 * h : 512 * h + 512, :], NT), NEG)
                    top = jnp.maximum(highs[h], jnp.max(s, axis=0, keepdims=True))
                    scales.append(jnp.exp(highs[h] - top))
                    p = jnp.where(s < 0.5 * NEG, 0.0, jnp.exp(s - top)).astype(BF)
                    part = mm(p, vbd[t, 256 * h : 256 * h + 256, :], TN)
                    total = part if total is None else total + part
                    fresh.append(top)
                rows = jnp.concatenate(scales + [jnp.zeros((125, 512), F32)], axis=0)
                columns = rows.T
                scales = [columns[:, h : h + 1] for h in range(3)]
                factor0 = jnp.where((lane5 >= 64) | (lane5 == 0), scales[0], 1.0)
                factor0 = jnp.where(lane5 == 1, scales[1], jnp.where(lane5 == 2, scales[2], factor0))
                factor1 = jnp.where(lane5 < 64, scales[1], scales[2])
                acc[:, 0:128] = a0 * factor0 + total[:, 0:128]
                acc[:, 128:256] = a1 * factor1 + total[:, 128:256]
                return tuple(fresh)

            lowest = tuple(jnp.full((1, 512), NEG, F32) for _ in range(3))
            highs = lax.fori_loop(start, end + 1, step, lowest)
            rows = jnp.concatenate(list(highs) + [jnp.zeros((125, 512), F32)], axis=0)
            finish(rows.T)

        return 0

    lax.fori_loop(0, 4, one_run, 0)


def bwd_kernel(meta, lab, *refs):
    q_refs, kv_own, kv_oth, do_ref = refs[0:4], refs[4:8], refs[8:12], refs[12]
    dq_refs, dkv_own, dkv_oth = refs[13:17], refs[17:21], refs[21:25]
    kaug, vaug, kt, qa, da, dq_acc, dk_acc, dv_acc, dq_rows = refs[25:]
    ix, iz, ic, iy = (meta[k] for k in range(4))
    lane = lanes(128)
    first, last = lab[0:1, :], lab[1:2, :]
    is_label = (lane >= LABEL_LANE) & (lane < LABEL_LANE + LABELS)
    zeros = jnp.zeros((128, 128), BF)

    low, high, _, _ = lane_masks()
    two = ((lane < 2).astype(F32)).astype(BF)

    def value_rows(at, k0, half, k1, v1):
        vaug[pl.ds(at, 128), 0:128] = k1 * high + two
        vaug[pl.ds(at, 128), 128:256] = v1

    stage_keys(meta, lab, kv_own, kv_oth, kaug, value_rows)

    def turn(t, _):
        at = pl.ds(pl.multiple_of(t * 256, 256), 256)
        kt[t] = kaug[at, :].T
        return 0

    lax.fori_loop(0, 16, turn, 0)
    dk_acc[...] = jnp.zeros_like(dk_acc)
    dv_acc[...] = jnp.zeros_like(dv_acc)

    def one_run(xr, _):
        i = (ix - xr) & 3
        begin = xr * 4096 + iz * 1024 + ic * 512
        for j in range(4):
            yq = (iy - j) & 3
            q0, q1 = q_refs[j][i, :, 0:128], q_refs[j][i, :, 128:256]
            d0, d1 = do_ref[xr, yq, :, 0:128], do_ref[xr, yq, :, 128:256]
            extra = d0.astype(F32)
            place = begin + yq * 128 + rows_of(128)
            mine = is_label & (place >= first) & (place < last)
            label = jnp.where(mine, 1.0, 0.0)
            for h in range(3):
                at = pl.ds(pl.multiple_of(512 * h + yq * 128, 128), 128)
                aug = jnp.where(
                    lane == 64,
                    extra[:, h : h + 1],
                    jnp.where(lane == 65, extra[:, h + 3 : h + 4], label),
                ).astype(BF)
                qa[at, 0:128] = q0 * (low, high, low * high)[h]
                qa[at, 128:256] = (q1 * low + aug) if h == 2 else aug
                aug = jnp.where(
                    lane == 0,
                    extra[:, h + 6 : h + 7],
                    jnp.where(lane == 1, extra[:, h + 9 : h + 10], 0.0),
                ).astype(BF)
                da[at, 0:128] = (d0 * high + aug) if h == 0 else aug
                da[at, 128:256] = d1 * (low * high, low, high)[h]
        start = meta[4 + xr]
        end = xr * 4 + iz
        dq_acc[...] = jnp.zeros_like(dq_acc)

        def tile(t, diagonal):
            at = pl.ds(pl.multiple_of(t * 256, 256), 256)
            keys, values = kaug[at, :], vaug[at, :]
            if diagonal:
                key_row = lax.broadcasted_iota(jnp.int32, (256, 512), 0)
                key_place = t * 1024 + iy * 128 + key_row + jnp.where(key_row >= 128, 512 - 128, 0)
                place = begin + lax.broadcasted_iota(jnp.int32, (256, 512), 1)
                allowed = key_place <= place
            s = mm(keys, qa[...], NT)
            dp = mm(values, da[...], NT)
            probs, grads = [], []
            for h in range(3):
                part = s[:, 512 * h : 512 * h + 512]
                if diagonal:
                    part = jnp.where(allowed, part, NEG)
                p = jnp.exp(part)
                ds = (p * dp[:, 512 * h : 512 * h + 512]).astype(BF)
                probs.append(p.astype(BF))
                grads.append(ds)
                dq_acc[h] += mm(kt[t, 64 * h : 64 * h + 64, :], ds)
            dv_acc[at, :] += mm(jnp.concatenate(probs, axis=1), da[...])
            dk_acc[at, :] += mm(jnp.concatenate(grads, axis=1), qa[...])

        def step(t, _):
            tile(start + 2 * t, False)
            tile(start + 2 * t + 1, False)
            return 0

        lax.fori_loop(0, (end - start) // 2, step, 0)

        @pl.when(((end - start) & 1) == 1)
        def _():
            tile(end - 1, False)

        tile(end, True)
        whole = jnp.concatenate([dq_acc[0], dq_acc[1], dq_acc[2], jnp.zeros((64, 512), F32)], axis=0)
        dq_rows[...] = whole.T.astype(BF)
        for j in range(4):
            yq = (iy - j) & 3
            dq_refs[j][i] = dq_rows[pl.ds(pl.multiple_of(yq * 128, 128), 128), :]
        return 0

    lax.fori_loop(0, 4, one_run, 0)

    def give(i, _):
        for j in range(4):
            ki = ((ix - i) & 3) * 4 + ((iz - j) & 3)
            for ref, core in ((dkv_own[j], ic), (dkv_oth[j], 1 - ic)):
                at = pl.ds(pl.multiple_of(ki * 256 + core * 128, 128), 128)
                middle = jnp.where(lane < 64, dk_acc[at, 128:256], dv_acc[at, 0:128])
                ref[i, :, 0:128] = dk_acc[at, 0:128].astype(BF)
                ref[i, :, 128:256] = middle.astype(BF)
                ref[i, :, 256:384] = dv_acc[at, 128:256].astype(BF)
        return 0

    lax.fori_loop(0, 4, give, 0)


def sds(shape, dtype=BF):
    return jax.ShapeDtypeStruct(shape, dtype)


VM = pl.BlockSpec(memory_space=pltpu.VMEM)
SM = pl.BlockSpec(memory_space=pltpu.SMEM)


def attend(meta, lab, q, kv_own, kv_oth):
    return pl.pallas_call(
        fwd_kernel,
        out_shape=sds((4, 4, 128, 256)),
        in_specs=[SM] + [VM] * 13,
        out_specs=VM,
        scratch_shapes=[
            pltpu.VMEM((4096, 256), BF),
            pltpu.VMEM((16, 768, 256), BF),
            pltpu.VMEM((1536, 256), BF),
            pltpu.VMEM((512, 256), F32),
        ],
        compiler_params=pltpu.CompilerParams(vmem_limit_bytes=48 * 2**20),
        cost_estimate=pl.CostEstimate(flops=20 * 10**9, bytes_accessed=8 * 2**20, transcendentals=10**7),
        name="attend",
    )(meta, lab, *q, *kv_own, *kv_oth)


def attend_back(meta, lab, q, kv_own, kv_oth, dout):
    outs = pl.pallas_call(
        bwd_kernel,
        out_shape=(sds((4, 128, 256)),) * 4 + (sds((4, 128, 384)),) * 8,
        in_specs=[SM] + [VM] * 14,
        out_specs=(VM,) * 12,
        scratch_shapes=[
            pltpu.VMEM((4096, 256), BF),
            pltpu.VMEM((4096, 256), BF),
            pltpu.VMEM((16, 256, 256), BF),
            pltpu.VMEM((1536, 256), BF),
            pltpu.VMEM((1536, 256), BF),
            pltpu.VMEM((3, 64, 512), F32),
            pltpu.VMEM((4096, 256), F32),
            pltpu.VMEM((4096, 256), F32),
            pltpu.VMEM((512, 256), BF),
        ],
        compiler_params=pltpu.CompilerParams(vmem_limit_bytes=56 * 2**20),
        cost_estimate=pl.CostEstimate(flops=50 * 10**9, bytes_accessed=16 * 2**20, transcendentals=10**7),
        name="attend_back",
    )(meta, lab, *q, *kv_own, *kv_oth, dout)
    return outs[0:4], outs[4:8], outs[8:12]


def spread_rows():
    row = lax.broadcasted_iota(jnp.int32, (1024, D), 0)
    column = lax.broadcasted_iota(jnp.int32, (1024, D), 1)
    inner = row % 8
    return jnp.where((inner < 6) & (row // 8 * 6 + inner == column), 1.0, 0.0).astype(BF)


def project_kernel(w_ref, t0, t1, t2, t3, cos_ref, sin_ref, q_ref, kv_ref, w_out, n_out, gain_out):
    w = mm(spread_rows(), w_ref[...], TN).astype(BF)
    w_out[...] = w
    tail = w[:, 512:640]
    row, lane = lax.broadcasted_iota(jnp.int32, (8, 128), 0), lax.broadcasted_iota(jnp.int32, (8, 128), 1)
    pick = jnp.where(lane == row + 64, 1.0, 0.0).astype(BF)
    gains = mm(pick, tail, NT)
    gain_out[...] = gains
    for i, ref in enumerate((t0, t1, t2, t3)):
        wide = ref[...].astype(F32)
        r1 = lax.rsqrt(jnp.mean(wide * wide, axis=1, keepdims=True) + EPSILON)
        n = (wide * r1 * gains[0:1, :]).astype(BF)
        n_out[i] = n
        y = mm(n, w_out[...])
        turned = turn_heads(y, cos_ref[i], sin_ref[i], 0.125)
        kv_ref[i] = turned[:, 0:384].astype(BF)
        q_ref[i] = turned[:, 384:640].astype(BF)


def turn_heads(y, cosine, sine, scale):
    lane = lax.broadcasted_iota(jnp.int32, y.shape, 1)
    other = jnp.where(lane % 64 < 32, pltpu.roll(y, WIDE - 32, 1), pltpu.roll(y, 32, 1))
    low = lanes(cosine.shape[0]) < 64
    cosines = [cosine, jnp.where(low, cosine, 1.0), jnp.ones_like(cosine), cosine * scale, cosine * scale]
    none = jnp.zeros_like(sine)
    sines = [sine, jnp.where(low, sine, 0.0), none, sine * scale, sine * scale]
    return y * jnp.concatenate(cosines, axis=1) + other * jnp.concatenate(sines, axis=1)


def project(w, rows, cosine, sine):
    return pl.pallas_call(
        project_kernel,
        out_shape=(
            sds((4, 128, 256)), sds((4, 128, 384)), sds((D, WIDE)), sds((4, 128, D)), sds((8, D), F32),
        ),
        in_specs=[VM] * 7,
        out_specs=(VM,) * 5,
        compiler_params=pltpu.CompilerParams(vmem_limit_bytes=32 * 2**20),
        cost_estimate=pl.CostEstimate(flops=2 * 10**9, bytes_accessed=4 * 2**20, transcendentals=0),
        name="project",
    )(w, *rows, cosine, sine)


def project_back_kernel(
    w_ref, n_ref, cos_ref, sin_ref, loss_ref, a0, a1, a2, a3, b0, b1, b2, b3,
    u0, u1, u2, u3, g_ref, d_scr,
):
    keep = jnp.where(lax.broadcasted_iota(jnp.int32, (D, 128), 1) < 64, 1.0, 0.0)
    tail = (w_ref[:, 512:640].astype(F32) * keep).astype(BF)
    w = jnp.concatenate([w_ref[:, 0:512], tail], axis=1)
    for i, u_ref in enumerate((u0, u1, u2, u3)):
        dkv = (b0[i].astype(F32) + b2[i].astype(F32)) + (b1[i].astype(F32) + b3[i].astype(F32))
        dq = (a0[i].astype(F32) + a2[i].astype(F32)) + (a1[i].astype(F32) + a3[i].astype(F32))
        dq1 = jnp.where(lanes(128) < 64, dq[:, 128:256], 0.0)
        y = jnp.concatenate([dkv, dq[:, 0:128], dq1], axis=1).astype(BF).astype(F32)
        d = turn_heads(y, cos_ref[i], -sin_ref[i], 0.125).astype(BF)
        d_scr[i * 128 : i * 128 + 128, :] = d
        u_ref[...] = mm(d, w, NT).astype(BF)
    rows = n_ref[...].reshape(512, D)
    g = mm(rows, d_scr[...], TN)
    last = jnp.where(lanes(D) < 64, g[:, 512:640], loss_ref[0:1, :])
    g = jnp.concatenate([g[:, 0:512], last], axis=1).astype(BF)
    g_ref[...] = mm(spread_rows(), g).astype(BF)


def project_back(w, n, cosine, sine, loss_row, dq, dkv):
    outs = pl.pallas_call(
        project_back_kernel,
        out_shape=(sds((128, D)),) * 4 + (sds((1024, WIDE)),),
        in_specs=[VM] * 13,
        out_specs=(VM,) * 5,
        scratch_shapes=[pltpu.VMEM((512, WIDE), BF)],
        compiler_params=pltpu.CompilerParams(vmem_limit_bytes=40 * 2**20),
        cost_estimate=pl.CostEstimate(flops=2 * 10**9, bytes_accessed=6 * 2**20, transcendentals=0),
        name="project_back",
    )(w, n, cosine, sine, loss_row, *dq, *dkv)
    return outs[0:4], outs[4]


def weights_back_kernel(n_ref, dgu_ref, hid_ref, gd_ref, mix_ref, gb_ref, out_ref, n_t, h_t, m_t):
    n_t[...] = n_ref[...].T
    h_t[...] = hid_ref[...].T
    for g in range(4):
        m_t[192 * g : 192 * g + 192, :] = mix_ref[g].T[64:256, :]

    def gate_up(k, _):
        part = mm(n_t[...], dgu_ref[:, pl.ds(pl.multiple_of(256 * k, 256), 256)])
        put(part, pl.multiple_of(48 * k, 48))
        return 0

    def put(part, at):
        for b in range(32):
            rows = part[24 * b : 24 * b + 24]
            both = jnp.concatenate([rows[:, 0:128], rows[:, 128:256]], axis=0)
            out_ref[b, pl.ds(at, 48), :] = both.astype(BF)

    lax.fori_loop(0, 16, gate_up, 0)
    for k in range(3):
        part = mm(h_t[...], gd_ref[:, 256 * k : 256 * k + 256])
        for b in range(32):
            rows = part[64 * b : 64 * b + 64]
            both = jnp.concatenate([rows[:, 0:128], rows[:, 128:256]], axis=0)
            out_ref[b, 768 + 128 * k : 896 + 128 * k, :] = both.astype(BF)
        put(mm(m_t[...], gb_ref[:, 256 * k : 256 * k + 256]), 1152 + 48 * k)


def weights_back(n, dgu, hidden, g_down, mixed, g_branch):
    return pl.pallas_call(
        weights_back_kernel,
        out_shape=sds((32, 1296, 128)),
        in_specs=[VM] * 6,
        out_specs=VM,
        scratch_shapes=[pltpu.VMEM((D, 128), BF), pltpu.VMEM((FF, 128), BF), pltpu.VMEM((D, 128), BF)],
        compiler_params=pltpu.CompilerParams(vmem_limit_bytes=40 * 2**20),
        cost_estimate=pl.CostEstimate(flops=5 * 10**9, bytes_accessed=13 * 2**20, transcendentals=0),
        name="weights_back",
    )(n, dgu, hidden, g_down, mixed, g_branch)


def middle_kernel(
    count, factor, pay, tok_ref, teach_ref, gains, w_out, w_gu, w_down,
    out_ref, sq_ref, n_ref, dgu_ref, hid_ref, gd_ref, mix_ref, gb_ref, gm_ref, pay_out,
    gu_scr, o_scr, lse_scr,
):
    lane = lanes(128)
    middle = tok_ref[...].astype(F32)
    for g in range(4):
        tiles = [pay[g * 4 + y].astype(F32) for y in range(4)]
        logs = [t[:, 0:128] + pltpu.roll(t[:, 0:128], 125, 1) for t in tiles]
        logs = [jnp.where(lane < 3, v, 0.0) for v in logs]
        top = jnp.maximum(jnp.maximum(logs[0], logs[1]), jnp.maximum(logs[2], logs[3]))
        shares = [jnp.exp(v - top) for v in logs]
        mass = (shares[0] + shares[1]) + (shares[2] + shares[3])
        o0 = o1 = None
        for t, share in zip(tiles, shares):
            w = share / mass
            p0 = t[:, 0:128] * w[:, 0:1]
            p1 = t[:, 128:256] * jnp.where(lane < 64, w[:, 1:2], w[:, 2:3])
            o0 = p0 if o0 is None else o0 + p0
            o1 = p1 if o1 is None else o1 + p1
        o0 = jnp.where(lane < 64, 0.0, o0)
        lse_scr[g] = top + jnp.log(mass)
        o = jnp.concatenate([o0, o1], axis=1)
        o_scr[g] = o
        mix_ref[g] = o.astype(BF)
        middle = middle + mm(o.astype(BF), w_out[192 * g : 192 * g + 256, :])
    r2 = lax.rsqrt(jnp.mean(middle * middle, axis=1, keepdims=True) + EPSILON)
    n2 = middle * r2
    n2b = (n2 * gains[1:2, :]).astype(BF)
    n_ref[...] = n2b
    for f in range(4):
        at, up_at = slice(512 * f, 512 * f + 512), slice(FF + 512 * f, FF + 512 * f + 512)
        gate = mm(n2b, w_gu[:, at])
        up = mm(n2b, w_gu[:, up_at])
        gu_scr[:, at] = gate
        gu_scr[:, up_at] = up
        hid = (gate / (1.0 + jnp.exp(-gate)) * up).astype(BF)
        hid_ref[:, at] = hid
    total = middle + mm(hid_ref[...], w_down[...])
    out_ref[...] = total.astype(BF)
    row = lax.broadcasted_iota(jnp.int32, (128, D), 0)
    diff = jnp.where(row < count[0], total - teach_ref[...].astype(F32), 0.0)
    square = diff * diff
    square = sum(square[:, 128 * n : 128 * n + 128] for n in range(6))
    square = jnp.sum(square, axis=0, keepdims=True)
    sq_ref[...] = jnp.broadcast_to(square + pltpu.roll(square, 64, 1), (8, 128))
    g = diff * factor[0]
    gb = g.astype(BF)
    gd_ref[...] = gb
    u = jnp.zeros((128, D), F32)
    for f in range(4):
        at, up_at = slice(512 * f, 512 * f + 512), slice(FF + 512 * f, FF + 512 * f + 512)
        gate, up = gu_scr[:, at], gu_scr[:, up_at]
        dh = mm(gb, w_down[at, :], NT)
        sig = 1.0 / (1.0 + jnp.exp(-gate))
        dgate = (dh * up * sig * (1.0 + gate * (1.0 - sig))).astype(BF)
        dup = (dh * gate * sig).astype(BF)
        dgu_ref[:, at] = dgate
        dgu_ref[:, up_at] = dup
        u = u + mm(dgate, w_gu[:, at], NT) + mm(dup, w_gu[:, up_at], NT)
    u = u * gains[1:2, :]
    gm = g + r2 * (u - n2 * jnp.mean(u * n2, axis=1, keepdims=True))
    gm_ref[...] = gm
    gmb = gm.astype(BF)
    gb_ref[...] = gmb
    for k in range(4):
        dm = mm(gmb, w_out[192 * k : 192 * k + 256, :], NT).astype(BF)
        d0, d1 = dm[:, 0:128].astype(F32), dm[:, 128:256].astype(F32)
        p0, p1 = d0 * o_scr[k, :, 0:128], d1 * o_scr[k, :, 128:256]
        deltas = [
            jnp.sum(p0, axis=1, keepdims=True),
            jnp.sum(jnp.where(lane < 64, p1, 0.0), axis=1, keepdims=True),
            jnp.sum(jnp.where(lane < 64, 0.0, p1), axis=1, keepdims=True),
        ]
        hi, lo = split_two(-lse_scr[k])
        delta = jnp.where(lane == 0, deltas[0], jnp.where(lane == 1, deltas[1], deltas[2]))
        dhi, dlo = split_two(-delta)
        aug = jnp.where(lane < 3, hi, jnp.where(lane < 6, pltpu.roll(lo, 3, 1), 0.0))
        aug = jnp.where((lane >= 6) & (lane < 9), pltpu.roll(dhi, 6, 1), aug)
        aug = jnp.where((lane >= 9) & (lane < 12), pltpu.roll(dlo, 9, 1), aug)
        pay_out[k, :, 0:128] = jnp.where(lane < 64, aug, d0).astype(BF)
        pay_out[k, :, 128:256] = dm[:, 128:256]


def middle_part(count, factor, pay, tokens, teacher, gains, w_out, w_gu, w_down):
    return pl.pallas_call(
        middle_kernel,
        out_shape=(
            sds((128, D)), sds((8, 128), F32), sds((128, D)), sds((128, 2 * FF)), sds((128, FF)),
            sds((128, D)), sds((4, 128, 256)), sds((128, D)), sds((128, D), F32), sds((4, 128, 256)),
        ),
        in_specs=[SM, SM] + [VM] * 7,
        out_specs=(VM,) * 10,
        scratch_shapes=[
            pltpu.VMEM((128, 2 * FF), F32),
            pltpu.VMEM((4, 128, 256), F32),
            pltpu.VMEM((4, 128, 128), F32),
        ],
        compiler_params=pltpu.CompilerParams(vmem_limit_bytes=40 * 2**20),
        cost_estimate=pl.CostEstimate(flops=3 * 10**9, bytes_accessed=16 * 2**20, transcendentals=10**6),
        name="middle_part",
    )(count, factor, pay, tokens, teacher, gains, w_out, w_gu, w_down)


def from_behind(x, axis, j):
    return lax.ppermute(x, axis, [(s, (s + j) % 4) for s in range(4)])


def from_ahead(x, axis, j):
    return lax.ppermute(x, axis, [(s, (s - j) % 4) for s in range(4)])


def from_core(x):
    return lax.ppermute(x, C, [(0, 1), (1, 0)])


def gather4(x, axis):
    return [x] + [from_behind(x, axis, j) for j in (1, 2, 3)]


def in_order(blocks, index, dim):
    r0, r1, r2, r3 = blocks
    twice = jnp.concatenate([r3, r2, r1, r0, r3, r2, r1], axis=dim)
    size = r0.shape[dim]
    return lax.dynamic_slice_in_dim(twice, (3 - index) * size, 4 * size, dim)


def block_of(x, index):
    return lax.dynamic_index_in_dim(x, index, 0, keepdims=False)


def scatter4(x, axis, index):
    own = block_of(x, index).astype(F32)
    far = [from_ahead(block_of(x, (index - j) & 3), axis, j).astype(F32) for j in (1, 2, 3)]
    return (own + far[1]) + (far[0] + far[2])


def per_device(
    tokens, attn_gain, w_query, w_key, w_value, w_out, mlp_gain, w_gate, w_up, w_down, segments, teacher
):
    ix, iz, ic, iy = (lax.axis_index(a) for a in (X, Z, C, Y))
    begin = iz * 1024 + ic * 512

    heads = jnp.concatenate([w.reshape(6, 4, 192) for w in (w_key, w_value, w_query)], axis=2)
    gains = jnp.stack([attn_gain, mlp_gain], axis=1)[:, None]
    gains = jnp.broadcast_to(jnp.pad(gains, ((0, 0), (0, 0), (0, 62))), (6, 4, 64))
    heads = jnp.concatenate([heads, gains], axis=2).transpose(1, 0, 2)
    heads = jnp.pad(heads, ((0, 0), (0, 2), (0, 0)))
    heads = jnp.broadcast_to(heads[:, None], (4, 32, 8, WIDE)).reshape(128, 8, WIDE)
    w_rows = lax.all_to_all(heads, BLK_HD, split_axis=0, concat_axis=0, tiled=True)
    w_rows = w_rows.reshape(1024, WIDE)

    t_rows = gather4(tokens, X)

    pack = jnp.concatenate([w_gate, w_up, w_out, w_down.reshape(6, FF)], axis=1)
    pack = in_order(gather4(pack, Y), iy, 0)
    pack = lax.all_gather(pack, BLK, axis=0, tiled=True)

    number = segments.reshape(128, 128)
    labels = jnp.arange(LABELS, dtype=jnp.int32)[:, None, None]
    some = number[None] != 0
    starts = jnp.sum((some & (number[None] < labels)).astype(jnp.int32), axis=(1, 2))
    ends = jnp.sum((some & (number[None] <= labels)).astype(jnp.int32), axis=(1, 2))
    counted = jnp.sum((number != 0).astype(jnp.int32))
    zero = jnp.arange(LABELS) == 0
    starts = jnp.where(zero, counted, starts)
    ends = jnp.where(zero, 16384, ends)
    lab = jnp.concatenate([jnp.zeros((1, 128), jnp.int32), jnp.full((7, 128), 16384, jnp.int32)])
    lab = lax.dynamic_update_slice(lab, jnp.stack([starts, ends]), (0, LABEL_LANE))
    firsts = jnp.stack(
        [lax.dynamic_index_in_dim(segments, xr * 4096 + begin, 0, keepdims=False) for xr in range(4)]
    )
    lowest = jnp.sum(jnp.where(firsts[:, None] == labels[None, :, 0, 0], starts[None], 0), axis=1)
    meta = jnp.concatenate([jnp.stack([ix, iz, ic, iy]).astype(jnp.int32), lowest // 1024])

    exponents = jnp.arange(32, dtype=jnp.float32) * (-2.0 / HEAD_SIZE)
    frequency = jnp.tile(ROPE_BASE**exponents, 4)
    runs = ((ix - jnp.arange(4, dtype=jnp.int32)) & 3) * 4096
    places = runs[:, None] + begin + iy * 128 + jnp.arange(128, dtype=jnp.int32)[None]
    angles = places.astype(F32)[:, :, None] * frequency[None, None, :]
    cosine = jnp.cos(angles)
    sine = jnp.sin(angles) * jnp.where(jnp.arange(128) % 64 < 32, -1.0, 1.0)

    q, kv, w_full, n_rows, gain_rows = project(w_rows, t_rows, cosine, sine)
    q_all, kv_own = gather4(q, Y), gather4(kv, Z)
    q_all, kv_own = lax.optimization_barrier((q_all, kv_own))
    kv_oth = [from_core(kv) for kv in kv_own]

    pay = attend(meta, lab, q_all, kv_own, kv_oth).reshape(16, 128, 256)
    pay = lax.all_to_all(pay, (X, Y), split_axis=0, concat_axis=0, tiled=True)
    mine = ix * 4096 + begin + iy * 128
    count = jnp.clip(counted - mine, 0, 128).reshape(1)
    factor = (16384.0 / counted.astype(F32)).reshape(1)
    w_out_all = jnp.pad(pack[:, 4096:4864], ((64, 0), (0, 0)))
    w_down_all = pack[:, 4864:].reshape(FF, D)
    out, squares, n2, dgu, hidden, g_down, mixed, g_branch, grad_middle, dpay = middle_part(
        count, factor, pay, tokens, teacher, gain_rows, w_out_all, pack, w_down_all
    )
    dpay = jnp.broadcast_to(dpay[:, None], (4, 4, 128, 256)).reshape(16, 128, 256)
    dout = lax.all_to_all(dpay, (X, Y), split_axis=0, concat_axis=0, tiled=True)

    grads = weights_back(n2, dgu, hidden, g_down, mixed, g_branch)
    grads = lax.psum_scatter(grads.reshape(-1, 128), BLK, scatter_dimension=0, tiled=True)

    dq, dkv_own, dkv_oth = attend_back(
        meta, lab, q_all, kv_own, kv_oth, dout.reshape(4, 4, 128, 256)
    )
    dq = [dq[0]] + [from_ahead(dq[j], Y, j) for j in (1, 2, 3)]
    dkv = [
        (a.astype(F32) + from_core(b).astype(F32)).astype(BF) for a, b in zip(dkv_own, dkv_oth)
    ]
    dkv = [dkv[0]] + [from_ahead(dkv[j], Z, j) for j in (1, 2, 3)]
    u, g = project_back(w_full, n_rows, cosine, sine, squares, dq, dkv)

    u = [u[0].astype(F32)] + [from_ahead(u[j], X, j).astype(F32) for j in (1, 2, 3)]
    u = ((u[0] + u[2]) + (u[1] + u[3])) * gain_rows[0:1]
    wide = tokens.astype(F32)
    r1 = lax.rsqrt(jnp.mean(wide * wide, axis=1, keepdims=True) + EPSILON)
    n1 = wide * r1
    grad_tokens = grad_middle + r1 * (u - n1 * jnp.mean(u * n1, axis=1, keepdims=True))

    g = lax.all_to_all(g.reshape(128, 8, WIDE), BLK_HD, split_axis=0, concat_axis=0, tiled=True)
    g = jnp.sum(g.reshape(4, 32, 8, WIDE).astype(F32), axis=1)[:, :6]
    loss = jnp.sum(g[:, 0, 576:], axis=0)
    mean_loss = jnp.sum(loss) / (counted.astype(F32) * D)
    grad_key, grad_value, grad_query = (
        g[:, :, 192 * k : 192 * k + 192].transpose(1, 0, 2).reshape(6, D) for k in range(3)
    )
    by_row = grad_key * w_key.astype(F32) + grad_value * w_value.astype(F32)
    by_row = by_row + grad_query * w_query.astype(F32)
    grad_attn_gain = jnp.sum(by_row, axis=1) / attn_gain.astype(F32)

    gu = grads[:768].reshape(32, 4, 6, 128).transpose(1, 0, 2, 3).reshape(4, 192, 128)
    down = grads[768:1152].reshape(6, 4, 16, 128).transpose(1, 0, 2, 3).reshape(4, 96, 128)
    outer = grads[1152:].reshape(6, 4, 6, 128).transpose(1, 0, 2, 3).reshape(4, 36, 128)
    grads = scatter4(jnp.concatenate([gu, down, outer], axis=1), Y, iy)
    gu = grads[:192].reshape(32, 6, 128).transpose(1, 0, 2).reshape(6, 2 * FF)
    down = grads[192:288].reshape(6, 16, 128).transpose(1, 0, 2).reshape(16, D)
    outer = grads[288:].reshape(6, 6, 128).transpose(1, 0, 2).reshape(6, D)
    grad_gate, grad_up = gu[:, :FF], gu[:, FF:]
    by_row = grad_gate * w_gate.astype(F32) + grad_up * w_up.astype(F32)
    grad_mlp_gain = jnp.sum(by_row, axis=1) / mlp_gain.astype(F32)
    return (
        out,
        grad_tokens.astype(BF),
        mean_loss,
        grad_attn_gain,
        grad_query,
        grad_key,
        grad_value,
        outer,
        grad_mlp_gain,
        grad_gate,
        grad_up,
        down,
    )


def solution(mesh):
    torus = Mesh(mesh.devices.reshape(4, 4, 2, mesh.shape["hd"]), BLK_HD)
    rows, vector = P(BLK_HD, None), P(BLK_HD)
    return jax.shard_map(
        per_device,
        mesh=torus,
        in_specs=(rows, vector, rows, rows, rows, rows, vector, rows, rows, rows, P(), rows),
        out_specs=(rows, rows, P(), vector, rows, rows, rows, rows, vector, rows, rows, rows),
        check_vma=False,
    )
```

```python
import jax
import jax.numpy as jnp
from jax import lax
from jax.experimental import pallas as pl
from jax.experimental.pallas import tpu as pltpu
from jax.sharding import Mesh
from jax.sharding import PartitionSpec as P

HEADS = 12
HEAD_SIZE = 64
D = 768
FF = 2048
EPSILON = 1e-05
ROPE_BASE = 10000.0
X, Z, C, Y = "blk_0", "blk_1", "blk_2", "hd"
BLK = (X, Z, C)
BLK_HD = (X, Z, C, Y)
WIDE = 640

BF = jnp.bfloat16
F32 = jnp.float32
NEG = -1e30
LABEL_LANE = 72
LABELS = 25
NT = (((1,), (1,)), ((), ()))
TN = (((0,), (0,)), ((), ()))
NN = (((1,), (0,)), ((), ()))
LIMIT = 70.0


def mm(a, b, dims=NN):
    return lax.dot_general(a, b, dims, preferred_element_type=F32)


def lanes(rows):
    return lax.broadcasted_iota(jnp.int32, (rows, 128), 1)


def rows_of(rows):
    return lax.broadcasted_iota(jnp.int32, (rows, 128), 0)


def lane_masks():
    lane = lanes(128)
    low = (lane < 64).astype(F32)
    head = rows_of(128) // 64
    first = (head == lane).astype(F32).astype(BF)
    second = ((head == 0) & (lane == 2)).astype(F32).astype(BF)
    return low.astype(BF), (1.0 - low).astype(BF), first, second


def one_lane(n):
    return (lanes(128) == n).astype(F32).astype(BF)


def stage_keys(meta, lab, own, oth, kaug, other):
    ix, iz, ic, iy = (meta[k] for k in range(4))
    lane = lanes(128)
    row = rows_of(128)
    first, last = lab[0:1, :], lab[1:2, :]
    one = ((lane >= 64) & (lane < 66)).astype(F32)
    low, _, _, _ = lane_masks()

    def place(i, _):
        for j in range(4):
            ki = ((ix - i) & 3) * 4 + ((iz - j) & 3)
            for ref, core in ((own[j], ic), (oth[j], 1 - ic)):
                at = pl.multiple_of(ki * 256 + core * 128, 128)
                k0, k1, v1 = (ref[i, :, 128 * n : 128 * n + 128] for n in range(3))
                place_at = ki * 1024 + core * 512 + iy * 128 + row
                outside = (place_at < first) | (place_at >= last)
                half = k1 * low
                kaug[pl.ds(at, 128), 0:128] = k0
                kaug[pl.ds(at, 128), 128:256] = half + jnp.where(outside, NEG, one).astype(BF)
                other(at, k0, half, k1, v1)
        return 0

    lax.fori_loop(0, 4, place, 0)


def split_two(x):
    hi = x.astype(BF).astype(F32)
    return hi, x - hi


def fwd_kernel(meta, lab, *refs):
    out_ref, kaug, vbd, qm, acc, q_in, kv_in, sems = refs[12:]
    fetches = [
        pltpu.make_async_copy(ref, q_in.at[n] if n < 4 else kv_in.at[n - 4], sems.at[n])
        for n, ref in enumerate(refs[0:12])
    ]
    for fetch in fetches[4:] + fetches[:4]:
        fetch.start()
    q_refs = [q_in.at[n] for n in range(4)]
    kv_own, kv_oth = ([kv_in.at[n + at] for n in range(4)] for at in (0, 4))
    for fetch in fetches[4:]:
        fetch.wait()
    ix, iz, ic, iy = (meta[k] for k in range(4))
    lane = lanes(128)
    first, last = lab[0:1, :], lab[1:2, :]
    is_label = (lane >= LABEL_LANE) & (lane < LABEL_LANE + LABELS)
    zeros = jnp.zeros((128, 128), BF)
    low, high, by_head0, by_head1 = lane_masks()
    ones = [one_lane(h) for h in range(3)]

    def value_rows(at, k0, half, k1, v1):
        t = at // 256
        inner = pl.multiple_of(at % 256, 128)
        rows = [pl.ds(256 * h + inner, 128) for h in range(3)]
        vbd[t, rows[0], 0:128] = k1 * high + ones[0]
        vbd[t, rows[0], 128:256] = zeros
        vbd[t, rows[1], 0:128] = ones[1]
        vbd[t, rows[1], 128:256] = v1 * low
        vbd[t, rows[2], 0:128] = ones[2]
        vbd[t, rows[2], 128:256] = v1 * high

    stage_keys(meta, lab, kv_own, kv_oth, kaug, value_rows)
    for fetch in fetches[:4]:
        fetch.wait()
    key_norms = query_norms = jnp.zeros((1, 128), F32)
    for n in range(4):
        for ref, at in ((kaug, pl.ds(1024 * n, 1024)), (q_refs[n], slice(None))):
            whole = ref[at].reshape(-1, 256)
            v0, v1 = whole[:, 0:128], whole[:, 128:256] * low[0:1, :]
            norms = mm(v0 * v0, by_head0) + mm(v1 * v1, by_head1)
            norms = jnp.max(norms, axis=0, keepdims=True)
            if ref is kaug:
                key_norms = jnp.maximum(key_norms, norms)
            else:
                query_norms = jnp.maximum(query_norms, norms)
    bound = key_norms * query_norms
    small = jnp.max(bound) < LIMIT * LIMIT

    def one_run(xr, _):
        i = (ix - xr) & 3
        begin = xr * 4096 + iz * 1024 + ic * 512
        for j in range(4):
            yq = (iy - j) & 3
            q0, q1 = q_refs[j][i, :, 0:128], q_refs[j][i, :, 128:256]
            place = begin + yq * 128 + rows_of(128)
            mine = is_label & (place >= first) & (place < last)
            label = jnp.where(mine, 1.0, 0.0).astype(BF)
            at = [pl.ds(pl.multiple_of(512 * h + yq * 128, 128), 128) for h in range(3)]
            qm[at[0], 0:128] = q0 * low
            qm[at[0], 128:256] = label
            qm[at[1], 0:128] = q0 * high
            qm[at[1], 128:256] = label
            qm[at[2], 0:128] = zeros
            qm[at[2], 128:256] = q1 * low + label
        start = meta[4 + xr]
        end = xr * 4 + iz

        def allowed_keys(t):
            key_row = lax.broadcasted_iota(jnp.int32, (256, 512), 0)
            key_place = t * 1024 + iy * 128 + key_row + jnp.where(key_row >= 128, 512 - 128, 0)
            return key_place <= begin + lax.broadcasted_iota(jnp.int32, (256, 512), 1)

        acc[...] = jnp.zeros((512, 256), F32)

        def fast(tiles, diagonal):
            probs = []
            for t in tiles:
                s = mm(qm[...], kaug[pl.ds(pl.multiple_of(t * 256, 256), 256), :], NT)
                if diagonal:
                    key_lane = lax.broadcasted_iota(jnp.int32, (512, 256), 1)
                    key_place = t * 1024 + iy * 128 + key_lane + jnp.where(key_lane >= 128, 512 - 128, 0)
                    allowed = key_place <= begin + lax.broadcasted_iota(jnp.int32, (512, 256), 0)
                for h in range(3):
                    part = s[512 * h : 512 * h + 512]
                    if diagonal:
                        part = jnp.where(allowed, part, NEG)
                    probs.append(jnp.exp(part).astype(BF))
            probs = jnp.concatenate(probs, axis=1)
            values = vbd[pl.ds(tiles[0], len(tiles))].reshape(768 * len(tiles), 256)
            acc[...] += mm(probs, values)

        def finish(highest):
            a0, a1 = acc[:, 0:128], acc[:, 128:256]
            lane5 = lanes(512)
            some = a0 > 0.0
            mass = jnp.where(some, a0, 1.0)
            inverse = jnp.where(some, 1.0 / mass, 0.0)
            log_mass = jnp.where(some, jnp.log(mass) + highest, NEG)
            hi, lo = split_two(log_mass)
            extra = jnp.where(lane5 < 3, hi, pltpu.roll(lo, 3, 1))
            scaled = [inverse[:, h : h + 1] for h in range(3)]
            o0 = jnp.where(lane5 >= 64, a0 * scaled[0], jnp.where(lane5 < 6, extra, 0.0)).astype(BF)
            o1 = (a1 * jnp.where(lane5 < 64, scaled[1], scaled[2])).astype(BF)
            for yq in range(4):
                at = slice(yq * 128, yq * 128 + 128)
                out_ref[xr, yq, :, 0:128] = o0[at]
                out_ref[xr, yq, :, 128:256] = o1[at]

        @pl.when(small)
        def _():
            def step(t, _):
                fast((start + 2 * t, start + 2 * t + 1), False)
                return 0

            lax.fori_loop(0, (end - start) // 2, step, 0)

            @pl.when(((end - start) & 1) == 1)
            def _():
                fast((end - 1,), False)

            fast((end,), True)
            finish(0.0)

        @pl.when(jnp.logical_not(small))
        def _():
            lane5 = lanes(512)

            def step(t, highs):
                at = pl.ds(pl.multiple_of(t * 256, 256), 256)
                keys = kaug[at, :]
                allowed = allowed_keys(t)
                a0, a1 = acc[:, 0:128], acc[:, 128:256]
                total, fresh, scales = None, [], []
                for h in range(3):
                    s = jnp.where(allowed, mm(keys, qm[512 * h : 512 * h + 512, :], NT), NEG)
                    top = jnp.maximum(highs[h], jnp.max(s, axis=0, keepdims=True))
                    scales.append(jnp.exp(highs[h] - top))
                    p = jnp.where(s < 0.5 * NEG, 0.0, jnp.exp(s - top)).astype(BF)
                    part = mm(p, vbd[t, 256 * h : 256 * h + 256, :], TN)
                    total = part if total is None else total + part
                    fresh.append(top)
                rows = jnp.concatenate(scales + [jnp.zeros((125, 512), F32)], axis=0)
                columns = rows.T
                scales = [columns[:, h : h + 1] for h in range(3)]
                factor0 = jnp.where((lane5 >= 64) | (lane5 == 0), scales[0], 1.0)
                factor0 = jnp.where(lane5 == 1, scales[1], jnp.where(lane5 == 2, scales[2], factor0))
                factor1 = jnp.where(lane5 < 64, scales[1], scales[2])
                acc[:, 0:128] = a0 * factor0 + total[:, 0:128]
                acc[:, 128:256] = a1 * factor1 + total[:, 128:256]
                return tuple(fresh)

            lowest = tuple(jnp.full((1, 512), NEG, F32) for _ in range(3))
            highs = lax.fori_loop(start, end + 1, step, lowest)
            rows = jnp.concatenate(list(highs) + [jnp.zeros((125, 512), F32)], axis=0)
            finish(rows.T)

        return 0

    lax.fori_loop(0, 4, one_run, 0)


def bwd_kernel(meta, lab, *refs):
    q_refs, kv_own, kv_oth, do_ref = refs[0:4], refs[4:8], refs[8:12], refs[12]
    dq_refs, dkv_own, dkv_oth = refs[13:17], refs[17], refs[18]
    kaug, vaug, kt, qa, da, dq_acc, dk_acc, dv_acc, dq_rows = refs[19:]
    ix, iz, ic, iy = (meta[k] for k in range(4))
    lane = lanes(128)
    first, last = lab[0:1, :], lab[1:2, :]
    is_label = (lane >= LABEL_LANE) & (lane < LABEL_LANE + LABELS)
    zeros = jnp.zeros((128, 128), BF)

    low, high, _, _ = lane_masks()
    two = ((lane < 2).astype(F32)).astype(BF)

    def value_rows(at, k0, half, k1, v1):
        vaug[pl.ds(at, 128), 0:128] = k1 * high + two
        vaug[pl.ds(at, 128), 128:256] = v1

    stage_keys(meta, lab, kv_own, kv_oth, kaug, value_rows)

    def turn(t, _):
        at = pl.ds(pl.multiple_of(t * 256, 256), 256)
        kt[t] = kaug[at, :].T
        return 0

    lax.fori_loop(0, 16, turn, 0)
    dk_acc[...] = jnp.zeros_like(dk_acc)
    dv_acc[...] = jnp.zeros_like(dv_acc)

    def one_run(xr, _):
        i = (ix - xr) & 3
        begin = xr * 4096 + iz * 1024 + ic * 512
        for j in range(4):
            yq = (iy - j) & 3
            q0, q1 = q_refs[j][i, :, 0:128], q_refs[j][i, :, 128:256]
            d0, d1 = do_ref[xr, yq, :, 0:128], do_ref[xr, yq, :, 128:256]
            extra = d0.astype(F32)
            place = begin + yq * 128 + rows_of(128)
            mine = is_label & (place >= first) & (place < last)
            label = jnp.where(mine, 1.0, 0.0)
            for h in range(3):
                at = pl.ds(pl.multiple_of(512 * h + yq * 128, 128), 128)
                aug = jnp.where(
                    lane == 64,
                    extra[:, h : h + 1],
                    jnp.where(lane == 65, extra[:, h + 3 : h + 4], label),
                ).astype(BF)
                qa[at, 0:128] = q0 * (low, high, low * high)[h]
                qa[at, 128:256] = (q1 * low + aug) if h == 2 else aug
                aug = jnp.where(
                    lane == 0,
                    extra[:, h + 6 : h + 7],
                    jnp.where(lane == 1, extra[:, h + 9 : h + 10], 0.0),
                ).astype(BF)
                da[at, 0:128] = (d0 * high + aug) if h == 0 else aug
                da[at, 128:256] = d1 * (low * high, low, high)[h]
        start = meta[4 + xr]
        end = xr * 4 + iz
        dq_acc[...] = jnp.zeros_like(dq_acc)

        def tile(t, diagonal):
            at = pl.ds(pl.multiple_of(t * 256, 256), 256)
            keys, values = kaug[at, :], vaug[at, :]
            if diagonal:
                key_row = lax.broadcasted_iota(jnp.int32, (256, 512), 0)
                key_place = t * 1024 + iy * 128 + key_row + jnp.where(key_row >= 128, 512 - 128, 0)
                place = begin + lax.broadcasted_iota(jnp.int32, (256, 512), 1)
                allowed = key_place <= place
            s = mm(keys, qa[...], NT)
            dp = mm(values, da[...], NT)
            probs, grads = [], []
            for h in range(3):
                part = s[:, 512 * h : 512 * h + 512]
                if diagonal:
                    part = jnp.where(allowed, part, NEG)
                p = jnp.exp(part)
                ds = (p * dp[:, 512 * h : 512 * h + 512]).astype(BF)
                probs.append(p.astype(BF))
                grads.append(ds)
                dq_acc[h] += mm(kt[t, 64 * h : 64 * h + 64, :], ds)
            dv_acc[at, :] += mm(jnp.concatenate(probs, axis=1), da[...])
            dk_acc[at, :] += mm(jnp.concatenate(grads, axis=1), qa[...])

        def step(t, _):
            tile(start + 2 * t, False)
            tile(start + 2 * t + 1, False)
            return 0

        lax.fori_loop(0, (end - start) // 2, step, 0)

        @pl.when(((end - start) & 1) == 1)
        def _():
            tile(end - 1, False)

        tile(end, True)
        whole = jnp.concatenate([dq_acc[0], dq_acc[1], dq_acc[2], jnp.zeros((64, 512), F32)], axis=0)
        dq_rows[...] = whole.T.astype(BF)
        for j in range(4):
            yq = (iy - j) & 3
            dq_refs[j][i] = dq_rows[pl.ds(pl.multiple_of(yq * 128, 128), 128), :]
        return 0

    lax.fori_loop(0, 4, one_run, 0)

    def give(i, _):
        for j in range(4):
            ki = ((ix - i) & 3) * 4 + ((iz - j) & 3)
            for ref, core in ((dkv_own, ic), (dkv_oth, 1 - ic)):
                at = pl.ds(pl.multiple_of(ki * 256 + core * 128, 128), 128)
                middle = jnp.where(lane < 64, dk_acc[at, 128:256], dv_acc[at, 0:128])
                ref[j, i, :, 0:128] = dk_acc[at, 0:128].astype(BF)
                ref[j, i, :, 128:256] = middle.astype(BF)
                ref[j, i, :, 256:384] = dv_acc[at, 128:256].astype(BF)
        return 0

    lax.fori_loop(0, 4, give, 0)


def sds(shape, dtype=BF):
    return jax.ShapeDtypeStruct(shape, dtype)


VM = pl.BlockSpec(memory_space=pltpu.VMEM)
SM = pl.BlockSpec(memory_space=pltpu.SMEM)


def attend(meta, lab, q, kv_own, kv_oth):
    return pl.pallas_call(
        fwd_kernel,
        out_shape=sds((4, 4, 128, 256)),
        in_specs=[SM, VM] + [pl.BlockSpec(memory_space=pl.ANY)] * 12,
        out_specs=VM,
        scratch_shapes=[
            pltpu.VMEM((4096, 256), BF),
            pltpu.VMEM((16, 768, 256), BF),
            pltpu.VMEM((1536, 256), BF),
            pltpu.VMEM((512, 256), F32),
            pltpu.VMEM((4, 4, 128, 256), BF),
            pltpu.VMEM((8, 4, 128, 384), BF),
            pltpu.SemaphoreType.DMA((12,)),
        ],
        compiler_params=pltpu.CompilerParams(vmem_limit_bytes=48 * 2**20),
        cost_estimate=pl.CostEstimate(flops=20 * 10**9, bytes_accessed=8 * 2**20, transcendentals=10**7),
        name="attend",
    )(meta, lab, *q, *kv_own, *kv_oth)


def attend_back(meta, lab, q, kv_own, kv_oth, dout):
    outs = pl.pallas_call(
        bwd_kernel,
        out_shape=(sds((4, 128, 256)),) * 4 + (sds((4, 4, 128, 384)),) * 2,
        in_specs=[SM] + [VM] * 14,
        out_specs=(VM,) * 6,
        scratch_shapes=[
            pltpu.VMEM((4096, 256), BF),
            pltpu.VMEM((4096, 256), BF),
            pltpu.VMEM((16, 256, 256), BF),
            pltpu.VMEM((1536, 256), BF),
            pltpu.VMEM((1536, 256), BF),
            pltpu.VMEM((3, 64, 512), F32),
            pltpu.VMEM((4096, 256), F32),
            pltpu.VMEM((4096, 256), F32),
            pltpu.VMEM((512, 256), BF),
        ],
        compiler_params=pltpu.CompilerParams(vmem_limit_bytes=56 * 2**20),
        cost_estimate=pl.CostEstimate(flops=50 * 10**9, bytes_accessed=16 * 2**20, transcendentals=10**7),
        name="attend_back",
    )(meta, lab, *q, *kv_own, *kv_oth, dout)
    return outs[0:4], outs[4], outs[5]


def spread_rows():
    row = lax.broadcasted_iota(jnp.int32, (1024, D), 0)
    column = lax.broadcasted_iota(jnp.int32, (1024, D), 1)
    inner = row % 8
    return jnp.where((inner < 6) & (row // 8 * 6 + inner == column), 1.0, 0.0).astype(BF)


def documents_kernel(place, seg_ref, meta, lab_ref):
    ix, iz, ic, iy = (place[k] for k in range(4))
    seg = seg_ref[...]
    lane = lax.broadcasted_iota(jnp.int32, (1, 128), 1)
    some = seg != 0
    counted = jnp.sum(some.astype(jnp.int32))
    starts, ends = jnp.zeros((1, 128), jnp.int32), jnp.full((1, 128), 16384, jnp.int32)
    begins = []
    for label in range(LABELS):
        start, end = counted, jnp.int32(16384)
        if label:
            start = jnp.sum((some & (seg < label)).astype(jnp.int32))
            end = jnp.sum((some & (seg <= label)).astype(jnp.int32))
        starts = jnp.where(lane == LABEL_LANE + label, start, starts)
        ends = jnp.where(lane == LABEL_LANE + label, end, ends)
        begins.append(start)
    row = lax.broadcasted_iota(jnp.int32, (8, 128), 0)
    lab_ref[...] = jnp.where(row == 0, starts, ends)
    for k in range(4):
        meta[k] = place[k]
    for xr in range(4):
        at = xr * 32 + iz * 8 + ic * 4
        mine = jnp.sum(jnp.where(lane == 0, seg_ref[pl.ds(at, 1), :], 0))
        first = jnp.int32(0)
        for label in range(LABELS):
            first = jnp.where(mine == label, begins[label], first)
        meta[4 + xr] = lax.shift_right_logical(first, 10)
    meta[8] = counted


def documents(place, segments):
    return pl.pallas_call(
        documents_kernel,
        out_shape=(sds((9,), jnp.int32), sds((8, 128), jnp.int32)),
        in_specs=[SM, VM],
        out_specs=(SM, VM),
        cost_estimate=pl.CostEstimate(flops=10**6, bytes_accessed=10**5, transcendentals=0),
        name="documents",
    )(place, segments)


def prepare_kernel(wq, wk, wv, ga, gm, wg, wu, wo, wd, heads_ref, pack_ref):
    row = lax.broadcasted_iota(jnp.int32, (8, 128), 0)
    lane = lax.broadcasted_iota(jnp.int32, (8, 128), 1)

    def eight(ref, width):
        empty = jnp.zeros((2, width), F32)
        return jnp.concatenate([ref[...].astype(F32), empty], axis=0)

    def column(ref):
        across = jnp.broadcast_to(jnp.pad(ref[...].astype(F32), ((0, 0), (0, 122))), (8, 128))
        return jnp.sum(jnp.where(lane == row, across, 0.0), axis=1, keepdims=True)

    wide = [eight(ref, D) for ref in (wk, wv, wq)]
    gains = jnp.where(lane == 64, column(ga), jnp.where(lane == 65, column(gm), 0.0))
    for g in range(4):
        k, v, q = (pltpu.roll(w, (D - 192 * g) % D, 1)[:, 0:256] if g else w[:, 0:256] for w in wide)
        low = lane < 64
        v = pltpu.roll(v, 64, 1)
        tiles = [
            k[:, 0:128],
            jnp.where(low, k[:, 128:256], v[:, 0:128]),
            v[:, 128:256],
            q[:, 0:128],
            jnp.where(low, q[:, 128:256], gains),
        ]
        block = jnp.concatenate(tiles, axis=1).astype(BF)
        for n in range(32):
            heads_ref[32 * g + n] = block
    pack_ref[:, 0:FF] = eight(wg, FF).astype(BF)
    pack_ref[:, FF : 2 * FF] = eight(wu, FF).astype(BF)
    pack_ref[:, 2 * FF : 2 * FF + D] = eight(wo, D).astype(BF)
    pack_ref[:, 2 * FF + D : 2 * FF + 2 * D] = wd[0:8, :]
    pack_ref[:, 2 * FF + 2 * D : 2 * FF + 3 * D] = wd[8:16, :]


def prepare(wq, wk, wv, ga, gm, wg, wu, wo, wd):
    return pl.pallas_call(
        prepare_kernel,
        out_shape=(sds((128, 8, WIDE)), sds((8, 2 * FF + 3 * D))),
        in_specs=[VM] * 9,
        out_specs=(VM, VM),
        cost_estimate=pl.CostEstimate(flops=10**6, bytes_accessed=2 * 10**6, transcendentals=0),
        name="prepare",
    )(wq, wk, wv, ga.reshape(1, 6), gm.reshape(1, 6), wg, wu, wo, wd)


def project_kernel(w_ref, t0, t1, t2, t3, cos_ref, sin_ref, q_ref, kv_ref, w_out, n_out, gain_out):
    w = mm(spread_rows(), w_ref[...], TN).astype(BF)
    w_out[...] = w
    tail = w[:, 512:640]
    row, lane = lax.broadcasted_iota(jnp.int32, (8, 128), 0), lax.broadcasted_iota(jnp.int32, (8, 128), 1)
    pick = jnp.where(lane == row + 64, 1.0, 0.0).astype(BF)
    gains = mm(pick, tail, NT)
    gain_out[...] = gains
    for i, ref in enumerate((t0, t1, t2, t3)):
        wide = ref[...].astype(F32)
        r1 = lax.rsqrt(jnp.mean(wide * wide, axis=1, keepdims=True) + EPSILON)
        n = (wide * r1 * gains[0:1, :]).astype(BF)
        n_out[i] = n
        y = mm(n, w_out[...])
        turned = turn_heads(y, cos_ref[i], sin_ref[i], 0.125)
        kv_ref[i] = turned[:, 0:384].astype(BF)
        q_ref[i] = turned[:, 384:640].astype(BF)


def turn_heads(y, cosine, sine, scale):
    lane = lax.broadcasted_iota(jnp.int32, y.shape, 1)
    other = jnp.where(lane % 64 < 32, pltpu.roll(y, WIDE - 32, 1), pltpu.roll(y, 32, 1))
    low = lanes(cosine.shape[0]) < 64
    cosines = [cosine, jnp.where(low, cosine, 1.0), jnp.ones_like(cosine), cosine * scale, cosine * scale]
    none = jnp.zeros_like(sine)
    sines = [sine, jnp.where(low, sine, 0.0), none, sine * scale, sine * scale]
    return y * jnp.concatenate(cosines, axis=1) + other * jnp.concatenate(sines, axis=1)


def project(w, rows, cosine, sine):
    return pl.pallas_call(
        project_kernel,
        out_shape=(
            sds((4, 128, 256)), sds((4, 128, 384)), sds((D, WIDE)), sds((4, 128, D)), sds((8, D), F32),
        ),
        in_specs=[VM] * 7,
        out_specs=(VM,) * 5,
        compiler_params=pltpu.CompilerParams(vmem_limit_bytes=32 * 2**20),
        cost_estimate=pl.CostEstimate(flops=2 * 10**9, bytes_accessed=4 * 2**20, transcendentals=0),
        name="project",
    )(w, *rows, cosine, sine)


def project_back_kernel(
    w_ref, n_ref, cos_ref, sin_ref, loss_ref, a0, a1, a2, a3, b0, b1, b2, b3,
    u0, u1, u2, u3, g_ref, d_scr,
):
    keep = jnp.where(lax.broadcasted_iota(jnp.int32, (D, 128), 1) < 64, 1.0, 0.0)
    tail = (w_ref[:, 512:640].astype(F32) * keep).astype(BF)
    w = jnp.concatenate([w_ref[:, 0:512], tail], axis=1)
    for i, u_ref in enumerate((u0, u1, u2, u3)):
        dkv = (b0[i].astype(F32) + b2[i].astype(F32)) + (b1[i].astype(F32) + b3[i].astype(F32))
        dq = (a0[i].astype(F32) + a2[i].astype(F32)) + (a1[i].astype(F32) + a3[i].astype(F32))
        dq1 = jnp.where(lanes(128) < 64, dq[:, 128:256], 0.0)
        y = jnp.concatenate([dkv, dq[:, 0:128], dq1], axis=1).astype(BF).astype(F32)
        d = turn_heads(y, cos_ref[i], -sin_ref[i], 0.125).astype(BF)
        d_scr[i * 128 : i * 128 + 128, :] = d
        u_ref[...] = mm(d, w, NT).astype(BF)
    rows = n_ref[...].reshape(512, D)
    g = mm(rows, d_scr[...], TN)
    last = jnp.where(lanes(D) < 64, g[:, 512:640], loss_ref[0:1, :])
    g = jnp.concatenate([g[:, 0:512], last], axis=1).astype(BF)
    g_ref[...] = mm(spread_rows(), g).astype(BF)


def project_back(w, n, cosine, sine, loss_row, dq, dkv):
    outs = pl.pallas_call(
        project_back_kernel,
        out_shape=(sds((128, D)),) * 4 + (sds((1024, WIDE)),),
        in_specs=[VM] * 13,
        out_specs=(VM,) * 5,
        scratch_shapes=[pltpu.VMEM((512, WIDE), BF)],
        compiler_params=pltpu.CompilerParams(vmem_limit_bytes=40 * 2**20),
        cost_estimate=pl.CostEstimate(flops=2 * 10**9, bytes_accessed=6 * 2**20, transcendentals=0),
        name="project_back",
    )(w, n, cosine, sine, loss_row, *dq, *dkv)
    return outs[0:4], outs[4]


PACKED = 2 * FF + FF + 3 * D + 1024


A_ROWS, B_ROWS = 384 + 144 + 128, 384 + 256


def weights_back_kernel(meta, own, oth, *refs):
    ix, iz, ic = meta[0], meta[1], meta[2]
    a_refs, b_refs = [refs[0].at[k] for k in range(4)], refs[1:5]
    n_t, m_t, h_t, left, rows = refs[5:]
    for k, ref in enumerate((own, oth)):
        at = slice(128 * k, 128 * k + 128)
        n_t[:, at] = ref[:, 3 * FF : 3 * FF + D].astype(F32).T
        h_t[:, at] = ref[:, 2 * FF : 3 * FF].T
        for g in range(4):
            first = 3 * FF + 3 * D + 256 * g
            m_t[192 * g : 192 * g + 192, at] = ref[:, first : first + 256].astype(F32).T[64:256, :]
        rows[at, :] = ref[:, 3 * FF + D : 3 * FF + 3 * D]

    def chips(x_outer):
        for m in range(16):
            yield m, m if x_outer else ((ix - m % 4) & 3) * 4 + ((iz - m // 4) & 3)

    def collect(source, x_outer):
        for m, chip in chips(x_outer):
            left[24 * m : 24 * m + 24, :] = source[pl.ds(pl.multiple_of(48 * chip + 24 * ic, 8), 24), :]
        return left[...].astype(BF)

    def collect_hidden(x_outer):
        picked = [
            h_t[pl.ds(pl.multiple_of(128 * chip + 64 * ic, 64), 64), :] for _, chip in chips(x_outer)
        ]
        return jnp.concatenate(picked, axis=0)

    def put(part, outs, at, height):
        for m in range(16):
            block = part[height * m : height * m + height]
            both = jnp.concatenate([block[:, 0:128], block[:, 128:256]], axis=0)
            outs[m // 4][m % 4, pl.ds(at, 2 * height), :] = both.astype(BF)

    def columns(first, k):
        at = pl.ds(pl.multiple_of(first + 256 * k, 256), 256)
        return jnp.concatenate([own[:, at], oth[:, at]], axis=0)

    for outs, first, x_outer in ((a_refs, 0, True), (b_refs, FF, False)):
        features = collect(n_t, x_outer)

        def gate_or_up(k, _):
            put(mm(features, columns(first, k)), outs, pl.multiple_of(48 * k, 48), 24)
            return 0

        lax.fori_loop(0, 8, gate_or_up, 0)
    outer = collect(m_t, True)
    for k in range(3):
        put(mm(outer, rows[:, D + 256 * k : D + 256 * k + 256]), a_refs, 384 + 48 * k, 24)
    put(mm(collect_hidden(True), rows[:, 0:256]), a_refs, 528, 64)
    down = collect_hidden(False)
    for k in range(2):
        put(mm(down, rows[:, 256 + 256 * k : 512 + 256 * k]), b_refs, 384 + 128 * k, 64)


def weights_back(meta, own, oth):
    outs = pl.pallas_call(
        weights_back_kernel,
        out_shape=(sds((4, 4, A_ROWS, 128)),) + (sds((4, B_ROWS, 128)),) * 4,
        in_specs=[SM, VM, VM],
        out_specs=(VM,) * 5,
        scratch_shapes=[
            pltpu.VMEM((D, 256), F32),
            pltpu.VMEM((D, 256), F32),
            pltpu.VMEM((FF, 256), BF),
            pltpu.VMEM((384, 256), F32),
            pltpu.VMEM((256, 2 * D), BF),
        ],
        compiler_params=pltpu.CompilerParams(vmem_limit_bytes=40 * 2**20),
        cost_estimate=pl.CostEstimate(flops=5 * 10**9, bytes_accessed=10 * 2**20, transcendentals=0),
        name="weights_back",
    )(meta, own, oth)
    return outs[0], outs[1:5]


def middle_kernel(
    meta, pay, tok_ref, teach_ref, gains, w_out, w_pack, w_down,
    out_ref, sq_ref, pack_ref, gm_ref, pay_out,
    gu_scr, o_scr, lse_scr, w_gu, sem,
):
    fetch = pltpu.make_async_copy(w_pack.at[:, 0 : 2 * FF], w_gu, sem)
    fetch.start()
    spread = spread_rows()
    lane = lanes(128)
    middle = tok_ref[...].astype(F32)
    for g in range(4):
        tiles = [pay[g * 4 + y].astype(F32) for y in range(4)]
        logs = [t[:, 0:128] + pltpu.roll(t[:, 0:128], 125, 1) for t in tiles]
        logs = [jnp.where(lane < 3, v, 0.0) for v in logs]
        top = jnp.maximum(jnp.maximum(logs[0], logs[1]), jnp.maximum(logs[2], logs[3]))
        shares = [jnp.exp(v - top) for v in logs]
        mass = (shares[0] + shares[1]) + (shares[2] + shares[3])
        o0 = o1 = None
        for t, share in zip(tiles, shares):
            w = share / mass
            p0 = t[:, 0:128] * w[:, 0:1]
            p1 = t[:, 128:256] * jnp.where(lane < 64, w[:, 1:2], w[:, 2:3])
            o0 = p0 if o0 is None else o0 + p0
            o1 = p1 if o1 is None else o1 + p1
        o0 = jnp.where(lane < 64, 0.0, o0)
        lse_scr[g] = top + jnp.log(mass)
        o = jnp.concatenate([o0, o1], axis=1)
        o_scr[g] = o
        pack_ref[:, 3 * FF + 3 * D + 256 * g : 3 * FF + 3 * D + 256 * g + 256] = o.astype(BF)
        middle = middle + mm(o.astype(BF), w_out[192 * g : 192 * g + 256, :])
    r2 = lax.rsqrt(jnp.mean(middle * middle, axis=1, keepdims=True) + EPSILON)
    n2 = middle * r2
    n2b = (n2 * gains[1:2, :]).astype(BF)
    pack_ref[:, 3 * FF : 3 * FF + D] = n2b
    n2p = mm(n2b, spread, NT).astype(BF)
    fetch.wait()
    for f in range(4):
        at, up_at = slice(512 * f, 512 * f + 512), slice(FF + 512 * f, FF + 512 * f + 512)
        gate = mm(n2p, w_gu[:, at])
        up = mm(n2p, w_gu[:, up_at])
        gu_scr[:, at] = gate
        gu_scr[:, up_at] = up
        hid = (gate / (1.0 + jnp.exp(-gate)) * up).astype(BF)
        pack_ref[:, 2 * FF + 512 * f : 2 * FF + 512 * f + 512] = hid
    total = middle + mm(pack_ref[:, 2 * FF : 3 * FF], w_down[...])
    out_ref[...] = total.astype(BF)
    row = lax.broadcasted_iota(jnp.int32, (128, D), 0)
    mine = meta[0] * 4096 + meta[1] * 1024 + meta[2] * 512 + meta[3] * 128
    diff = jnp.where(row < meta[8] - mine, total - teach_ref[...].astype(F32), 0.0)
    square = diff * diff
    square = sum(square[:, 128 * n : 128 * n + 128] for n in range(6))
    square = jnp.sum(square, axis=0, keepdims=True)
    sq_ref[...] = jnp.broadcast_to(square + pltpu.roll(square, 64, 1), (8, 128))
    g = diff * (16384.0 / jnp.full((1, D), meta[8], jnp.int32).astype(F32))
    gb = g.astype(BF)
    pack_ref[:, 3 * FF + D : 3 * FF + 2 * D] = gb
    u = jnp.zeros((128, 1024), F32)
    for f in range(4):
        at, up_at = slice(512 * f, 512 * f + 512), slice(FF + 512 * f, FF + 512 * f + 512)
        gate, up = gu_scr[:, at], gu_scr[:, up_at]
        dh = mm(gb, w_down[at, :], NT)
        sig = 1.0 / (1.0 + jnp.exp(-gate))
        dgate = (dh * up * sig * (1.0 + gate * (1.0 - sig))).astype(BF)
        dup = (dh * gate * sig).astype(BF)
        pack_ref[:, at] = dgate
        pack_ref[:, up_at] = dup
        u = u + mm(dgate, w_gu[:, at], NT) + mm(dup, w_gu[:, up_at], NT)
    u_hi, u_rest = split_two(u)
    u_mid, u_low = split_two(u_rest)
    u = mm(u_hi.astype(BF), spread) + (mm(u_mid.astype(BF), spread) + mm(u_low.astype(BF), spread))
    u = u * gains[1:2, :]
    gm = g + r2 * (u - n2 * jnp.mean(u * n2, axis=1, keepdims=True))
    gm_ref[...] = gm
    gmb = gm.astype(BF)
    pack_ref[:, 3 * FF + 2 * D : 3 * FF + 3 * D] = gmb
    for k in range(4):
        dm = mm(gmb, w_out[192 * k : 192 * k + 256, :], NT).astype(BF)
        d0, d1 = dm[:, 0:128].astype(F32), dm[:, 128:256].astype(F32)
        p0, p1 = d0 * o_scr[k, :, 0:128], d1 * o_scr[k, :, 128:256]
        deltas = [
            jnp.sum(p0, axis=1, keepdims=True),
            jnp.sum(jnp.where(lane < 64, p1, 0.0), axis=1, keepdims=True),
            jnp.sum(jnp.where(lane < 64, 0.0, p1), axis=1, keepdims=True),
        ]
        hi, lo = split_two(-lse_scr[k])
        delta = jnp.where(lane == 0, deltas[0], jnp.where(lane == 1, deltas[1], deltas[2]))
        dhi, dlo = split_two(-delta)
        aug = jnp.where(lane < 3, hi, jnp.where(lane < 6, pltpu.roll(lo, 3, 1), 0.0))
        aug = jnp.where((lane >= 6) & (lane < 9), pltpu.roll(dhi, 6, 1), aug)
        aug = jnp.where((lane >= 9) & (lane < 12), pltpu.roll(dlo, 9, 1), aug)
        d0 = jnp.where(lane < 64, aug, d0).astype(BF)
        for y in range(4):
            pay_out[4 * k + y, :, 0:128] = d0
            pay_out[4 * k + y, :, 128:256] = dm[:, 128:256]


def middle_part(meta, pay, tokens, teacher, gains, w_out, w_gu, w_down):
    return pl.pallas_call(
        middle_kernel,
        out_shape=(
            sds((128, D)), sds((8, 128), F32), sds((128, PACKED)), sds((128, D), F32), sds((16, 128, 256)),
        ),
        in_specs=[SM] + [VM] * 5 + [pl.BlockSpec(memory_space=pl.ANY), VM],
        out_specs=(VM,) * 5,
        scratch_shapes=[
            pltpu.VMEM((128, 2 * FF), F32),
            pltpu.VMEM((4, 128, 256), F32),
            pltpu.VMEM((4, 128, 128), F32),
            pltpu.VMEM((1024, 2 * FF), BF),
            pltpu.SemaphoreType.DMA,
        ],
        compiler_params=pltpu.CompilerParams(vmem_limit_bytes=40 * 2**20),
        cost_estimate=pl.CostEstimate(flops=3 * 10**9, bytes_accessed=16 * 2**20, transcendentals=10**6),
        name="middle_part",
    )(meta, pay, tokens, teacher, gains, w_out, w_gu, w_down)


def from_behind(x, axis, j):
    return lax.ppermute(x, axis, [(s, (s + j) % 4) for s in range(4)])


def from_ahead(x, axis, j):
    return lax.ppermute(x, axis, [(s, (s - j) % 4) for s in range(4)])


def from_core(x):
    return lax.ppermute(x, C, [(0, 1), (1, 0)])


def gather4(x, axis):
    return [x] + [from_behind(x, axis, j) for j in (1, 2, 3)]


def in_order(blocks, index, dim):
    r0, r1, r2, r3 = blocks
    twice = jnp.concatenate([r3, r2, r1, r0, r3, r2, r1], axis=dim)
    size = r0.shape[dim]
    return lax.dynamic_slice_in_dim(twice, (3 - index) * size, 4 * size, dim)


def block_of(x, index):
    return lax.dynamic_index_in_dim(x, index, 0, keepdims=False)


def scatter4(x, axis, index):
    own = block_of(x, index).astype(F32)
    far = [from_ahead(block_of(x, (index - j) & 3), axis, j).astype(F32) for j in (1, 2, 3)]
    return (own + far[1]) + (far[0] + far[2])


def summed(parts):
    a, b, c, d = (p.astype(F32) for p in parts)
    return (a + c) + (b + d)


def per_device(
    tokens, attn_gain, w_query, w_key, w_value, w_out, mlp_gain, w_gate, w_up, w_down, segments, teacher
):
    ix, iz, ic, iy = (lax.axis_index(a) for a in (X, Z, C, Y))
    begin = iz * 1024 + ic * 512

    heads, pack = prepare(
        w_query, w_key, w_value, attn_gain, mlp_gain, w_gate, w_up, w_out, w_down
    )
    pack = lax.all_gather(pack, BLK_HD)
    w_rows = lax.all_to_all(heads, BLK_HD, split_axis=0, concat_axis=0, tiled=True)
    w_rows = w_rows.reshape(1024, WIDE)
    t_rows = gather4(tokens, X)

    place = jnp.where(
        jnp.arange(4) == 0, ix, jnp.where(jnp.arange(4) == 1, iz, jnp.where(jnp.arange(4) == 2, ic, iy))
    ).astype(jnp.int32)
    meta, lab = documents(place, segments.reshape(128, 128))
    counted = meta[8].astype(F32)

    exponents = jnp.arange(32, dtype=jnp.float32) * (-2.0 / HEAD_SIZE)
    frequency = jnp.tile(ROPE_BASE**exponents, 4)
    runs = ((ix - jnp.arange(4, dtype=jnp.int32)) & 3) * 4096
    places = runs[:, None] + begin + iy * 128 + jnp.arange(128, dtype=jnp.int32)[None]
    angles = places.astype(F32)[:, :, None] * frequency[None, None, :]
    cosine = jnp.cos(angles)
    sine = jnp.sin(angles) * jnp.where(jnp.arange(128) % 64 < 32, -1.0, 1.0)

    w_rows, t_rows = lax.optimization_barrier((w_rows, t_rows))
    q, kv, w_full, n_rows, gain_rows = project(w_rows, t_rows, cosine, sine)
    q_all, kv_own = gather4(q, Y), gather4(kv, Z)
    q_all, kv_own = lax.optimization_barrier((q_all, kv_own))
    kv_oth = [from_core(kv) for kv in kv_own]

    pay = attend(meta, lab, q_all, kv_own, kv_oth).reshape(16, 128, 256)
    pay = lax.all_to_all(pay, (X, Y), split_axis=0, concat_axis=0, tiled=True)
    w_out_all = jnp.pad(pack[:, :6, 4096:4864].reshape(D, D), ((64, 0), (0, 0)))
    w_down_all = pack[:, :, 4864:].reshape(128, 8, 2, D).transpose(0, 2, 1, 3).reshape(FF, D)
    out, squares, packed, grad_middle, dpay = middle_part(
        meta, pay, tokens, teacher, gain_rows, w_out_all, pack.reshape(1024, -1), w_down_all
    )
    dout = lax.all_to_all(dpay, (X, Y), split_axis=0, concat_axis=0, tiled=True)

    part_a, part_b = weights_back(meta, packed, from_core(packed))
    dout, _, _ = lax.optimization_barrier((dout, part_a, part_b))
    part_a = lax.psum_scatter(part_a.reshape(-1, 128), X, scatter_dimension=0, tiled=True)
    part_a = lax.psum_scatter(part_a, Z, scatter_dimension=0, tiled=True)
    far_b = [from_ahead(part_b[j], Z, j) for j in (1, 2, 3)]

    dq, dkv_own, dkv_oth = attend_back(
        meta, lab, q_all, kv_own, kv_oth, dout.reshape(4, 4, 128, 256)
    )
    dq, dkv_own, dkv_oth, far_b = lax.optimization_barrier((dq, dkv_own, dkv_oth, far_b))
    dq = [dq[0]] + [from_ahead(dq[j], Y, j) for j in (1, 2, 3)]
    dkv_oth = from_core(dkv_oth)
    dkv = [(dkv_own[j].astype(F32) + dkv_oth[j].astype(F32)).astype(BF) for j in range(4)]
    dkv = [dkv[0]] + [from_ahead(dkv[j], Z, j) for j in (1, 2, 3)]
    part_b = summed([part_b[0]] + far_b).astype(BF)
    far_b = [from_ahead(part_b[j], X, j) for j in (1, 2, 3)]
    dq, dkv, far_b, part_a = lax.optimization_barrier((dq, dkv, far_b, part_a))
    part_b = summed([part_b[0]] + far_b).astype(BF)
    u, g = project_back(w_full, n_rows, cosine, sine, squares, dq, dkv)

    gu = jnp.concatenate([part_a[:384], part_b[:384]]).reshape(32, 4, 6, 128)
    gu = gu.transpose(1, 0, 2, 3).reshape(4, 192, 128)
    down = jnp.concatenate([part_a[528:], part_b[384:]]).reshape(6, 4, 16, 128)
    down = down.transpose(1, 0, 2, 3).reshape(4, 96, 128)
    outer = part_a[384:528].reshape(6, 4, 6, 128).transpose(1, 0, 2, 3).reshape(4, 36, 128)
    grads = jnp.concatenate([gu, down, outer], axis=1)
    own_grads = block_of(grads, iy)
    far_grads = [from_ahead(block_of(grads, (iy - j) & 3), Y, j) for j in (1, 2, 3)]
    far_u = [from_ahead(u[j], X, j) for j in (1, 2, 3)]
    g = lax.all_to_all(g.reshape(128, 8, WIDE), BLK_HD, split_axis=0, concat_axis=0, tiled=True)
    g, far_grads, far_u = lax.optimization_barrier((g, far_grads, far_u))
    grads = summed([own_grads] + far_grads)

    u = summed([u[0]] + far_u) * gain_rows[0:1]
    wide = tokens.astype(F32)
    r1 = lax.rsqrt(jnp.mean(wide * wide, axis=1, keepdims=True) + EPSILON)
    n1 = wide * r1
    grad_tokens = grad_middle + r1 * (u - n1 * jnp.mean(u * n1, axis=1, keepdims=True))

    g = jnp.sum(g.reshape(4, 32, 8, WIDE).astype(F32), axis=1)[:, :6]
    loss = jnp.sum(g[:, 0, 576:], axis=0)
    mean_loss = jnp.sum(loss) / (counted * D)
    grad_key, grad_value, grad_query = (
        g[:, :, 192 * k : 192 * k + 192].transpose(1, 0, 2).reshape(6, D) for k in range(3)
    )
    by_row = grad_key * w_key.astype(F32) + grad_value * w_value.astype(F32)
    by_row = by_row + grad_query * w_query.astype(F32)
    grad_attn_gain = jnp.sum(by_row, axis=1) / attn_gain.astype(F32)

    gu = grads[:192].reshape(32, 6, 128).transpose(1, 0, 2).reshape(6, 2 * FF)
    down = grads[192:288].reshape(6, 16, 128).transpose(1, 0, 2).reshape(16, D)
    outer = grads[288:].reshape(6, 6, 128).transpose(1, 0, 2).reshape(6, D)
    grad_gate, grad_up = gu[:, :FF], gu[:, FF:]
    by_row = grad_gate * w_gate.astype(F32) + grad_up * w_up.astype(F32)
    grad_mlp_gain = jnp.sum(by_row, axis=1) / mlp_gain.astype(F32)
    return (
        out,
        grad_tokens.astype(BF),
        mean_loss,
        grad_attn_gain,
        grad_query,
        grad_key,
        grad_value,
        outer,
        grad_mlp_gain,
        grad_gate,
        grad_up,
        down,
    )


def solution(mesh):
    torus = Mesh(mesh.devices.reshape(4, 4, 2, mesh.shape["hd"]), BLK_HD)
    rows, vector = P(BLK_HD, None), P(BLK_HD)
    return jax.shard_map(
        per_device,
        mesh=torus,
        in_specs=(rows, vector, rows, rows, rows, rows, vector, rows, rows, rows, P(), rows),
        out_specs=(rows, rows, P(), vector, rows, rows, rows, rows, vector, rows, rows, rows),
        check_vma=False,
    )
```

```python
import jax
import jax.numpy as jnp
from jax import lax
from jax.experimental import pallas as pl
from jax.experimental.pallas import tpu as pltpu
from jax.sharding import Mesh
from jax.sharding import PartitionSpec as P

HEADS = 12
HEAD_SIZE = 64
D = 768
FF = 2048
EPSILON = 1e-05
ROPE_BASE = 10000.0
X, Z, C, Y = "blk_0", "blk_1", "blk_2", "hd"
BLK = (X, Z, C)
BLK_HD = (X, Z, C, Y)
WIDE = 640

BF = jnp.bfloat16
F32 = jnp.float32
NEG = -1e30
LABEL_LANE = 72
LABELS = 25
NT = (((1,), (1,)), ((), ()))
TN = (((0,), (0,)), ((), ()))
NN = (((1,), (0,)), ((), ()))
LIMIT = 70.0


def mm(a, b, dims=NN):
    return lax.dot_general(a, b, dims, preferred_element_type=F32)


def lanes(rows):
    return lax.broadcasted_iota(jnp.int32, (rows, 128), 1)


def rows_of(rows):
    return lax.broadcasted_iota(jnp.int32, (rows, 128), 0)


def lane_masks():
    lane = lanes(128)
    low = (lane < 64).astype(F32)
    head = rows_of(128) // 64
    first = (head == lane).astype(F32).astype(BF)
    second = ((head == 0) & (lane == 2)).astype(F32).astype(BF)
    return low.astype(BF), (1.0 - low).astype(BF), first, second


def one_lane(n):
    return (lanes(128) == n).astype(F32).astype(BF)


def stage_keys(meta, lab, own, oth, kaug, other):
    ix, iz, ic, iy = (meta[k] for k in range(4))
    lane = lanes(128)
    row = rows_of(128)
    first, last = lab[0:1, :], lab[1:2, :]
    one = ((lane >= 64) & (lane < 66)).astype(F32)
    low, _, _, _ = lane_masks()

    def place(i, _):
        for j in range(4):
            ki = ((ix - i) & 3) * 4 + ((iz - j) & 3)
            for ref, core in ((own[j], ic), (oth[j], 1 - ic)):
                at = pl.multiple_of(ki * 256 + core * 128, 128)
                k0, k1, v1 = (ref[i, :, 128 * n : 128 * n + 128] for n in range(3))
                place_at = ki * 1024 + core * 512 + iy * 128 + row
                outside = (place_at < first) | (place_at >= last)
                half = k1 * low
                kaug[pl.ds(at, 128), 0:128] = k0
                kaug[pl.ds(at, 128), 128:256] = half + jnp.where(outside, NEG, one).astype(BF)
                other(at, k0, half, k1, v1)
        return 0

    lax.fori_loop(0, 4, place, 0)


def split_two(x):
    hi = x.astype(BF).astype(F32)
    return hi, x - hi


def fwd_kernel(meta, lab, *refs):
    out_ref, kaug, vbd, qm, acc, q_in, kv_in, sems = refs[12:]
    fetches = [
        pltpu.make_async_copy(ref, q_in.at[n] if n < 4 else kv_in.at[n - 4], sems.at[n])
        for n, ref in enumerate(refs[0:12])
    ]
    for fetch in fetches[4:] + fetches[:4]:
        fetch.start()
    q_refs = [q_in.at[n] for n in range(4)]
    kv_own, kv_oth = ([kv_in.at[n + at] for n in range(4)] for at in (0, 4))
    for fetch in fetches[4:]:
        fetch.wait()
    ix, iz, ic, iy = (meta[k] for k in range(4))
    lane = lanes(128)
    first, last = lab[0:1, :], lab[1:2, :]
    is_label = (lane >= LABEL_LANE) & (lane < LABEL_LANE + LABELS)
    zeros = jnp.zeros((128, 128), BF)
    low, high, by_head0, by_head1 = lane_masks()
    ones = [one_lane(h) for h in range(3)]

    def value_rows(at, k0, half, k1, v1):
        t = at // 256
        inner = pl.multiple_of(at % 256, 128)
        rows = [pl.ds(256 * h + inner, 128) for h in range(3)]
        vbd[t, rows[0], 0:128] = k1 * high + ones[0]
        vbd[t, rows[0], 128:256] = zeros
        vbd[t, rows[1], 0:128] = ones[1]
        vbd[t, rows[1], 128:256] = v1 * low
        vbd[t, rows[2], 0:128] = ones[2]
        vbd[t, rows[2], 128:256] = v1 * high

    stage_keys(meta, lab, kv_own, kv_oth, kaug, value_rows)
    for fetch in fetches[:4]:
        fetch.wait()
    key_norms = query_norms = jnp.zeros((1, 128), F32)
    for n in range(4):
        for ref, at in ((kaug, pl.ds(1024 * n, 1024)), (q_refs[n], slice(None))):
            whole = ref[at].reshape(-1, 256)
            v0, v1 = whole[:, 0:128], whole[:, 128:256] * low[0:1, :]
            norms = mm(v0 * v0, by_head0) + mm(v1 * v1, by_head1)
            norms = jnp.max(norms, axis=0, keepdims=True)
            if ref is kaug:
                key_norms = jnp.maximum(key_norms, norms)
            else:
                query_norms = jnp.maximum(query_norms, norms)
    bound = key_norms * query_norms
    small = jnp.max(bound) < LIMIT * LIMIT

    def one_run(xr, _):
        i = (ix - xr) & 3
        begin = xr * 4096 + iz * 1024 + ic * 512
        for j in range(4):
            yq = (iy - j) & 3
            q0, q1 = q_refs[j][i, :, 0:128], q_refs[j][i, :, 128:256]
            place = begin + yq * 128 + rows_of(128)
            mine = is_label & (place >= first) & (place < last)
            label = jnp.where(mine, 1.0, 0.0).astype(BF)
            at = [pl.ds(pl.multiple_of(512 * h + yq * 128, 128), 128) for h in range(3)]
            qm[at[0], 0:128] = q0 * low
            qm[at[0], 128:256] = label
            qm[at[1], 0:128] = q0 * high
            qm[at[1], 128:256] = label
            qm[at[2], 0:128] = zeros
            qm[at[2], 128:256] = q1 * low + label
        start = meta[4 + xr]
        end = xr * 4 + iz

        def allowed_keys(t):
            key_row = lax.broadcasted_iota(jnp.int32, (256, 512), 0)
            key_place = t * 1024 + iy * 128 + key_row + jnp.where(key_row >= 128, 512 - 128, 0)
            return key_place <= begin + lax.broadcasted_iota(jnp.int32, (256, 512), 1)

        acc[...] = jnp.zeros((512, 256), F32)

        def fast(tiles, diagonal):
            probs = []
            for t in tiles:
                s = mm(qm[...], kaug[pl.ds(pl.multiple_of(t * 256, 256), 256), :], NT)
                if diagonal:
                    key_lane = lax.broadcasted_iota(jnp.int32, (512, 256), 1)
                    key_place = t * 1024 + iy * 128 + key_lane + jnp.where(key_lane >= 128, 512 - 128, 0)
                    allowed = key_place <= begin + lax.broadcasted_iota(jnp.int32, (512, 256), 0)
                for h in range(3):
                    part = s[512 * h : 512 * h + 512]
                    if diagonal:
                        part = jnp.where(allowed, part, NEG)
                    probs.append(jnp.exp(part).astype(BF))
            probs = jnp.concatenate(probs, axis=1)
            values = vbd[pl.ds(tiles[0], len(tiles))].reshape(768 * len(tiles), 256)
            acc[...] += mm(probs, values)

        def finish(highest):
            a0, a1 = acc[:, 0:128], acc[:, 128:256]
            lane5 = lanes(512)
            some = a0 > 0.0
            mass = jnp.where(some, a0, 1.0)
            inverse = jnp.where(some, 1.0 / mass, 0.0)
            log_mass = jnp.where(some, jnp.log(mass) + highest, NEG)
            hi, lo = split_two(log_mass)
            extra = jnp.where(lane5 < 3, hi, pltpu.roll(lo, 3, 1))
            scaled = [inverse[:, h : h + 1] for h in range(3)]
            o0 = jnp.where(lane5 >= 64, a0 * scaled[0], jnp.where(lane5 < 6, extra, 0.0)).astype(BF)
            o1 = (a1 * jnp.where(lane5 < 64, scaled[1], scaled[2])).astype(BF)
            for yq in range(4):
                at = slice(yq * 128, yq * 128 + 128)
                out_ref[xr, yq, :, 0:128] = o0[at]
                out_ref[xr, yq, :, 128:256] = o1[at]

        @pl.when(small)
        def _():
            def step(t, _):
                fast((start + 2 * t, start + 2 * t + 1), False)
                return 0

            lax.fori_loop(0, (end - start) // 2, step, 0)

            @pl.when(((end - start) & 1) == 1)
            def _():
                fast((end - 1,), False)

            fast((end,), True)
            finish(0.0)

        @pl.when(jnp.logical_not(small))
        def _():
            lane5 = lanes(512)

            def step(t, highs):
                at = pl.ds(pl.multiple_of(t * 256, 256), 256)
                keys = kaug[at, :]
                allowed = allowed_keys(t)
                a0, a1 = acc[:, 0:128], acc[:, 128:256]
                total, fresh, scales = None, [], []
                for h in range(3):
                    s = jnp.where(allowed, mm(keys, qm[512 * h : 512 * h + 512, :], NT), NEG)
                    top = jnp.maximum(highs[h], jnp.max(s, axis=0, keepdims=True))
                    scales.append(jnp.exp(highs[h] - top))
                    p = jnp.where(s < 0.5 * NEG, 0.0, jnp.exp(s - top)).astype(BF)
                    part = mm(p, vbd[t, 256 * h : 256 * h + 256, :], TN)
                    total = part if total is None else total + part
                    fresh.append(top)
                rows = jnp.concatenate(scales + [jnp.zeros((125, 512), F32)], axis=0)
                columns = rows.T
                scales = [columns[:, h : h + 1] for h in range(3)]
                factor0 = jnp.where((lane5 >= 64) | (lane5 == 0), scales[0], 1.0)
                factor0 = jnp.where(lane5 == 1, scales[1], jnp.where(lane5 == 2, scales[2], factor0))
                factor1 = jnp.where(lane5 < 64, scales[1], scales[2])
                acc[:, 0:128] = a0 * factor0 + total[:, 0:128]
                acc[:, 128:256] = a1 * factor1 + total[:, 128:256]
                return tuple(fresh)

            lowest = tuple(jnp.full((1, 512), NEG, F32) for _ in range(3))
            highs = lax.fori_loop(start, end + 1, step, lowest)
            rows = jnp.concatenate(list(highs) + [jnp.zeros((125, 512), F32)], axis=0)
            finish(rows.T)

        return 0

    lax.fori_loop(0, 4, one_run, 0)


def bwd_kernel(meta, lab, *refs):
    q_refs, kv_own, kv_oth, do_ref = refs[0:4], refs[4:8], refs[8:12], refs[12]
    dq_refs, dkv_own, dkv_oth = refs[13:17], refs[17], refs[18]
    kaug, vaug, kt, qa, da, dq_acc, dk_acc, dv_acc, dq_rows = refs[19:]
    ix, iz, ic, iy = (meta[k] for k in range(4))
    lane = lanes(128)
    first, last = lab[0:1, :], lab[1:2, :]
    is_label = (lane >= LABEL_LANE) & (lane < LABEL_LANE + LABELS)
    zeros = jnp.zeros((128, 128), BF)

    low, high, _, _ = lane_masks()
    two = ((lane < 2).astype(F32)).astype(BF)

    def value_rows(at, k0, half, k1, v1):
        vaug[pl.ds(at, 128), 0:128] = k1 * high + two
        vaug[pl.ds(at, 128), 128:256] = v1

    stage_keys(meta, lab, kv_own, kv_oth, kaug, value_rows)

    def turn(t, _):
        at = pl.ds(pl.multiple_of(t * 256, 256), 256)
        kt[t] = kaug[at, :].T
        return 0

    lax.fori_loop(0, 16, turn, 0)
    dk_acc[...] = jnp.zeros_like(dk_acc)
    dv_acc[...] = jnp.zeros_like(dv_acc)

    def one_run(xr, _):
        i = (ix - xr) & 3
        begin = xr * 4096 + iz * 1024 + ic * 512
        for j in range(4):
            yq = (iy - j) & 3
            q0, q1 = q_refs[j][i, :, 0:128], q_refs[j][i, :, 128:256]
            d0, d1 = do_ref[xr, yq, :, 0:128], do_ref[xr, yq, :, 128:256]
            extra = d0.astype(F32)
            place = begin + yq * 128 + rows_of(128)
            mine = is_label & (place >= first) & (place < last)
            label = jnp.where(mine, 1.0, 0.0)
            for h in range(3):
                at = pl.ds(pl.multiple_of(512 * h + yq * 128, 128), 128)
                aug = jnp.where(
                    lane == 64,
                    extra[:, h : h + 1],
                    jnp.where(lane == 65, extra[:, h + 3 : h + 4], label),
                ).astype(BF)
                qa[at, 0:128] = q0 * (low, high, low * high)[h]
                qa[at, 128:256] = (q1 * low + aug) if h == 2 else aug
                aug = jnp.where(
                    lane == 0,
                    extra[:, h + 6 : h + 7],
                    jnp.where(lane == 1, extra[:, h + 9 : h + 10], 0.0),
                ).astype(BF)
                da[at, 0:128] = (d0 * high + aug) if h == 0 else aug
                da[at, 128:256] = d1 * (low * high, low, high)[h]
        start = meta[4 + xr]
        end = xr * 4 + iz
        dq_acc[...] = jnp.zeros_like(dq_acc)

        def tile(t, diagonal):
            at = pl.ds(pl.multiple_of(t * 256, 256), 256)
            keys, values = kaug[at, :], vaug[at, :]
            if diagonal:
                key_row = lax.broadcasted_iota(jnp.int32, (256, 512), 0)
                key_place = t * 1024 + iy * 128 + key_row + jnp.where(key_row >= 128, 512 - 128, 0)
                place = begin + lax.broadcasted_iota(jnp.int32, (256, 512), 1)
                allowed = key_place <= place
            s = mm(keys, qa[...], NT)
            dp = mm(values, da[...], NT)
            probs, grads = [], []
            for h in range(3):
                part = s[:, 512 * h : 512 * h + 512]
                if diagonal:
                    part = jnp.where(allowed, part, NEG)
                p = jnp.exp(part)
                ds = (p * dp[:, 512 * h : 512 * h + 512]).astype(BF)
                probs.append(p.astype(BF))
                grads.append(ds)
                dq_acc[h] += mm(kt[t, 64 * h : 64 * h + 64, :], ds)
            dv_acc[at, :] += mm(jnp.concatenate(probs, axis=1), da[...])
            dk_acc[at, :] += mm(jnp.concatenate(grads, axis=1), qa[...])

        def step(t, _):
            tile(start + 2 * t, False)
            tile(start + 2 * t + 1, False)
            return 0

        lax.fori_loop(0, (end - start) // 2, step, 0)

        @pl.when(((end - start) & 1) == 1)
        def _():
            tile(end - 1, False)

        tile(end, True)
        whole = jnp.concatenate([dq_acc[0], dq_acc[1], dq_acc[2], jnp.zeros((64, 512), F32)], axis=0)
        dq_rows[...] = whole.T.astype(BF)
        for j in range(4):
            yq = (iy - j) & 3
            dq_refs[j][i] = dq_rows[pl.ds(pl.multiple_of(yq * 128, 128), 128), :]
        return 0

    lax.fori_loop(0, 4, one_run, 0)

    def give(i, _):
        for j in range(4):
            ki = ((ix - i) & 3) * 4 + ((iz - j) & 3)
            for ref, core in ((dkv_own, ic), (dkv_oth, 1 - ic)):
                at = pl.ds(pl.multiple_of(ki * 256 + core * 128, 128), 128)
                middle = jnp.where(lane < 64, dk_acc[at, 128:256], dv_acc[at, 0:128])
                ref[j, i, :, 0:128] = dk_acc[at, 0:128].astype(BF)
                ref[j, i, :, 128:256] = middle.astype(BF)
                ref[j, i, :, 256:384] = dv_acc[at, 128:256].astype(BF)
        return 0

    lax.fori_loop(0, 4, give, 0)


def sds(shape, dtype=BF):
    return jax.ShapeDtypeStruct(shape, dtype)


VM = pl.BlockSpec(memory_space=pltpu.VMEM)
SM = pl.BlockSpec(memory_space=pltpu.SMEM)


def attend(meta, lab, q, kv_own, kv_oth):
    return pl.pallas_call(
        fwd_kernel,
        out_shape=sds((4, 4, 128, 256)),
        in_specs=[SM, VM] + [pl.BlockSpec(memory_space=pl.ANY)] * 12,
        out_specs=VM,
        scratch_shapes=[
            pltpu.VMEM((4096, 256), BF),
            pltpu.VMEM((16, 768, 256), BF),
            pltpu.VMEM((1536, 256), BF),
            pltpu.VMEM((512, 256), F32),
            pltpu.VMEM((4, 4, 128, 256), BF),
            pltpu.VMEM((8, 4, 128, 384), BF),
            pltpu.SemaphoreType.DMA((12,)),
        ],
        compiler_params=pltpu.CompilerParams(vmem_limit_bytes=48 * 2**20),
        cost_estimate=pl.CostEstimate(flops=20 * 10**9, bytes_accessed=8 * 2**20, transcendentals=10**7),
        name="attend",
    )(meta, lab, *q, *kv_own, *kv_oth)


def attend_back(meta, lab, q, kv_own, kv_oth, dout):
    outs = pl.pallas_call(
        bwd_kernel,
        out_shape=(sds((4, 128, 256)),) * 4 + (sds((4, 4, 128, 384)),) * 2,
        in_specs=[SM] + [VM] * 14,
        out_specs=(VM,) * 6,
        scratch_shapes=[
            pltpu.VMEM((4096, 256), BF),
            pltpu.VMEM((4096, 256), BF),
            pltpu.VMEM((16, 256, 256), BF),
            pltpu.VMEM((1536, 256), BF),
            pltpu.VMEM((1536, 256), BF),
            pltpu.VMEM((3, 64, 512), F32),
            pltpu.VMEM((4096, 256), F32),
            pltpu.VMEM((4096, 256), F32),
            pltpu.VMEM((512, 256), BF),
        ],
        compiler_params=pltpu.CompilerParams(vmem_limit_bytes=56 * 2**20),
        cost_estimate=pl.CostEstimate(flops=50 * 10**9, bytes_accessed=16 * 2**20, transcendentals=10**7),
        name="attend_back",
    )(meta, lab, *q, *kv_own, *kv_oth, dout)
    return outs[0:4], outs[4], outs[5]


def spread_rows():
    row = lax.broadcasted_iota(jnp.int32, (1024, D), 0)
    column = lax.broadcasted_iota(jnp.int32, (1024, D), 1)
    inner = row % 8
    return jnp.where((inner < 6) & (row // 8 * 6 + inner == column), 1.0, 0.0).astype(BF)


AN = pl.BlockSpec(memory_space=pl.ANY)


def fetch_all(sources, targets, sems):
    copies = [pltpu.make_async_copy(a, b, sems.at[n]) for n, (a, b) in enumerate(zip(sources, targets))]
    for copy in copies:
        copy.start()
    return targets, copies


def documents_kernel(place, seg_ref, meta, lab_ref):
    ix, iz, ic, iy = (place[k] for k in range(4))
    seg = seg_ref[...]
    lane = lax.broadcasted_iota(jnp.int32, (1, 128), 1)
    some = seg != 0
    counted = jnp.sum(some.astype(jnp.int32))
    starts, ends = jnp.zeros((1, 128), jnp.int32), jnp.full((1, 128), 16384, jnp.int32)
    begins = []
    for label in range(LABELS):
        start, end = counted, jnp.int32(16384)
        if label:
            start = jnp.sum((some & (seg < label)).astype(jnp.int32))
            end = jnp.sum((some & (seg <= label)).astype(jnp.int32))
        starts = jnp.where(lane == LABEL_LANE + label, start, starts)
        ends = jnp.where(lane == LABEL_LANE + label, end, ends)
        begins.append(start)
    row = lax.broadcasted_iota(jnp.int32, (8, 128), 0)
    lab_ref[...] = jnp.where(row == 0, starts, ends)
    for k in range(4):
        meta[k] = place[k]
    for xr in range(4):
        at = xr * 32 + iz * 8 + ic * 4
        mine = jnp.sum(jnp.where(lane == 0, seg_ref[pl.ds(at, 1), :], 0))
        first = jnp.int32(0)
        for label in range(LABELS):
            first = jnp.where(mine == label, begins[label], first)
        meta[4 + xr] = lax.shift_right_logical(first, 10)
    meta[8] = counted


def documents(place, segments):
    return pl.pallas_call(
        documents_kernel,
        out_shape=(sds((9,), jnp.int32), sds((8, 128), jnp.int32)),
        in_specs=[SM, VM],
        out_specs=(SM, VM),
        cost_estimate=pl.CostEstimate(flops=10**6, bytes_accessed=10**5, transcendentals=0),
        name="documents",
    )(place, segments)


def prepare_kernel(wq, wk, wv, ga, gm, wg, wu, wo, wd, heads_ref, pack_ref):
    row = lax.broadcasted_iota(jnp.int32, (8, 128), 0)
    lane = lax.broadcasted_iota(jnp.int32, (8, 128), 1)

    def eight(ref, width):
        empty = jnp.zeros((2, width), F32)
        return jnp.concatenate([ref[...].astype(F32), empty], axis=0)

    def column(ref):
        across = jnp.broadcast_to(jnp.pad(ref[...].astype(F32), ((0, 0), (0, 122))), (8, 128))
        return jnp.sum(jnp.where(lane == row, across, 0.0), axis=1, keepdims=True)

    wide = [eight(ref, D) for ref in (wk, wv, wq)]
    gains = jnp.where(lane == 64, column(ga), jnp.where(lane == 65, column(gm), 0.0))
    for g in range(4):
        k, v, q = (pltpu.roll(w, (D - 192 * g) % D, 1)[:, 0:256] if g else w[:, 0:256] for w in wide)
        low = lane < 64
        v = pltpu.roll(v, 64, 1)
        tiles = [
            k[:, 0:128],
            jnp.where(low, k[:, 128:256], v[:, 0:128]),
            v[:, 128:256],
            q[:, 0:128],
            jnp.where(low, q[:, 128:256], gains),
        ]
        block = jnp.concatenate(tiles, axis=1).astype(BF)
        for n in range(16):
            heads_ref[16 * g + n] = block
    pack_ref[:, 0:FF] = eight(wg, FF).astype(BF)
    pack_ref[:, FF : 2 * FF] = eight(wu, FF).astype(BF)
    pack_ref[:, 2 * FF : 2 * FF + D] = eight(wo, D).astype(BF)
    pack_ref[:, 2 * FF + D : 2 * FF + 2 * D] = wd[0:8, :]
    pack_ref[:, 2 * FF + 2 * D : 2 * FF + 3 * D] = wd[8:16, :]


def prepare(wq, wk, wv, ga, gm, wg, wu, wo, wd):
    return pl.pallas_call(
        prepare_kernel,
        out_shape=(sds((64, 8, WIDE)), sds((8, 2 * FF + 3 * D))),
        in_specs=[VM] * 9,
        out_specs=(VM, VM),
        cost_estimate=pl.CostEstimate(flops=10**6, bytes_accessed=2 * 10**6, transcendentals=0),
        name="prepare",
    )(wq, wk, wv, ga.reshape(1, 6), gm.reshape(1, 6), wg, wu, wo, wd)


def project_kernel(
    meta, w_own, w_oth, t0, t1, t2, t3, cos_ref, sin_ref, q_out, kv_out, w_far, n_far, gain_out,
    w_scr, w_in, t_in, q_ref, kv_ref, w_out, n_out, turn_in, sems,
):
    targets = [w_in.at[0], w_in.at[1]] + [t_in.at[n] for n in range(4)] + [turn_in.at[0], turn_in.at[1]]
    sources = (w_own, w_oth, t0, t1, t2, t3, cos_ref, sin_ref)
    (w_own, w_oth, *_, cos_ref, sin_ref), fetches = fetch_all(sources, targets, sems)
    for fetch in fetches[0:2]:
        fetch.wait()
    sent = []

    def give(source, target):
        sent.append(pltpu.make_async_copy(source, target, sems.at[8 + len(sent)]))
        sent[-1].start()

    for ref, core in ((w_own, meta[2]), (w_oth, 1 - meta[2])):
        for chip in range(16):
            at = pl.multiple_of(64 * chip + 32 * core, 32)
            w_scr[pl.ds(at, 32), :] = ref[32 * chip : 32 * chip + 32, :]
    w = mm(spread_rows(), w_scr[...], TN).astype(BF)
    w_out[...] = w
    give(w_out, w_far)
    tail = w[:, 512:640]
    row, lane = lax.broadcasted_iota(jnp.int32, (8, 128), 0), lax.broadcasted_iota(jnp.int32, (8, 128), 1)
    pick = jnp.where(lane == row + 64, 1.0, 0.0).astype(BF)
    gains = mm(pick, tail, NT)
    gain_out[...] = gains
    for fetch in fetches[2:]:
        fetch.wait()
    for i in range(4):
        wide = t_in[i].astype(F32)
        r1 = lax.rsqrt(jnp.mean(wide * wide, axis=1, keepdims=True) + EPSILON)
        n = (wide * r1 * gains[0:1, :]).astype(BF)
        n_out[i] = n
        y = mm(n, w_out[...])
        turned = turn_heads(y, cos_ref[i], sin_ref[i], 0.125)
        kv_ref[i] = turned[:, 0:384].astype(BF)
        q_ref[i] = turned[:, 384:640].astype(BF)
        give(kv_ref.at[i], kv_out.at[i])
        give(q_ref.at[i], q_out.at[i])
    give(n_out, n_far)
    for copy in sent:
        copy.wait()


def turn_heads(y, cosine, sine, scale):
    lane = lax.broadcasted_iota(jnp.int32, y.shape, 1)
    other = jnp.where(lane % 64 < 32, pltpu.roll(y, WIDE - 32, 1), pltpu.roll(y, 32, 1))
    low = lanes(cosine.shape[0]) < 64
    cosines = [cosine, jnp.where(low, cosine, 1.0), jnp.ones_like(cosine), cosine * scale, cosine * scale]
    none = jnp.zeros_like(sine)
    sines = [sine, jnp.where(low, sine, 0.0), none, sine * scale, sine * scale]
    return y * jnp.concatenate(cosines, axis=1) + other * jnp.concatenate(sines, axis=1)


def project(meta, w, rows, cosine, sine):
    return pl.pallas_call(
        project_kernel,
        out_shape=(
            sds((4, 128, 256)), sds((4, 128, 384)), sds((D, WIDE)), sds((4, 128, D)), sds((8, D), F32),
        ),
        in_specs=[SM] + [AN] * 8,
        out_specs=(AN, AN, AN, AN, VM),
        scratch_shapes=[
            pltpu.VMEM((1024, WIDE), BF),
            pltpu.VMEM((2, 512, WIDE), BF),
            pltpu.VMEM((4, 128, D), BF),
            pltpu.VMEM((4, 128, 256), BF),
            pltpu.VMEM((4, 128, 384), BF),
            pltpu.VMEM((D, WIDE), BF),
            pltpu.VMEM((4, 128, D), BF),
            pltpu.VMEM((2, 4, 128, 128), F32),
            pltpu.SemaphoreType.DMA((18,)),
        ],
        compiler_params=pltpu.CompilerParams(vmem_limit_bytes=58 * 2**20),
        cost_estimate=pl.CostEstimate(flops=2 * 10**9, bytes_accessed=4 * 2**20, transcendentals=0),
        name="project",
    )(meta, *w, *rows, cosine, sine)


def project_back_kernel(
    meta, w_ref, n_ref, cos_ref, sin_ref, loss_ref, *refs
):
    outs, (d_scr, g_scr, a_in, b_in, u_scr, g_out, w_in, n_in, turn_in, sems) = refs[8:14], refs[14:]
    targets = [a_in.at[n] for n in range(4)] + [b_in.at[n] for n in range(4)]
    targets = targets + [turn_in.at[0], turn_in.at[1], w_in, n_in]
    sources = (*refs[0:8], cos_ref, sin_ref, w_ref, n_ref)
    landed, fetches = fetch_all(sources, targets, sems)
    cos_ref, sin_ref, w_ref, n_ref = landed[8:12]
    (a0, a1, a2, a3), (b0, b1, b2, b3) = landed[0:4], landed[4:8]
    for fetch in fetches:
        fetch.wait()
    sent = []

    def give(source, n):
        sent.append(pltpu.make_async_copy(source, outs[n], sems.at[12 + n]))
        sent[-1].start()

    keep = jnp.where(lax.broadcasted_iota(jnp.int32, (D, 128), 1) < 64, 1.0, 0.0)
    tail = (w_ref[:, 512:640].astype(F32) * keep).astype(BF)
    w = jnp.concatenate([w_ref[:, 0:512], tail], axis=1)
    for i in range(4):
        dkv = (b0[i].astype(F32) + b2[i].astype(F32)) + (b1[i].astype(F32) + b3[i].astype(F32))
        dq = (a0[i].astype(F32) + a2[i].astype(F32)) + (a1[i].astype(F32) + a3[i].astype(F32))
        dq1 = jnp.where(lanes(128) < 64, dq[:, 128:256], 0.0)
        y = jnp.concatenate([dkv, dq[:, 0:128], dq1], axis=1).astype(BF).astype(F32)
        d = turn_heads(y, cos_ref[i], -sin_ref[i], 0.125).astype(BF)
        d_scr[i * 128 : i * 128 + 128, :] = d
        u_scr[i] = mm(d, w, NT).astype(BF)
        give(u_scr.at[i], i)
    rows = n_ref[...].reshape(512, D)
    g = mm(rows, d_scr[...], TN)
    last = jnp.where(lanes(D) < 64, g[:, 512:640], loss_ref[0:1, :])
    g = jnp.concatenate([g[:, 0:512], last], axis=1).astype(BF)
    g_scr[...] = mm(spread_rows(), g).astype(BF)
    for n, core in enumerate((1 - meta[2], meta[2])):
        for chip in range(16):
            at = pl.multiple_of(64 * chip + 32 * core, 32)
            g_out[n, 32 * chip : 32 * chip + 32, :] = g_scr[pl.ds(at, 32), :]
        give(g_out.at[n], 5 - n)
    for copy in sent:
        copy.wait()


def project_back(meta, w, n, cosine, sine, loss_row, dq, dkv):
    outs = pl.pallas_call(
        project_back_kernel,
        out_shape=(sds((128, D)),) * 4 + (sds((512, WIDE)),) * 2,
        in_specs=[SM] + [AN] * 4 + [VM] + [AN] * 8,
        out_specs=(AN,) * 6,
        scratch_shapes=[
            pltpu.VMEM((512, WIDE), BF),
            pltpu.VMEM((1024, WIDE), BF),
            pltpu.VMEM((4, 4, 128, 256), BF),
            pltpu.VMEM((4, 4, 128, 384), BF),
            pltpu.VMEM((4, 128, D), BF),
            pltpu.VMEM((2, 512, WIDE), BF),
            pltpu.VMEM((D, WIDE), BF),
            pltpu.VMEM((4, 128, D), BF),
            pltpu.VMEM((2, 4, 128, 128), F32),
            pltpu.SemaphoreType.DMA((18,)),
        ],
        compiler_params=pltpu.CompilerParams(vmem_limit_bytes=58 * 2**20),
        cost_estimate=pl.CostEstimate(flops=2 * 10**9, bytes_accessed=6 * 2**20, transcendentals=0),
        name="project_back",
    )(meta, w, n, cosine, sine, loss_row, *dq, *dkv)
    return outs[0:4], outs[4], outs[5]


PACKED = 2 * FF + FF + 3 * D + 1024


A_ROWS, B_ROWS = 384 + 144, 384 + 384


def weights_back_kernel(meta, own, oth, *refs):
    ix, iz, ic = meta[0], meta[1], meta[2]
    a_refs, b_refs = [refs[0].at[k] for k in range(4)], refs[1:5]
    n_t, m_t, h_t, left, rows, held, sems = refs[5:]
    (own, oth), fetches = fetch_all((own, oth), [held.at[0], held.at[1]], sems)
    for fetch in fetches:
        fetch.wait()
    for k, ref in enumerate((own, oth)):
        at = slice(128 * k, 128 * k + 128)
        n_t[:, at] = ref[:, 3 * FF : 3 * FF + D].astype(F32).T
        h_t[:, at] = ref[:, 2 * FF : 3 * FF].T
        for g in range(4):
            first = 3 * FF + 3 * D + 256 * g
            m_t[192 * g : 192 * g + 192, at] = ref[:, first : first + 256].astype(F32).T[64:256, :]
        rows[at, :] = ref[:, 3 * FF + D : 3 * FF + 3 * D]

    def chips(x_outer):
        for m in range(16):
            yield m, m if x_outer else ((ix - m % 4) & 3) * 4 + ((iz - m // 4) & 3)

    def collect(source, x_outer):
        for m, chip in chips(x_outer):
            left[24 * m : 24 * m + 24, :] = source[pl.ds(pl.multiple_of(48 * chip + 24 * ic, 8), 24), :]
        return left[...].astype(BF)

    def collect_hidden(x_outer):
        picked = [
            h_t[pl.ds(pl.multiple_of(128 * chip + 64 * ic, 64), 64), :] for _, chip in chips(x_outer)
        ]
        return jnp.concatenate(picked, axis=0)

    def put(part, outs, at, height):
        for m in range(16):
            block = part[height * m : height * m + height]
            both = jnp.concatenate([block[:, 0:128], block[:, 128:256]], axis=0)
            outs[m // 4][m % 4, pl.ds(at, 2 * height), :] = both.astype(BF)

    def columns(first, k):
        at = pl.ds(pl.multiple_of(first + 256 * k, 256), 256)
        return jnp.concatenate([own[:, at], oth[:, at]], axis=0)

    for outs, first, x_outer in ((a_refs, 0, True), (b_refs, FF, False)):
        features = collect(n_t, x_outer)

        def gate_or_up(k, _):
            put(mm(features, columns(first, k)), outs, pl.multiple_of(48 * k, 48), 24)
            return 0

        lax.fori_loop(0, 8, gate_or_up, 0)
    outer, down = collect(m_t, True), collect_hidden(False)
    for k in range(3):
        put(mm(outer, rows[:, D + 256 * k : D + 256 * k + 256]), a_refs, 384 + 48 * k, 24)
        put(mm(down, rows[:, 256 * k : 256 * k + 256]), b_refs, 384 + 128 * k, 64)


def weights_back(meta, own, oth):
    outs = pl.pallas_call(
        weights_back_kernel,
        out_shape=(sds((4, 4, A_ROWS, 128)),) + (sds((4, B_ROWS, 128)),) * 4,
        in_specs=[SM, AN, AN],
        out_specs=(VM,) * 5,
        scratch_shapes=[
            pltpu.VMEM((D, 256), F32),
            pltpu.VMEM((D, 256), F32),
            pltpu.VMEM((FF, 256), BF),
            pltpu.VMEM((384, 256), F32),
            pltpu.VMEM((256, 2 * D), BF),
            pltpu.VMEM((2, 128, PACKED), BF),
            pltpu.SemaphoreType.DMA((2,)),
        ],
        compiler_params=pltpu.CompilerParams(vmem_limit_bytes=58 * 2**20),
        cost_estimate=pl.CostEstimate(flops=5 * 10**9, bytes_accessed=10 * 2**20, transcendentals=0),
        name="weights_back",
    )(meta, own, oth)
    return outs[0], outs[1:5]


def middle_kernel(
    meta, pay, tok_ref, teach_ref, gains, w_out, w_pack, w_down,
    out_ref, sq_ref, pack_out, gm_ref, pay_far,
    gu_scr, o_scr, lse_scr, w_gu, pay_in, out_in, down_in, pack_ref, pay_out, sems,
):
    sources = [pay.at[pl.ds(4 * g, 4)] for g in range(4)] + [w_out, w_pack.at[:, 0 : 2 * FF], w_down]
    targets = [pay_in.at[pl.ds(4 * g, 4)] for g in range(4)] + [out_in, w_gu, down_in]
    _, fetches = fetch_all(sources, targets, sems)
    pay, w_out, w_down = pay_in, out_in, down_in
    sent = []

    def give(source, target):
        sent.append(pltpu.make_async_copy(source, target, sems.at[7 + len(sent)]))
        sent[-1].start()

    spread = spread_rows()
    lane = lanes(128)
    middle = tok_ref[...].astype(F32)
    for g in range(4):
        fetches[g].wait()
        if g == 0:
            fetches[4].wait()
        tiles = [pay[g * 4 + y].astype(F32) for y in range(4)]
        logs = [t[:, 0:128] + pltpu.roll(t[:, 0:128], 125, 1) for t in tiles]
        logs = [jnp.where(lane < 3, v, 0.0) for v in logs]
        top = jnp.maximum(jnp.maximum(logs[0], logs[1]), jnp.maximum(logs[2], logs[3]))
        shares = [jnp.exp(v - top) for v in logs]
        mass = (shares[0] + shares[1]) + (shares[2] + shares[3])
        o0 = o1 = None
        for t, share in zip(tiles, shares):
            w = share / mass
            p0 = t[:, 0:128] * w[:, 0:1]
            p1 = t[:, 128:256] * jnp.where(lane < 64, w[:, 1:2], w[:, 2:3])
            o0 = p0 if o0 is None else o0 + p0
            o1 = p1 if o1 is None else o1 + p1
        o0 = jnp.where(lane < 64, 0.0, o0)
        lse_scr[g] = top + jnp.log(mass)
        o = jnp.concatenate([o0, o1], axis=1)
        o_scr[g] = o
        pack_ref[:, 3 * FF + 3 * D + 256 * g : 3 * FF + 3 * D + 256 * g + 256] = o.astype(BF)
        middle = middle + mm(o.astype(BF), w_out[192 * g : 192 * g + 256, :])
    r2 = lax.rsqrt(jnp.mean(middle * middle, axis=1, keepdims=True) + EPSILON)
    n2 = middle * r2
    n2b = (n2 * gains[1:2, :]).astype(BF)
    pack_ref[:, 3 * FF : 3 * FF + D] = n2b
    n2p = mm(n2b, spread, NT).astype(BF)
    fetches[5].wait()
    for f in range(4):
        at, up_at = slice(512 * f, 512 * f + 512), slice(FF + 512 * f, FF + 512 * f + 512)
        gate = mm(n2p, w_gu[:, at])
        up = mm(n2p, w_gu[:, up_at])
        gu_scr[:, at] = gate
        gu_scr[:, up_at] = up
        hid = (gate / (1.0 + jnp.exp(-gate)) * up).astype(BF)
        pack_ref[:, 2 * FF + 512 * f : 2 * FF + 512 * f + 512] = hid
    fetches[6].wait()
    total = middle + mm(pack_ref[:, 2 * FF : 3 * FF], w_down[...])
    out_ref[...] = total.astype(BF)
    row = lax.broadcasted_iota(jnp.int32, (128, D), 0)
    mine = meta[0] * 4096 + meta[1] * 1024 + meta[2] * 512 + meta[3] * 128
    diff = jnp.where(row < meta[8] - mine, total - teach_ref[...].astype(F32), 0.0)
    square = diff * diff
    square = sum(square[:, 128 * n : 128 * n + 128] for n in range(6))
    square = jnp.sum(square, axis=0, keepdims=True)
    sq_ref[...] = jnp.broadcast_to(square + pltpu.roll(square, 64, 1), (8, 128))
    g = diff * (16384.0 / jnp.full((1, D), meta[8], jnp.int32).astype(F32))
    gb = g.astype(BF)
    pack_ref[:, 3 * FF + D : 3 * FF + 2 * D] = gb
    give(pack_ref.at[:, 2 * FF : 3 * FF + 2 * D], pack_out.at[:, 2 * FF : 3 * FF + 2 * D])
    give(pack_ref.at[:, 3 * FF + 3 * D : PACKED], pack_out.at[:, 3 * FF + 3 * D : PACKED])
    u = jnp.zeros((128, 1024), F32)
    for f in range(4):
        at, up_at = slice(512 * f, 512 * f + 512), slice(FF + 512 * f, FF + 512 * f + 512)
        gate, up = gu_scr[:, at], gu_scr[:, up_at]
        dh = mm(gb, w_down[at, :], NT)
        sig = 1.0 / (1.0 + jnp.exp(-gate))
        dgate = (dh * up * sig * (1.0 + gate * (1.0 - sig))).astype(BF)
        dup = (dh * gate * sig).astype(BF)
        pack_ref[:, at] = dgate
        pack_ref[:, up_at] = dup
        u = u + mm(dgate, w_gu[:, at], NT) + mm(dup, w_gu[:, up_at], NT)
    give(pack_ref.at[:, 0 : 2 * FF], pack_out.at[:, 0 : 2 * FF])
    u_hi, u_rest = split_two(u)
    u_mid, u_low = split_two(u_rest)
    u = mm(u_hi.astype(BF), spread) + (mm(u_mid.astype(BF), spread) + mm(u_low.astype(BF), spread))
    u = u * gains[1:2, :]
    gm = g + r2 * (u - n2 * jnp.mean(u * n2, axis=1, keepdims=True))
    gm_ref[...] = gm
    gmb = gm.astype(BF)
    pack_ref[:, 3 * FF + 2 * D : 3 * FF + 3 * D] = gmb
    give(pack_ref.at[:, 3 * FF + 2 * D : 3 * FF + 3 * D], pack_out.at[:, 3 * FF + 2 * D : 3 * FF + 3 * D])
    for k in range(4):
        dm = mm(gmb, w_out[192 * k : 192 * k + 256, :], NT).astype(BF)
        d0, d1 = dm[:, 0:128].astype(F32), dm[:, 128:256].astype(F32)
        p0, p1 = d0 * o_scr[k, :, 0:128], d1 * o_scr[k, :, 128:256]
        deltas = [
            jnp.sum(p0, axis=1, keepdims=True),
            jnp.sum(jnp.where(lane < 64, p1, 0.0), axis=1, keepdims=True),
            jnp.sum(jnp.where(lane < 64, 0.0, p1), axis=1, keepdims=True),
        ]
        hi, lo = split_two(-lse_scr[k])
        delta = jnp.where(lane == 0, deltas[0], jnp.where(lane == 1, deltas[1], deltas[2]))
        dhi, dlo = split_two(-delta)
        aug = jnp.where(lane < 3, hi, jnp.where(lane < 6, pltpu.roll(lo, 3, 1), 0.0))
        aug = jnp.where((lane >= 6) & (lane < 9), pltpu.roll(dhi, 6, 1), aug)
        aug = jnp.where((lane >= 9) & (lane < 12), pltpu.roll(dlo, 9, 1), aug)
        d0 = jnp.where(lane < 64, aug, d0).astype(BF)
        for y in range(4):
            pay_out[4 * k + y, :, 0:128] = d0
            pay_out[4 * k + y, :, 128:256] = dm[:, 128:256]
        give(pay_out.at[pl.ds(4 * k, 4)], pay_far.at[pl.ds(4 * k, 4)])
    for copy in sent:
        copy.wait()


def middle_part(meta, pay, tokens, teacher, gains, w_out, w_gu, w_down):
    return pl.pallas_call(
        middle_kernel,
        out_shape=(
            sds((128, D)), sds((8, 128), F32), sds((128, PACKED)), sds((128, D), F32), sds((16, 128, 256)),
        ),
        in_specs=[SM, AN] + [VM] * 3 + [AN] * 3,
        out_specs=(VM, VM, AN, VM, AN),
        scratch_shapes=[
            pltpu.VMEM((128, 2 * FF), F32),
            pltpu.VMEM((4, 128, 256), F32),
            pltpu.VMEM((4, 128, 128), F32),
            pltpu.VMEM((1024, 2 * FF), BF),
            pltpu.VMEM((16, 128, 256), BF),
            pltpu.VMEM((832, D), BF),
            pltpu.VMEM((FF, D), BF),
            pltpu.VMEM((128, PACKED), BF),
            pltpu.VMEM((16, 128, 256), BF),
            pltpu.SemaphoreType.DMA((15,)),
        ],
        compiler_params=pltpu.CompilerParams(vmem_limit_bytes=58 * 2**20),
        cost_estimate=pl.CostEstimate(flops=3 * 10**9, bytes_accessed=16 * 2**20, transcendentals=10**6),
        name="middle_part",
    )(meta, pay, tokens, teacher, gains, w_out, w_gu, w_down)


def from_behind(x, axis, j):
    return lax.ppermute(x, axis, [(s, (s + j) % 4) for s in range(4)])


def from_ahead(x, axis, j):
    return lax.ppermute(x, axis, [(s, (s - j) % 4) for s in range(4)])


def from_core(x):
    return lax.ppermute(x, C, [(0, 1), (1, 0)])


def gather4(x, axis):
    return [x] + [from_behind(x, axis, j) for j in (1, 2, 3)]


def in_order(blocks, index, dim):
    r0, r1, r2, r3 = blocks
    twice = jnp.concatenate([r3, r2, r1, r0, r3, r2, r1], axis=dim)
    size = r0.shape[dim]
    return lax.dynamic_slice_in_dim(twice, (3 - index) * size, 4 * size, dim)


def block_of(x, index):
    return lax.dynamic_index_in_dim(x, index, 0, keepdims=False)


def scatter4(x, axis, index):
    own = block_of(x, index).astype(F32)
    far = [from_ahead(block_of(x, (index - j) & 3), axis, j).astype(F32) for j in (1, 2, 3)]
    return (own + far[1]) + (far[0] + far[2])


def summed(parts):
    a, b, c, d = (p.astype(F32) for p in parts)
    return (a + c) + (b + d)


def per_device(
    tokens, attn_gain, w_query, w_key, w_value, w_out, mlp_gain, w_gate, w_up, w_down, segments, teacher
):
    ix, iz, ic, iy = (lax.axis_index(a) for a in (X, Z, C, Y))
    begin = iz * 1024 + ic * 512

    heads, pack = prepare(
        w_query, w_key, w_value, attn_gain, mlp_gain, w_gate, w_up, w_out, w_down
    )
    pack = lax.all_gather(pack, BLK_HD)
    w_rows = lax.all_to_all(heads, (X, Z, Y), split_axis=0, concat_axis=0, tiled=True)
    w_rows = w_rows.reshape(512, WIDE)
    w_rows = [w_rows, from_core(w_rows)]
    t_rows = gather4(tokens, X)

    place = jnp.where(
        jnp.arange(4) == 0, ix, jnp.where(jnp.arange(4) == 1, iz, jnp.where(jnp.arange(4) == 2, ic, iy))
    ).astype(jnp.int32)
    meta, lab = documents(place, segments.reshape(128, 128))
    counted = meta[8].astype(F32)

    exponents = jnp.arange(32, dtype=jnp.float32) * (-2.0 / HEAD_SIZE)
    frequency = jnp.tile(ROPE_BASE**exponents, 4)
    runs = ((ix - jnp.arange(4, dtype=jnp.int32)) & 3) * 4096
    places = runs[:, None] + begin + iy * 128 + jnp.arange(128, dtype=jnp.int32)[None]
    angles = places.astype(F32)[:, :, None] * frequency[None, None, :]
    cosine = jnp.cos(angles)
    sine = jnp.sin(angles) * jnp.where(jnp.arange(128) % 64 < 32, -1.0, 1.0)

    w_rows, t_rows = lax.optimization_barrier((w_rows, t_rows))
    q, kv, w_full, n_rows, gain_rows = project(meta, w_rows, t_rows, cosine, sine)
    q_all, kv_own = gather4(q, Y), gather4(kv, Z)
    q_all, kv_own = lax.optimization_barrier((q_all, kv_own))
    kv_oth = [from_core(kv) for kv in kv_own]

    pay = attend(meta, lab, q_all, kv_own, kv_oth).reshape(16, 128, 256)
    pay = lax.all_to_all(pay, (X, Y), split_axis=0, concat_axis=0, tiled=True)
    w_out_all = jnp.pad(pack[:, :6, 4096:4864].reshape(D, D), ((64, 0), (0, 0)))
    w_down_all = pack[:, :, 4864:].reshape(128, 8, 2, D).transpose(0, 2, 1, 3).reshape(FF, D)
    out, squares, packed, grad_middle, dpay = middle_part(
        meta, pay, tokens, teacher, gain_rows, w_out_all, pack.reshape(1024, -1), w_down_all
    )
    dout = lax.all_to_all(dpay, (X, Y), split_axis=0, concat_axis=0, tiled=True)

    part_a, part_b = weights_back(meta, packed, from_core(packed))
    dout, _, _ = lax.optimization_barrier((dout, part_a, part_b))
    part_a = lax.psum_scatter(part_a.reshape(-1, 128), X, scatter_dimension=0, tiled=True)
    part_a = lax.psum_scatter(part_a, Z, scatter_dimension=0, tiled=True)
    far_b = [from_ahead(part_b[j], Z, j) for j in (1, 2, 3)]

    dq, dkv_own, dkv_oth = attend_back(
        meta, lab, q_all, kv_own, kv_oth, dout.reshape(4, 4, 128, 256)
    )
    dq, dkv_own, dkv_oth, far_b = lax.optimization_barrier((dq, dkv_own, dkv_oth, far_b))
    dq = [dq[0]] + [from_ahead(dq[j], Y, j) for j in (1, 2, 3)]
    dkv_oth = from_core(dkv_oth)
    dkv = [(dkv_own[j].astype(F32) + dkv_oth[j].astype(F32)).astype(BF) for j in range(4)]
    dkv = [dkv[0]] + [from_ahead(dkv[j], Z, j) for j in (1, 2, 3)]
    part_b = summed([part_b[0]] + far_b).astype(BF)
    far_b = [from_ahead(part_b[j], X, j) for j in (1, 2, 3)]
    dq, dkv, far_b, part_a = lax.optimization_barrier((dq, dkv, far_b, part_a))
    part_b = summed([part_b[0]] + far_b).astype(BF)
    u, keep, send = project_back(meta, w_full, n_rows, cosine, sine, squares, dq, dkv)

    gu = jnp.concatenate([part_a[:384], part_b[:384]]).reshape(32, 4, 6, 128)
    gu = gu.transpose(1, 0, 2, 3).reshape(4, 192, 128)
    down = part_b[384:].reshape(6, 4, 16, 128)
    down = down.transpose(1, 0, 2, 3).reshape(4, 96, 128)
    outer = part_a[384:].reshape(6, 4, 6, 128).transpose(1, 0, 2, 3).reshape(4, 36, 128)
    grads = jnp.concatenate([gu, down, outer], axis=1)
    own_grads = block_of(grads, iy)
    far_grads = [from_ahead(block_of(grads, (iy - j) & 3), Y, j) for j in (1, 2, 3)]
    far_u = [from_ahead(u[j], X, j) for j in (1, 2, 3)]
    g = (keep.astype(F32) + from_core(send).astype(F32)).astype(BF).reshape(64, 8, WIDE)
    g = lax.all_to_all(g, (X, Z, Y), split_axis=0, concat_axis=0, tiled=True)
    g, far_grads, far_u = lax.optimization_barrier((g, far_grads, far_u))
    grads = summed([own_grads] + far_grads)

    u = summed([u[0]] + far_u) * gain_rows[0:1]
    wide = tokens.astype(F32)
    r1 = lax.rsqrt(jnp.mean(wide * wide, axis=1, keepdims=True) + EPSILON)
    n1 = wide * r1
    grad_tokens = grad_middle + r1 * (u - n1 * jnp.mean(u * n1, axis=1, keepdims=True))

    g = jnp.sum(g.reshape(4, 16, 8, WIDE).astype(F32), axis=1)[:, :6]
    loss = jnp.sum(g[:, 0, 576:], axis=0)
    mean_loss = jnp.sum(loss) / (counted * D)
    grad_key, grad_value, grad_query = (
        g[:, :, 192 * k : 192 * k + 192].transpose(1, 0, 2).reshape(6, D) for k in range(3)
    )
    by_row = grad_key * w_key.astype(F32) + grad_value * w_value.astype(F32)
    by_row = by_row + grad_query * w_query.astype(F32)
    grad_attn_gain = jnp.sum(by_row, axis=1) / attn_gain.astype(F32)

    gu = grads[:192].reshape(32, 6, 128).transpose(1, 0, 2).reshape(6, 2 * FF)
    down = grads[192:288].reshape(6, 16, 128).transpose(1, 0, 2).reshape(16, D)
    outer = grads[288:].reshape(6, 6, 128).transpose(1, 0, 2).reshape(6, D)
    grad_gate, grad_up = gu[:, :FF], gu[:, FF:]
    by_row = grad_gate * w_gate.astype(F32) + grad_up * w_up.astype(F32)
    grad_mlp_gain = jnp.sum(by_row, axis=1) / mlp_gain.astype(F32)
    return (
        out,
        grad_tokens.astype(BF),
        mean_loss,
        grad_attn_gain,
        grad_query,
        grad_key,
        grad_value,
        outer,
        grad_mlp_gain,
        grad_gate,
        grad_up,
        down,
    )


def solution(mesh):
    torus = Mesh(mesh.devices.reshape(4, 4, 2, mesh.shape["hd"]), BLK_HD)
    rows, vector = P(BLK_HD, None), P(BLK_HD)
    return jax.shard_map(
        per_device,
        mesh=torus,
        in_specs=(rows, vector, rows, rows, rows, rows, vector, rows, rows, rows, P(), rows),
        out_specs=(rows, rows, P(), vector, rows, rows, rows, rows, vector, rows, rows, rows),
        check_vma=False,
    )
```

```python
import jax
import jax.numpy as jnp
from jax import lax
from jax.experimental import pallas as pl
from jax.experimental.pallas import tpu as pltpu
from jax.sharding import Mesh
from jax.sharding import PartitionSpec as P

HEADS = 12
HEAD_SIZE = 64
D = 768
FF = 2048
EPSILON = 1e-05
ROPE_BASE = 10000.0
X, Z, C, Y = "blk_0", "blk_1", "blk_2", "hd"
BLK = (X, Z, C)
BLK_HD = (X, Z, C, Y)
WIDE = 640

BF = jnp.bfloat16
F32 = jnp.float32
NEG = -1e30
LABEL_LANE = 72
LABELS = 25
NT = (((1,), (1,)), ((), ()))
TN = (((0,), (0,)), ((), ()))
NN = (((1,), (0,)), ((), ()))
LIMIT = 70.0


def mm(a, b, dims=NN):
    return lax.dot_general(a, b, dims, preferred_element_type=F32)


def lanes(rows):
    return lax.broadcasted_iota(jnp.int32, (rows, 128), 1)


def rows_of(rows):
    return lax.broadcasted_iota(jnp.int32, (rows, 128), 0)


def lane_masks():
    lane = lanes(128)
    low = (lane < 64).astype(F32)
    head = rows_of(128) // 64
    first = (head == lane).astype(F32).astype(BF)
    second = ((head == 0) & (lane == 2)).astype(F32).astype(BF)
    return low.astype(BF), (1.0 - low).astype(BF), first, second


def one_lane(n):
    return (lanes(128) == n).astype(F32).astype(BF)


def stage_keys(meta, lab, own, oth, kaug, other):
    ix, iz, ic, iy = (meta[k] for k in range(4))
    lane = lanes(128)
    row = rows_of(128)
    first, last = lab[0:1, :], lab[1:2, :]
    one = ((lane >= 64) & (lane < 66)).astype(F32)
    low, _, _, _ = lane_masks()

    def place(i, _):
        for j in range(4):
            ki = ((ix - i) & 3) * 4 + ((iz - j) & 3)
            for ref, core in ((own[j], ic), (oth[j], 1 - ic)):
                at = pl.multiple_of(ki * 256 + core * 128, 128)
                k0, k1, v1 = (ref[i, :, 128 * n : 128 * n + 128] for n in range(3))
                place_at = ki * 1024 + core * 512 + iy * 128 + row
                outside = (place_at < first) | (place_at >= last)
                half = k1 * low
                kaug[pl.ds(at, 128), 0:128] = k0
                kaug[pl.ds(at, 128), 128:256] = half + jnp.where(outside, NEG, one).astype(BF)
                other(at, k0, half, k1, v1)
        return 0

    lax.fori_loop(0, 4, place, 0)


def split_two(x):
    hi = x.astype(BF).astype(F32)
    return hi, x - hi


def fwd_kernel(meta, lab, *refs):
    out_ref, kaug, vbd, qm, acc, q_in, kv_in, sems = refs[12:]
    fetches = [
        pltpu.make_async_copy(ref, q_in.at[n] if n < 4 else kv_in.at[n - 4], sems.at[n])
        for n, ref in enumerate(refs[0:12])
    ]
    for fetch in fetches[4:] + fetches[:4]:
        fetch.start()
    q_refs = [q_in.at[n] for n in range(4)]
    kv_own, kv_oth = ([kv_in.at[n + at] for n in range(4)] for at in (0, 4))
    for fetch in fetches[4:]:
        fetch.wait()
    ix, iz, ic, iy = (meta[k] for k in range(4))
    lane = lanes(128)
    first, last = lab[0:1, :], lab[1:2, :]
    is_label = (lane >= LABEL_LANE) & (lane < LABEL_LANE + LABELS)
    zeros = jnp.zeros((128, 128), BF)
    low, high, by_head0, by_head1 = lane_masks()
    ones = [one_lane(h) for h in range(3)]

    def value_rows(at, k0, half, k1, v1):
        t = at // 256
        inner = pl.multiple_of(at % 256, 128)
        rows = [pl.ds(256 * h + inner, 128) for h in range(3)]
        vbd[t, rows[0], 0:128] = k1 * high + ones[0]
        vbd[t, rows[0], 128:256] = zeros
        vbd[t, rows[1], 0:128] = ones[1]
        vbd[t, rows[1], 128:256] = v1 * low
        vbd[t, rows[2], 0:128] = ones[2]
        vbd[t, rows[2], 128:256] = v1 * high

    stage_keys(meta, lab, kv_own, kv_oth, kaug, value_rows)
    for fetch in fetches[:4]:
        fetch.wait()
    key_norms = query_norms = jnp.zeros((1, 128), F32)
    for n in range(4):
        for ref, at in ((kaug, pl.ds(1024 * n, 1024)), (q_refs[n], slice(None))):
            whole = ref[at].reshape(-1, 256)
            v0, v1 = whole[:, 0:128], whole[:, 128:256] * low[0:1, :]
            norms = mm(v0 * v0, by_head0) + mm(v1 * v1, by_head1)
            norms = jnp.max(norms, axis=0, keepdims=True)
            if ref is kaug:
                key_norms = jnp.maximum(key_norms, norms)
            else:
                query_norms = jnp.maximum(query_norms, norms)
    bound = key_norms * query_norms
    small = jnp.max(bound) < LIMIT * LIMIT

    def one_run(xr, _):
        i = (ix - xr) & 3
        begin = xr * 4096 + iz * 1024 + ic * 512
        for j in range(4):
            yq = (iy - j) & 3
            q0, q1 = q_refs[j][i, :, 0:128], q_refs[j][i, :, 128:256]
            place = begin + yq * 128 + rows_of(128)
            mine = is_label & (place >= first) & (place < last)
            label = jnp.where(mine, 1.0, 0.0).astype(BF)
            at = [pl.ds(pl.multiple_of(512 * h + yq * 128, 128), 128) for h in range(3)]
            qm[at[0], 0:128] = q0 * low
            qm[at[0], 128:256] = label
            qm[at[1], 0:128] = q0 * high
            qm[at[1], 128:256] = label
            qm[at[2], 0:128] = zeros
            qm[at[2], 128:256] = q1 * low + label
        start = meta[4 + xr]
        end = xr * 4 + iz

        def allowed_keys(t):
            key_row = lax.broadcasted_iota(jnp.int32, (256, 512), 0)
            key_place = t * 1024 + iy * 128 + key_row + jnp.where(key_row >= 128, 512 - 128, 0)
            return key_place <= begin + lax.broadcasted_iota(jnp.int32, (256, 512), 1)

        acc[...] = jnp.zeros((512, 256), F32)

        def fast(tiles, diagonal):
            probs = []
            for t in tiles:
                s = mm(qm[...], kaug[pl.ds(pl.multiple_of(t * 256, 256), 256), :], NT)
                if diagonal:
                    key_lane = lax.broadcasted_iota(jnp.int32, (512, 256), 1)
                    key_place = t * 1024 + iy * 128 + key_lane + jnp.where(key_lane >= 128, 512 - 128, 0)
                    allowed = key_place <= begin + lax.broadcasted_iota(jnp.int32, (512, 256), 0)
                for h in range(3):
                    part = s[512 * h : 512 * h + 512]
                    if diagonal:
                        part = jnp.where(allowed, part, NEG)
                    probs.append(jnp.exp(part).astype(BF))
            probs = jnp.concatenate(probs, axis=1)
            values = vbd[pl.ds(tiles[0], len(tiles))].reshape(768 * len(tiles), 256)
            acc[...] += mm(probs, values)

        def finish(highest):
            a0, a1 = acc[:, 0:128], acc[:, 128:256]
            lane5 = lanes(512)
            some = a0 > 0.0
            mass = jnp.where(some, a0, 1.0)
            inverse = jnp.where(some, 1.0 / mass, 0.0)
            log_mass = jnp.where(some, jnp.log(mass) + highest, NEG)
            hi, lo = split_two(log_mass)
            extra = jnp.where(lane5 < 3, hi, pltpu.roll(lo, 3, 1))
            scaled = [inverse[:, h : h + 1] for h in range(3)]
            o0 = jnp.where(lane5 >= 64, a0 * scaled[0], jnp.where(lane5 < 6, extra, 0.0)).astype(BF)
            o1 = (a1 * jnp.where(lane5 < 64, scaled[1], scaled[2])).astype(BF)
            for yq in range(4):
                at = slice(yq * 128, yq * 128 + 128)
                out_ref[xr, yq, :, 0:128] = o0[at]
                out_ref[xr, yq, :, 128:256] = o1[at]

        @pl.when(small)
        def _():
            def step(t, _):
                fast((start + 2 * t, start + 2 * t + 1), False)
                return 0

            lax.fori_loop(0, (end - start) // 2, step, 0)

            @pl.when(((end - start) & 1) == 1)
            def _():
                fast((end - 1,), False)

            fast((end,), True)
            finish(0.0)

        @pl.when(jnp.logical_not(small))
        def _():
            lane5 = lanes(512)

            def step(t, highs):
                at = pl.ds(pl.multiple_of(t * 256, 256), 256)
                keys = kaug[at, :]
                allowed = allowed_keys(t)
                a0, a1 = acc[:, 0:128], acc[:, 128:256]
                total, fresh, scales = None, [], []
                for h in range(3):
                    s = jnp.where(allowed, mm(keys, qm[512 * h : 512 * h + 512, :], NT), NEG)
                    top = jnp.maximum(highs[h], jnp.max(s, axis=0, keepdims=True))
                    scales.append(jnp.exp(highs[h] - top))
                    p = jnp.where(s < 0.5 * NEG, 0.0, jnp.exp(s - top)).astype(BF)
                    part = mm(p, vbd[t, 256 * h : 256 * h + 256, :], TN)
                    total = part if total is None else total + part
                    fresh.append(top)
                rows = jnp.concatenate(scales + [jnp.zeros((125, 512), F32)], axis=0)
                columns = rows.T
                scales = [columns[:, h : h + 1] for h in range(3)]
                factor0 = jnp.where((lane5 >= 64) | (lane5 == 0), scales[0], 1.0)
                factor0 = jnp.where(lane5 == 1, scales[1], jnp.where(lane5 == 2, scales[2], factor0))
                factor1 = jnp.where(lane5 < 64, scales[1], scales[2])
                acc[:, 0:128] = a0 * factor0 + total[:, 0:128]
                acc[:, 128:256] = a1 * factor1 + total[:, 128:256]
                return tuple(fresh)

            lowest = tuple(jnp.full((1, 512), NEG, F32) for _ in range(3))
            highs = lax.fori_loop(start, end + 1, step, lowest)
            rows = jnp.concatenate(list(highs) + [jnp.zeros((125, 512), F32)], axis=0)
            finish(rows.T)

        return 0

    lax.fori_loop(0, 4, one_run, 0)


def bwd_kernel(meta, lab, *refs):
    q_refs, kv_own, kv_oth, do_ref = refs[0:4], refs[4:8], refs[8:12], refs[12]
    dq_refs, dkv_own, dkv_oth = refs[13:17], refs[17], refs[18]
    kaug, vaug, kt, qa, da, dq_acc, dk_acc, dv_acc, dq_rows = refs[19:]
    ix, iz, ic, iy = (meta[k] for k in range(4))
    lane = lanes(128)
    first, last = lab[0:1, :], lab[1:2, :]
    is_label = (lane >= LABEL_LANE) & (lane < LABEL_LANE + LABELS)
    zeros = jnp.zeros((128, 128), BF)

    low, high, _, _ = lane_masks()
    two = ((lane < 2).astype(F32)).astype(BF)
    row = rows_of(128)

    def pick(pairs):
        chosen = [(row == a) & (lane == b) for a, b in pairs]
        return jnp.where(chosen[0] | chosen[1], 1.0, 0.0).astype(BF)

    shift_pick = [pick(((h, 64), (h + 3, 65))) for h in range(3)]
    delta_pick = [pick(((h + 6, 0), (h + 9, 1))) for h in range(3)]

    def value_rows(at, k0, half, k1, v1):
        vaug[pl.ds(at, 128), 0:128] = k1 * high + two
        vaug[pl.ds(at, 128), 128:256] = v1

    stage_keys(meta, lab, kv_own, kv_oth, kaug, value_rows)

    def turn(t, _):
        at = pl.ds(pl.multiple_of(t * 256, 256), 256)
        kt[t] = kaug[at, :].T
        return 0

    lax.fori_loop(0, 16, turn, 0)
    dk_acc[...] = jnp.zeros_like(dk_acc)
    dv_acc[...] = jnp.zeros_like(dv_acc)

    def one_run(xr, _):
        i = (ix - xr) & 3
        begin = xr * 4096 + iz * 1024 + ic * 512
        for j in range(4):
            yq = (iy - j) & 3
            q0, q1 = q_refs[j][i, :, 0:128], q_refs[j][i, :, 128:256]
            d0, d1 = do_ref[xr, yq, :, 0:128], do_ref[xr, yq, :, 128:256]
            place = begin + yq * 128 + rows_of(128)
            mine = is_label & (place >= first) & (place < last)
            label = jnp.where(mine, 1.0, 0.0)
            for h in range(3):
                at = pl.ds(pl.multiple_of(512 * h + yq * 128, 128), 128)
                aug = (mm(d0, shift_pick[h]) + label).astype(BF)
                qa[at, 0:128] = q0 * (low, high, low * high)[h]
                qa[at, 128:256] = (q1 * low + aug) if h == 2 else aug
                aug = mm(d0, delta_pick[h]).astype(BF)
                da[at, 0:128] = (d0 * high + aug) if h == 0 else aug
                da[at, 128:256] = d1 * (low * high, low, high)[h]
        start = meta[4 + xr]
        end = xr * 4 + iz
        dq_acc[...] = jnp.zeros_like(dq_acc)

        def tile(t, diagonal):
            at = pl.ds(pl.multiple_of(t * 256, 256), 256)
            keys, values = kaug[at, :], vaug[at, :]
            if diagonal:
                key_row = lax.broadcasted_iota(jnp.int32, (256, 512), 0)
                key_place = t * 1024 + iy * 128 + key_row + jnp.where(key_row >= 128, 512 - 128, 0)
                place = begin + lax.broadcasted_iota(jnp.int32, (256, 512), 1)
                allowed = key_place <= place
            s = mm(keys, qa[...], NT)
            dp = mm(values, da[...], NT)
            probs, grads = [], []
            for h in range(3):
                part = s[:, 512 * h : 512 * h + 512]
                if diagonal:
                    part = jnp.where(allowed, part, NEG)
                p = jnp.exp(part)
                ds = (p * dp[:, 512 * h : 512 * h + 512]).astype(BF)
                probs.append(p.astype(BF))
                grads.append(ds)
                dq_acc[h] += mm(kt[t, 64 * h : 64 * h + 64, :], ds)
            dv_acc[at, :] += mm(jnp.concatenate(probs, axis=1), da[...])
            dk_acc[at, :] += mm(jnp.concatenate(grads, axis=1), qa[...])

        def step(t, _):
            tile(start + 2 * t, False)
            tile(start + 2 * t + 1, False)
            return 0

        lax.fori_loop(0, (end - start) // 2, step, 0)

        @pl.when(((end - start) & 1) == 1)
        def _():
            tile(end - 1, False)

        tile(end, True)
        whole = jnp.concatenate([dq_acc[0], dq_acc[1], dq_acc[2], jnp.zeros((64, 512), F32)], axis=0)
        dq_rows[...] = whole.T.astype(BF)
        for j in range(4):
            yq = (iy - j) & 3
            dq_refs[j][i] = dq_rows[pl.ds(pl.multiple_of(yq * 128, 128), 128), :]
        return 0

    lax.fori_loop(0, 4, one_run, 0)

    def give(i, _):
        for j in range(4):
            ki = ((ix - i) & 3) * 4 + ((iz - j) & 3)
            for ref, core in ((dkv_own, ic), (dkv_oth, 1 - ic)):
                at = pl.ds(pl.multiple_of(ki * 256 + core * 128, 128), 128)
                middle = jnp.where(lane < 64, dk_acc[at, 128:256], dv_acc[at, 0:128])
                ref[j, i, :, 0:128] = dk_acc[at, 0:128].astype(BF)
                ref[j, i, :, 128:256] = middle.astype(BF)
                ref[j, i, :, 256:384] = dv_acc[at, 128:256].astype(BF)
        return 0

    lax.fori_loop(0, 4, give, 0)


def sds(shape, dtype=BF):
    return jax.ShapeDtypeStruct(shape, dtype)


VM = pl.BlockSpec(memory_space=pltpu.VMEM)
SM = pl.BlockSpec(memory_space=pltpu.SMEM)


def attend(meta, lab, q, kv_own, kv_oth):
    return pl.pallas_call(
        fwd_kernel,
        out_shape=sds((4, 4, 128, 256)),
        in_specs=[SM, VM] + [pl.BlockSpec(memory_space=pl.ANY)] * 12,
        out_specs=VM,
        scratch_shapes=[
            pltpu.VMEM((4096, 256), BF),
            pltpu.VMEM((16, 768, 256), BF),
            pltpu.VMEM((1536, 256), BF),
            pltpu.VMEM((512, 256), F32),
            pltpu.VMEM((4, 4, 128, 256), BF),
            pltpu.VMEM((8, 4, 128, 384), BF),
            pltpu.SemaphoreType.DMA((12,)),
        ],
        compiler_params=pltpu.CompilerParams(vmem_limit_bytes=58 * 2**20),
        cost_estimate=pl.CostEstimate(flops=20 * 10**9, bytes_accessed=8 * 2**20, transcendentals=10**7),
        name="attend",
    )(meta, lab, *q, *kv_own, *kv_oth)


def attend_back(meta, lab, q, kv_own, kv_oth, dout):
    outs = pl.pallas_call(
        bwd_kernel,
        out_shape=(sds((4, 128, 256)),) * 4 + (sds((4, 4, 128, 384)),) * 2,
        in_specs=[SM] + [VM] * 14,
        out_specs=(VM,) * 6,
        scratch_shapes=[
            pltpu.VMEM((4096, 256), BF),
            pltpu.VMEM((4096, 256), BF),
            pltpu.VMEM((16, 256, 256), BF),
            pltpu.VMEM((1536, 256), BF),
            pltpu.VMEM((1536, 256), BF),
            pltpu.VMEM((3, 64, 512), F32),
            pltpu.VMEM((4096, 256), F32),
            pltpu.VMEM((4096, 256), F32),
            pltpu.VMEM((512, 256), BF),
        ],
        compiler_params=pltpu.CompilerParams(vmem_limit_bytes=56 * 2**20),
        cost_estimate=pl.CostEstimate(flops=50 * 10**9, bytes_accessed=16 * 2**20, transcendentals=10**7),
        name="attend_back",
    )(meta, lab, *q, *kv_own, *kv_oth, dout)
    return outs[0:4], outs[4], outs[5]


def spread_rows():
    row = lax.broadcasted_iota(jnp.int32, (1024, D), 0)
    column = lax.broadcasted_iota(jnp.int32, (1024, D), 1)
    inner = row % 8
    return jnp.where((inner < 6) & (row // 8 * 6 + inner == column), 1.0, 0.0).astype(BF)


AN = pl.BlockSpec(memory_space=pl.ANY)


def fetch_all(sources, targets, sems):
    copies = [pltpu.make_async_copy(a, b, sems.at[n]) for n, (a, b) in enumerate(zip(sources, targets))]
    for copy in copies:
        copy.start()
    return targets, copies


def documents_kernel(place, seg_ref, meta, lab_ref):
    ix, iz, ic, iy = (place[k] for k in range(4))
    seg = seg_ref[...]
    lane = lax.broadcasted_iota(jnp.int32, (1, 128), 1)
    some = seg != 0
    counted = jnp.sum(some.astype(jnp.int32))
    starts, ends = jnp.zeros((1, 128), jnp.int32), jnp.full((1, 128), 16384, jnp.int32)
    begins = []
    for label in range(LABELS):
        start, end = counted, jnp.int32(16384)
        if label:
            start = jnp.sum((some & (seg < label)).astype(jnp.int32))
            end = jnp.sum((some & (seg <= label)).astype(jnp.int32))
        starts = jnp.where(lane == LABEL_LANE + label, start, starts)
        ends = jnp.where(lane == LABEL_LANE + label, end, ends)
        begins.append(start)
    row = lax.broadcasted_iota(jnp.int32, (8, 128), 0)
    lab_ref[...] = jnp.where(row == 0, starts, ends)
    for k in range(4):
        meta[k] = place[k]
    for xr in range(4):
        at = xr * 32 + iz * 8 + ic * 4
        mine = jnp.sum(jnp.where(lane == 0, seg_ref[pl.ds(at, 1), :], 0))
        first = jnp.int32(0)
        for label in range(LABELS):
            first = jnp.where(mine == label, begins[label], first)
        meta[4 + xr] = lax.shift_right_logical(first, 10)
    meta[8] = counted


def documents(place, segments):
    return pl.pallas_call(
        documents_kernel,
        out_shape=(sds((9,), jnp.int32), sds((8, 128), jnp.int32)),
        in_specs=[SM, VM],
        out_specs=(SM, VM),
        cost_estimate=pl.CostEstimate(flops=10**6, bytes_accessed=10**5, transcendentals=0),
        name="documents",
    )(place, segments)


def prepare_kernel(wq, wk, wv, ga, gm, wg, wu, wo, wd, heads_ref, pack_ref):
    row = lax.broadcasted_iota(jnp.int32, (8, 128), 0)
    lane = lax.broadcasted_iota(jnp.int32, (8, 128), 1)

    def eight(ref, width):
        empty = jnp.zeros((2, width), F32)
        return jnp.concatenate([ref[...].astype(F32), empty], axis=0)

    def column(ref):
        across = jnp.broadcast_to(jnp.pad(ref[...].astype(F32), ((0, 0), (0, 122))), (8, 128))
        return jnp.sum(jnp.where(lane == row, across, 0.0), axis=1, keepdims=True)

    wide = [eight(ref, D) for ref in (wk, wv, wq)]
    gains = jnp.where(lane == 64, column(ga), jnp.where(lane == 65, column(gm), 0.0))
    for g in range(4):
        k, v, q = (pltpu.roll(w, (D - 192 * g) % D, 1)[:, 0:256] if g else w[:, 0:256] for w in wide)
        low = lane < 64
        v = pltpu.roll(v, 64, 1)
        tiles = [
            k[:, 0:128],
            jnp.where(low, k[:, 128:256], v[:, 0:128]),
            v[:, 128:256],
            q[:, 0:128],
            jnp.where(low, q[:, 128:256], gains),
        ]
        block = jnp.concatenate(tiles, axis=1).astype(BF)
        for n in range(16):
            heads_ref[16 * g + n] = block
    pack_ref[:, 0:FF] = eight(wg, FF).astype(BF)
    pack_ref[:, FF : 2 * FF] = eight(wu, FF).astype(BF)
    pack_ref[:, 2 * FF : 2 * FF + D] = eight(wo, D).astype(BF)
    pack_ref[:, 2 * FF + D : 2 * FF + 2 * D] = wd[0:8, :]
    pack_ref[:, 2 * FF + 2 * D : 2 * FF + 3 * D] = wd[8:16, :]


def prepare(wq, wk, wv, ga, gm, wg, wu, wo, wd):
    return pl.pallas_call(
        prepare_kernel,
        out_shape=(sds((64, 8, WIDE)), sds((8, 2 * FF + 3 * D))),
        in_specs=[VM] * 9,
        out_specs=(VM, VM),
        cost_estimate=pl.CostEstimate(flops=10**6, bytes_accessed=2 * 10**6, transcendentals=0),
        name="prepare",
    )(wq, wk, wv, ga.reshape(1, 6), gm.reshape(1, 6), wg, wu, wo, wd)


def close_rows():
    row = lax.broadcasted_iota(jnp.int32, (D, 1024), 0)
    column = lax.broadcasted_iota(jnp.int32, (D, 1024), 1)
    inner = column % 8
    return jnp.where((inner < 6) & (column // 8 * 6 + inner == row), 1.0, 0.0).astype(BF)


def project_kernel(
    meta, w_own, w_oth, t0, t1, t2, t3, cos_ref, sin_ref, q_out, kv_out, w_far, n_far, gain_out,
    w_scr, w_in, t_in, q_ref, kv_ref, w_out, n_out, turn_in, sems,
):
    targets = [w_in.at[0], w_in.at[1]] + [t_in.at[n] for n in range(4)] + [turn_in.at[0], turn_in.at[1]]
    sources = (w_own, w_oth, t0, t1, t2, t3, cos_ref, sin_ref)
    (w_own, w_oth, *_, cos_ref, sin_ref), fetches = fetch_all(sources, targets, sems)
    for fetch in fetches[0:2]:
        fetch.wait()
    sent = []

    def give(source, target):
        sent.append(pltpu.make_async_copy(source, target, sems.at[8 + len(sent)]))
        sent[-1].start()

    for ref, core in ((w_own, meta[2]), (w_oth, 1 - meta[2])):
        for chip in range(16):
            at = pl.multiple_of(64 * chip + 32 * core, 32)
            w_scr[pl.ds(at, 32), :] = ref[32 * chip : 32 * chip + 32, :]
    w = mm(close_rows(), w_scr[...]).astype(BF)
    w_out[...] = w
    give(w_out, w_far)
    tail = w[:, 512:640]
    row, lane = lax.broadcasted_iota(jnp.int32, (8, 128), 0), lax.broadcasted_iota(jnp.int32, (8, 128), 1)
    pick = jnp.where(lane == row + 64, 1.0, 0.0).astype(BF)
    gains = mm(pick, tail, NT)
    gain_out[...] = gains
    for fetch in fetches[2:]:
        fetch.wait()
    for i in range(4):
        wide = t_in[i].astype(F32)
        r1 = lax.rsqrt(jnp.mean(wide * wide, axis=1, keepdims=True) + EPSILON)
        n = (wide * r1 * gains[0:1, :]).astype(BF)
        n_out[i] = n
        y = mm(n, w_out[...])
        turned = turn_heads(y, cos_ref[i], sin_ref[i], 0.125)
        kv_ref[i] = turned[:, 0:384].astype(BF)
        q_ref[i] = turned[:, 384:640].astype(BF)
        give(kv_ref.at[i], kv_out.at[i])
        give(q_ref.at[i], q_out.at[i])
    give(n_out, n_far)
    for copy in sent:
        copy.wait()


def turn_heads(y, cosine, sine, scale):
    lane = lax.broadcasted_iota(jnp.int32, y.shape, 1)
    other = jnp.where(lane % 64 < 32, pltpu.roll(y, WIDE - 32, 1), pltpu.roll(y, 32, 1))
    low = lanes(cosine.shape[0]) < 64
    cosines = [cosine, jnp.where(low, cosine, 1.0), jnp.ones_like(cosine), cosine * scale, cosine * scale]
    none = jnp.zeros_like(sine)
    sines = [sine, jnp.where(low, sine, 0.0), none, sine * scale, sine * scale]
    return y * jnp.concatenate(cosines, axis=1) + other * jnp.concatenate(sines, axis=1)


def project(meta, w, rows, cosine, sine):
    return pl.pallas_call(
        project_kernel,
        out_shape=(
            sds((4, 128, 256)), sds((4, 128, 384)), sds((D, WIDE)), sds((4, 128, D)), sds((8, D), F32),
        ),
        in_specs=[SM] + [AN] * 8,
        out_specs=(AN, AN, AN, AN, VM),
        scratch_shapes=[
            pltpu.VMEM((1024, WIDE), BF),
            pltpu.VMEM((2, 512, WIDE), BF),
            pltpu.VMEM((4, 128, D), BF),
            pltpu.VMEM((4, 128, 256), BF),
            pltpu.VMEM((4, 128, 384), BF),
            pltpu.VMEM((D, WIDE), BF),
            pltpu.VMEM((4, 128, D), BF),
            pltpu.VMEM((2, 4, 128, 128), F32),
            pltpu.SemaphoreType.DMA((18,)),
        ],
        compiler_params=pltpu.CompilerParams(vmem_limit_bytes=58 * 2**20),
        cost_estimate=pl.CostEstimate(flops=2 * 10**9, bytes_accessed=4 * 2**20, transcendentals=0),
        name="project",
    )(meta, *w, *rows, cosine, sine)


def project_back_kernel(
    meta, w_ref, n_ref, cos_ref, sin_ref, loss_ref, *refs
):
    outs, (d_scr, g_scr, a_in, b_in, u_scr, g_out, w_in, n_in, turn_in, sems) = refs[8:14], refs[14:]
    targets = [a_in.at[n] for n in range(4)] + [b_in.at[n] for n in range(4)]
    targets = targets + [turn_in.at[0], turn_in.at[1], w_in, n_in]
    sources = (*refs[0:8], cos_ref, sin_ref, w_ref, n_ref)
    landed, fetches = fetch_all(sources, targets, sems)
    cos_ref, sin_ref, w_ref, n_ref = landed[8:12]
    (a0, a1, a2, a3), (b0, b1, b2, b3) = landed[0:4], landed[4:8]
    for fetch in fetches:
        fetch.wait()
    sent = []

    def give(source, n):
        sent.append(pltpu.make_async_copy(source, outs[n], sems.at[12 + n]))
        sent[-1].start()

    keep = jnp.where(lax.broadcasted_iota(jnp.int32, (D, 128), 1) < 64, 1.0, 0.0)
    tail = (w_ref[:, 512:640].astype(F32) * keep).astype(BF)
    w = jnp.concatenate([w_ref[:, 0:512], tail], axis=1)
    for i in range(4):
        dkv = (b0[i].astype(F32) + b2[i].astype(F32)) + (b1[i].astype(F32) + b3[i].astype(F32))
        dq = (a0[i].astype(F32) + a2[i].astype(F32)) + (a1[i].astype(F32) + a3[i].astype(F32))
        dq1 = jnp.where(lanes(128) < 64, dq[:, 128:256], 0.0)
        y = jnp.concatenate([dkv, dq[:, 0:128], dq1], axis=1).astype(BF).astype(F32)
        d = turn_heads(y, cos_ref[i], -sin_ref[i], 0.125).astype(BF)
        d_scr[i * 128 : i * 128 + 128, :] = d
        u_scr[i] = mm(d, w, NT).astype(BF)
        give(u_scr.at[i], i)
    rows = n_ref[...].reshape(512, D)
    g = mm(rows, d_scr[...], TN)
    last = jnp.where(lanes(D) < 64, g[:, 512:640], loss_ref[0:1, :])
    g = jnp.concatenate([g[:, 0:512], last], axis=1).astype(BF)
    g_scr[...] = mm(spread_rows(), g).astype(BF)
    for n, core in enumerate((1 - meta[2], meta[2])):
        for chip in range(16):
            at = pl.multiple_of(64 * chip + 32 * core, 32)
            g_out[n, 32 * chip : 32 * chip + 32, :] = g_scr[pl.ds(at, 32), :]
        give(g_out.at[n], 5 - n)
    for copy in sent:
        copy.wait()


def project_back(meta, w, n, cosine, sine, loss_row, dq, dkv):
    outs = pl.pallas_call(
        project_back_kernel,
        out_shape=(sds((128, D)),) * 4 + (sds((512, WIDE)),) * 2,
        in_specs=[SM] + [AN] * 4 + [VM] + [AN] * 8,
        out_specs=(AN,) * 6,
        scratch_shapes=[
            pltpu.VMEM((512, WIDE), BF),
            pltpu.VMEM((1024, WIDE), BF),
            pltpu.VMEM((4, 4, 128, 256), BF),
            pltpu.VMEM((4, 4, 128, 384), BF),
            pltpu.VMEM((4, 128, D), BF),
            pltpu.VMEM((2, 512, WIDE), BF),
            pltpu.VMEM((D, WIDE), BF),
            pltpu.VMEM((4, 128, D), BF),
            pltpu.VMEM((2, 4, 128, 128), F32),
            pltpu.SemaphoreType.DMA((18,)),
        ],
        compiler_params=pltpu.CompilerParams(vmem_limit_bytes=58 * 2**20),
        cost_estimate=pl.CostEstimate(flops=2 * 10**9, bytes_accessed=6 * 2**20, transcendentals=0),
        name="project_back",
    )(meta, w, n, cosine, sine, loss_row, *dq, *dkv)
    return outs[0:4], outs[4], outs[5]


PACKED = 2 * FF + FF + 3 * D + 1024


A_ROWS, B_ROWS = 384 + 144, 384 + 384


def weights_back_kernel(meta, own, oth, *refs):
    ix, iz, ic = meta[0], meta[1], meta[2]
    a_refs, b_refs = [refs[0].at[k] for k in range(4)], refs[1:5]
    n_t, m_t, h_t, left, rows, held, sems = refs[5:]
    (own, oth), fetches = fetch_all((own, oth), [held.at[0], held.at[1]], sems)
    for fetch in fetches:
        fetch.wait()
    for k, ref in enumerate((own, oth)):
        at = slice(128 * k, 128 * k + 128)
        n_t[:, at] = ref[:, 3 * FF : 3 * FF + D].astype(F32).T
        h_t[:, at] = ref[:, 2 * FF : 3 * FF].T
        for g in range(4):
            first = 3 * FF + 3 * D + 256 * g
            m_t[192 * g : 192 * g + 192, at] = ref[:, first : first + 256].astype(F32).T[64:256, :]
        rows[at, :] = ref[:, 3 * FF + D : 3 * FF + 3 * D]

    def chips(x_outer):
        for m in range(16):
            yield m, m if x_outer else ((ix - m % 4) & 3) * 4 + ((iz - m // 4) & 3)

    def collect(source, x_outer):
        for m, chip in chips(x_outer):
            left[24 * m : 24 * m + 24, :] = source[pl.ds(pl.multiple_of(48 * chip + 24 * ic, 8), 24), :]
        return left[...].astype(BF)

    def collect_hidden(x_outer):
        picked = [
            h_t[pl.ds(pl.multiple_of(128 * chip + 64 * ic, 64), 64), :] for _, chip in chips(x_outer)
        ]
        return jnp.concatenate(picked, axis=0)

    def put(part, outs, at, height):
        for m in range(16):
            block = part[height * m : height * m + height]
            both = jnp.concatenate([block[:, 0:128], block[:, 128:256]], axis=0)
            outs[m // 4][m % 4, pl.ds(at, 2 * height), :] = both.astype(BF)

    def columns(first, k):
        at = pl.ds(pl.multiple_of(first + 256 * k, 256), 256)
        return jnp.concatenate([own[:, at], oth[:, at]], axis=0)

    for outs, first, x_outer in ((a_refs, 0, True), (b_refs, FF, False)):
        features = collect(n_t, x_outer)

        def gate_or_up(k, _):
            put(mm(features, columns(first, k)), outs, pl.multiple_of(48 * k, 48), 24)
            return 0

        lax.fori_loop(0, 8, gate_or_up, 0)
    outer, down = collect(m_t, True), collect_hidden(False)
    for k in range(3):
        put(mm(outer, rows[:, D + 256 * k : D + 256 * k + 256]), a_refs, 384 + 48 * k, 24)
        put(mm(down, rows[:, 256 * k : 256 * k + 256]), b_refs, 384 + 128 * k, 64)


def weights_back(meta, own, oth):
    outs = pl.pallas_call(
        weights_back_kernel,
        out_shape=(sds((4, 4, A_ROWS, 128)),) + (sds((4, B_ROWS, 128)),) * 4,
        in_specs=[SM, AN, AN],
        out_specs=(VM,) * 5,
        scratch_shapes=[
            pltpu.VMEM((D, 256), F32),
            pltpu.VMEM((D, 256), F32),
            pltpu.VMEM((FF, 256), BF),
            pltpu.VMEM((384, 256), F32),
            pltpu.VMEM((256, 2 * D), BF),
            pltpu.VMEM((2, 128, PACKED), BF),
            pltpu.SemaphoreType.DMA((2,)),
        ],
        compiler_params=pltpu.CompilerParams(vmem_limit_bytes=58 * 2**20),
        cost_estimate=pl.CostEstimate(flops=5 * 10**9, bytes_accessed=10 * 2**20, transcendentals=0),
        name="weights_back",
    )(meta, own, oth)
    return outs[0], outs[1:5]


def middle_kernel(
    meta, pay, tok_ref, teach_ref, gains, w_out, w_pack, w_down,
    out_ref, sq_ref, pack_out, gm_ref, pay_far,
    gu_scr, o_scr, lse_scr, w_gu, pay_in, out_in, down_in, pack_ref, pay_out, sems,
):
    sources = [pay.at[pl.ds(4 * g, 4)] for g in range(4)] + [w_out, w_pack.at[:, 0 : 2 * FF], w_down]
    targets = [pay_in.at[pl.ds(4 * g, 4)] for g in range(4)] + [out_in, w_gu, down_in]
    _, fetches = fetch_all(sources, targets, sems)
    pay, w_out, w_down = pay_in, out_in, down_in
    sent = []

    def give(source, target):
        sent.append(pltpu.make_async_copy(source, target, sems.at[7 + len(sent)]))
        sent[-1].start()

    spread = spread_rows()
    lane = lanes(128)
    middle = tok_ref[...].astype(F32)
    for g in range(4):
        fetches[g].wait()
        if g == 0:
            fetches[4].wait()
        tiles = [pay[g * 4 + y].astype(F32) for y in range(4)]
        logs = [t[:, 0:128] + pltpu.roll(t[:, 0:128], 125, 1) for t in tiles]
        logs = [jnp.where(lane < 3, v, 0.0) for v in logs]
        top = jnp.maximum(jnp.maximum(logs[0], logs[1]), jnp.maximum(logs[2], logs[3]))
        shares = [jnp.exp(v - top) for v in logs]
        mass = (shares[0] + shares[1]) + (shares[2] + shares[3])
        o0 = o1 = None
        for t, share in zip(tiles, shares):
            w = share / mass
            p0 = t[:, 0:128] * w[:, 0:1]
            p1 = t[:, 128:256] * jnp.where(lane < 64, w[:, 1:2], w[:, 2:3])
            o0 = p0 if o0 is None else o0 + p0
            o1 = p1 if o1 is None else o1 + p1
        o0 = jnp.where(lane < 64, 0.0, o0)
        lse_scr[g] = top + jnp.log(mass)
        o = jnp.concatenate([o0, o1], axis=1)
        o_scr[g] = o
        pack_ref[:, 3 * FF + 3 * D + 256 * g : 3 * FF + 3 * D + 256 * g + 256] = o.astype(BF)
        middle = middle + mm(o.astype(BF), w_out[192 * g : 192 * g + 256, :])
    r2 = lax.rsqrt(jnp.mean(middle * middle, axis=1, keepdims=True) + EPSILON)
    n2 = middle * r2
    n2b = (n2 * gains[1:2, :]).astype(BF)
    pack_ref[:, 3 * FF : 3 * FF + D] = n2b
    n2p = mm(n2b, spread, NT).astype(BF)
    fetches[5].wait()
    for f in range(4):
        at, up_at = slice(512 * f, 512 * f + 512), slice(FF + 512 * f, FF + 512 * f + 512)
        gate = mm(n2p, w_gu[:, at])
        up = mm(n2p, w_gu[:, up_at])
        gu_scr[:, at] = gate
        gu_scr[:, up_at] = up
        hid = (gate / (1.0 + jnp.exp(-gate)) * up).astype(BF)
        pack_ref[:, 2 * FF + 512 * f : 2 * FF + 512 * f + 512] = hid
    fetches[6].wait()
    total = middle + mm(pack_ref[:, 2 * FF : 3 * FF], w_down[...])
    out_ref[...] = total.astype(BF)
    row = lax.broadcasted_iota(jnp.int32, (128, D), 0)
    mine = meta[0] * 4096 + meta[1] * 1024 + meta[2] * 512 + meta[3] * 128
    diff = jnp.where(row < meta[8] - mine, total - teach_ref[...].astype(F32), 0.0)
    square = diff * diff
    square = sum(square[:, 128 * n : 128 * n + 128] for n in range(6))
    square = jnp.sum(square, axis=0, keepdims=True)
    sq_ref[...] = jnp.broadcast_to(square + pltpu.roll(square, 64, 1), (8, 128))
    g = diff * (16384.0 / jnp.full((1, D), meta[8], jnp.int32).astype(F32))
    gb = g.astype(BF)
    pack_ref[:, 3 * FF + D : 3 * FF + 2 * D] = gb
    give(pack_ref.at[:, 2 * FF : 3 * FF + 2 * D], pack_out.at[:, 2 * FF : 3 * FF + 2 * D])
    give(pack_ref.at[:, 3 * FF + 3 * D : PACKED], pack_out.at[:, 3 * FF + 3 * D : PACKED])
    u = jnp.zeros((128, 1024), F32)
    for f in range(4):
        at, up_at = slice(512 * f, 512 * f + 512), slice(FF + 512 * f, FF + 512 * f + 512)
        gate, up = gu_scr[:, at], gu_scr[:, up_at]
        dh = mm(gb, w_down[at, :], NT)
        sig = 1.0 / (1.0 + jnp.exp(-gate))
        dgate = (dh * up * sig * (1.0 + gate * (1.0 - sig))).astype(BF)
        dup = (dh * gate * sig).astype(BF)
        pack_ref[:, at] = dgate
        pack_ref[:, up_at] = dup
        u = u + mm(dgate, w_gu[:, at], NT) + mm(dup, w_gu[:, up_at], NT)
    give(pack_ref.at[:, 0 : 2 * FF], pack_out.at[:, 0 : 2 * FF])
    u_hi, u_rest = split_two(u)
    u_mid, u_low = split_two(u_rest)
    u = mm(u_hi.astype(BF), spread) + (mm(u_mid.astype(BF), spread) + mm(u_low.astype(BF), spread))
    u = u * gains[1:2, :]
    gm = g + r2 * (u - n2 * jnp.mean(u * n2, axis=1, keepdims=True))
    gm_ref[...] = gm
    gmb = gm.astype(BF)
    pack_ref[:, 3 * FF + 2 * D : 3 * FF + 3 * D] = gmb
    give(pack_ref.at[:, 3 * FF + 2 * D : 3 * FF + 3 * D], pack_out.at[:, 3 * FF + 2 * D : 3 * FF + 3 * D])
    for k in range(4):
        dm = mm(gmb, w_out[192 * k : 192 * k + 256, :], NT).astype(BF)
        d0, d1 = dm[:, 0:128].astype(F32), dm[:, 128:256].astype(F32)
        p0, p1 = d0 * o_scr[k, :, 0:128], d1 * o_scr[k, :, 128:256]
        deltas = [
            jnp.sum(p0, axis=1, keepdims=True),
            jnp.sum(jnp.where(lane < 64, p1, 0.0), axis=1, keepdims=True),
            jnp.sum(jnp.where(lane < 64, 0.0, p1), axis=1, keepdims=True),
        ]
        hi, lo = split_two(-lse_scr[k])
        delta = jnp.where(lane == 0, deltas[0], jnp.where(lane == 1, deltas[1], deltas[2]))
        dhi, dlo = split_two(-delta)
        aug = jnp.where(lane < 3, hi, jnp.where(lane < 6, pltpu.roll(lo, 3, 1), 0.0))
        aug = jnp.where((lane >= 6) & (lane < 9), pltpu.roll(dhi, 6, 1), aug)
        aug = jnp.where((lane >= 9) & (lane < 12), pltpu.roll(dlo, 9, 1), aug)
        d0 = jnp.where(lane < 64, aug, d0).astype(BF)
        for y in range(4):
            pay_out[4 * k + y, :, 0:128] = d0
            pay_out[4 * k + y, :, 128:256] = dm[:, 128:256]
        give(pay_out.at[pl.ds(4 * k, 4)], pay_far.at[pl.ds(4 * k, 4)])
    for copy in sent:
        copy.wait()


def middle_part(meta, pay, tokens, teacher, gains, w_out, w_gu, w_down):
    return pl.pallas_call(
        middle_kernel,
        out_shape=(
            sds((128, D)), sds((8, 128), F32), sds((128, PACKED)), sds((128, D), F32), sds((16, 128, 256)),
        ),
        in_specs=[SM, AN] + [VM] * 3 + [AN] * 3,
        out_specs=(VM, VM, AN, VM, AN),
        scratch_shapes=[
            pltpu.VMEM((128, 2 * FF), F32),
            pltpu.VMEM((4, 128, 256), F32),
            pltpu.VMEM((4, 128, 128), F32),
            pltpu.VMEM((1024, 2 * FF), BF),
            pltpu.VMEM((16, 128, 256), BF),
            pltpu.VMEM((832, D), BF),
            pltpu.VMEM((FF, D), BF),
            pltpu.VMEM((128, PACKED), BF),
            pltpu.VMEM((16, 128, 256), BF),
            pltpu.SemaphoreType.DMA((15,)),
        ],
        compiler_params=pltpu.CompilerParams(vmem_limit_bytes=58 * 2**20),
        cost_estimate=pl.CostEstimate(flops=3 * 10**9, bytes_accessed=16 * 2**20, transcendentals=10**6),
        name="middle_part",
    )(meta, pay, tokens, teacher, gains, w_out, w_gu, w_down)


def finish_kernel(meta, g_ref, wq, wk, wv, gain, q_out, k_out, v_out, ga_out, loss_out):
    total, tail = None, None
    for x in range(4):
        part = g_ref[16 * x].astype(F32)
        for n in range(1, 16):
            part = part + g_ref[16 * x + n].astype(F32)
        lane = lax.broadcasted_iota(jnp.int32, (8, 128), 1)
        none = jnp.zeros((8, 512), F32)
        kv1 = part[:, 128:256]
        keys = [part[:, 0:128], jnp.where(lane < 64, kv1, 0.0)]
        values = [jnp.where(lane < 64, 0.0, kv1), part[:, 256:384]]
        last = part[:, 512:640]
        queries = [part[:, 384:512], jnp.where(lane < 64, last, 0.0)]
        wide = [jnp.concatenate(t + [none], axis=1) for t in (keys, values, queries)]
        shifts = (192 * x, (192 * x - 64) % D, 192 * x)
        wide = [pltpu.roll(a, s, 1) if s else a for a, s in zip(wide, shifts)]
        total = wide if total is None else [a + b for a, b in zip(total, wide)]
        tail = last if tail is None else tail + last
    keys, values, queries = total
    q_out[...], k_out[...], v_out[...] = queries[0:6], keys[0:6], values[0:6]
    by_row = keys[0:6] * wk[...].astype(F32) + values[0:6] * wv[...].astype(F32)
    by_row = by_row + queries[0:6] * wq[...].astype(F32)
    rows = jnp.sum(by_row, axis=1, keepdims=True)
    row = lax.broadcasted_iota(jnp.int32, (6, 128), 0)
    lane = lax.broadcasted_iota(jnp.int32, (6, 128), 1)
    across = jnp.sum(jnp.where(row == lane, rows, 0.0), axis=0, keepdims=True)
    ga_out[...] = across[:, 0:6] / gain[...].astype(F32)
    counted = jnp.full((1, 128), meta[8], jnp.int32).astype(F32)
    high = lax.broadcasted_iota(jnp.int32, (1, 128), 1) >= 64
    loss = jnp.sum(jnp.where(high, tail[0:1, :], 0.0), axis=1, keepdims=True)
    loss_out[...] = jnp.broadcast_to(loss / (counted * D), (1, 128))


def finish(meta, g, wq, wk, wv, gain):
    return pl.pallas_call(
        finish_kernel,
        out_shape=(sds((6, D), F32),) * 3 + (sds((1, 6), F32), sds((1, 128), F32)),
        in_specs=[SM] + [VM] * 5,
        out_specs=(VM,) * 5,
        cost_estimate=pl.CostEstimate(flops=10**6, bytes_accessed=10**6, transcendentals=0),
        name="finish",
    )(meta, g, wq, wk, wv, gain.reshape(1, 6))


def from_behind(x, axis, j):
    return lax.ppermute(x, axis, [(s, (s + j) % 4) for s in range(4)])


def from_ahead(x, axis, j):
    return lax.ppermute(x, axis, [(s, (s - j) % 4) for s in range(4)])


def from_core(x):
    return lax.ppermute(x, C, [(0, 1), (1, 0)])


def gather4(x, axis):
    return [x] + [from_behind(x, axis, j) for j in (1, 2, 3)]


def in_order(blocks, index, dim):
    r0, r1, r2, r3 = blocks
    twice = jnp.concatenate([r3, r2, r1, r0, r3, r2, r1], axis=dim)
    size = r0.shape[dim]
    return lax.dynamic_slice_in_dim(twice, (3 - index) * size, 4 * size, dim)


def block_of(x, index):
    return lax.dynamic_index_in_dim(x, index, 0, keepdims=False)


def scatter4(x, axis, index):
    own = block_of(x, index).astype(F32)
    far = [from_ahead(block_of(x, (index - j) & 3), axis, j).astype(F32) for j in (1, 2, 3)]
    return (own + far[1]) + (far[0] + far[2])


def summed(parts):
    a, b, c, d = (p.astype(F32) for p in parts)
    return (a + c) + (b + d)


def per_device(
    tokens, attn_gain, w_query, w_key, w_value, w_out, mlp_gain, w_gate, w_up, w_down, segments, teacher
):
    ix, iz, ic, iy = (lax.axis_index(a) for a in (X, Z, C, Y))
    begin = iz * 1024 + ic * 512

    heads, pack = prepare(
        w_query, w_key, w_value, attn_gain, mlp_gain, w_gate, w_up, w_out, w_down
    )
    pack = lax.all_gather(pack, BLK_HD)
    w_rows = lax.all_to_all(heads, (X, Z, Y), split_axis=0, concat_axis=0, tiled=True)
    w_rows = w_rows.reshape(512, WIDE)
    t_rows = gather4(tokens, X)

    place = jnp.where(
        jnp.arange(4) == 0, ix, jnp.where(jnp.arange(4) == 1, iz, jnp.where(jnp.arange(4) == 2, ic, iy))
    ).astype(jnp.int32)
    meta, lab = documents(place, segments.reshape(128, 128))

    exponents = jnp.arange(32, dtype=jnp.float32) * (-2.0 / HEAD_SIZE)
    frequency = jnp.tile(ROPE_BASE**exponents, 4)
    runs = ((ix - jnp.arange(4, dtype=jnp.int32)) & 3) * 4096
    places = runs[:, None] + begin + iy * 128 + jnp.arange(128, dtype=jnp.int32)[None]
    angles = places.astype(F32)[:, :, None] * frequency[None, None, :]
    cosine = jnp.cos(angles)
    sine = jnp.sin(angles) * jnp.where(jnp.arange(128) % 64 < 32, -1.0, 1.0)

    w_rows, t_rows, cosine, sine, meta, lab = lax.optimization_barrier(
        (w_rows, t_rows, cosine, sine, meta, lab)
    )
    w_rows = [w_rows, from_core(w_rows)]
    q, kv, w_full, n_rows, gain_rows = project(meta, w_rows, t_rows, cosine, sine)
    q_all, kv_own = gather4(q, Y), gather4(kv, Z)
    q_all, kv_own = lax.optimization_barrier((q_all, kv_own))
    kv_oth = [from_core(kv) for kv in kv_own]

    pay = attend(meta, lab, q_all, kv_own, kv_oth).reshape(16, 128, 256)
    pay = lax.all_to_all(pay, (X, Y), split_axis=0, concat_axis=0, tiled=True)
    w_out_all = jnp.pad(pack[:, :6, 4096:4864].reshape(D, D), ((64, 0), (0, 0)))
    w_down_all = pack[:, :, 4864:].reshape(128, 8, 2, D).transpose(0, 2, 1, 3).reshape(FF, D)
    out, squares, packed, grad_middle, dpay = middle_part(
        meta, pay, tokens, teacher, gain_rows, w_out_all, pack.reshape(1024, -1), w_down_all
    )
    dout = lax.all_to_all(dpay, (X, Y), split_axis=0, concat_axis=0, tiled=True)

    part_a, part_b = weights_back(meta, packed, from_core(packed))
    dout, _, _ = lax.optimization_barrier((dout, part_a, part_b))
    part_a = lax.psum_scatter(part_a.reshape(-1, 128), X, scatter_dimension=0, tiled=True)
    part_a = lax.psum_scatter(part_a, Z, scatter_dimension=0, tiled=True)
    far_b = [from_ahead(part_b[j], Z, j) for j in (1, 2, 3)]

    dq, dkv_own, dkv_oth = attend_back(
        meta, lab, q_all, kv_own, kv_oth, dout.reshape(4, 4, 128, 256)
    )
    dq, dkv_own, dkv_oth, far_b = lax.optimization_barrier((dq, dkv_own, dkv_oth, far_b))
    dq = [dq[0]] + [from_ahead(dq[j], Y, j) for j in (1, 2, 3)]
    dkv_oth = from_core(dkv_oth)
    dkv = [(dkv_own[j].astype(F32) + dkv_oth[j].astype(F32)).astype(BF) for j in range(4)]
    dkv, far_b = lax.optimization_barrier((dkv, far_b))
    dkv = [dkv[0]] + [from_ahead(dkv[j], Z, j) for j in (1, 2, 3)]
    part_b = summed([part_b[0]] + far_b).astype(BF)
    far_b = [from_ahead(part_b[j], X, j) for j in (1, 2, 3)]
    dq, dkv, far_b, part_a = lax.optimization_barrier((dq, dkv, far_b, part_a))
    part_b = summed([part_b[0]] + far_b).astype(BF)
    u, keep, send = project_back(meta, w_full, n_rows, cosine, sine, squares, dq, dkv)

    gu = jnp.concatenate([part_a[:384], part_b[:384]]).reshape(32, 4, 6, 128)
    gu = gu.transpose(1, 0, 2, 3).reshape(4, 192, 128)
    down = part_b[384:].reshape(6, 4, 16, 128)
    down = down.transpose(1, 0, 2, 3).reshape(4, 96, 128)
    outer = part_a[384:].reshape(6, 4, 6, 128).transpose(1, 0, 2, 3).reshape(4, 36, 128)
    grads = jnp.concatenate([gu, down, outer], axis=1)
    own_grads = block_of(grads, iy)
    far_grads = [from_ahead(block_of(grads, (iy - j) & 3), Y, j) for j in (1, 2, 3)]
    far_u = [from_ahead(u[j], X, j) for j in (1, 2, 3)]
    g = (keep.astype(F32) + from_core(send).astype(F32)).astype(BF).reshape(64, 8, WIDE)
    g = lax.all_to_all(g, (X, Z, Y), split_axis=0, concat_axis=0, tiled=True)
    g, far_grads, far_u = lax.optimization_barrier((g, far_grads, far_u))
    grads = summed([own_grads] + far_grads)

    u = summed([u[0]] + far_u) * gain_rows[0:1]
    wide = tokens.astype(F32)
    r1 = lax.rsqrt(jnp.mean(wide * wide, axis=1, keepdims=True) + EPSILON)
    n1 = wide * r1
    grad_tokens = grad_middle + r1 * (u - n1 * jnp.mean(u * n1, axis=1, keepdims=True))

    grad_query, grad_key, grad_value, grad_attn_gain, mean_loss = finish(
        meta, g, w_query, w_key, w_value, attn_gain
    )
    mean_loss, grad_attn_gain = mean_loss[0, 0], grad_attn_gain.reshape(6)

    gu = grads[:192].reshape(32, 6, 128).transpose(1, 0, 2).reshape(6, 2 * FF)
    down = grads[192:288].reshape(6, 16, 128).transpose(1, 0, 2).reshape(16, D)
    outer = grads[288:].reshape(6, 6, 128).transpose(1, 0, 2).reshape(6, D)
    grad_gate, grad_up = gu[:, :FF], gu[:, FF:]
    by_row = grad_gate * w_gate.astype(F32) + grad_up * w_up.astype(F32)
    grad_mlp_gain = jnp.sum(by_row, axis=1) / mlp_gain.astype(F32)
    return (
        out,
        grad_tokens.astype(BF),
        mean_loss,
        grad_attn_gain,
        grad_query,
        grad_key,
        grad_value,
        outer,
        grad_mlp_gain,
        grad_gate,
        grad_up,
        down,
    )


def solution(mesh):
    torus = Mesh(mesh.devices.reshape(4, 4, 2, mesh.shape["hd"]), BLK_HD)
    rows, vector = P(BLK_HD, None), P(BLK_HD)
    return jax.shard_map(
        per_device,
        mesh=torus,
        in_specs=(rows, vector, rows, rows, rows, rows, vector, rows, rows, rows, P(), rows),
        out_specs=(rows, rows, P(), vector, rows, rows, rows, rows, vector, rows, rows, rows),
        check_vma=False,
    )
```

```python
import jax
import jax.numpy as jnp
from jax import lax
from jax.experimental import pallas as pl
from jax.experimental.pallas import tpu as pltpu
from jax.sharding import Mesh
from jax.sharding import PartitionSpec as P

HEADS = 12
HEAD_SIZE = 64
D = 768
FF = 2048
EPSILON = 1e-05
ROPE_BASE = 10000.0
X, Z, C, Y = "blk_0", "blk_1", "blk_2", "hd"
BLK = (X, Z, C)
BLK_HD = (X, Z, C, Y)
WIDE = 640

BF = jnp.bfloat16
F32 = jnp.float32
NEG = -1e30
LABEL_LANE = 72
LABELS = 25
NT = (((1,), (1,)), ((), ()))
TN = (((0,), (0,)), ((), ()))
NN = (((1,), (0,)), ((), ()))
LIMIT = 70.0


def mm(a, b, dims=NN):
    return lax.dot_general(a, b, dims, preferred_element_type=F32)


def lanes(rows):
    return lax.broadcasted_iota(jnp.int32, (rows, 128), 1)


def rows_of(rows):
    return lax.broadcasted_iota(jnp.int32, (rows, 128), 0)


def lane_masks():
    lane = lanes(128)
    low = (lane < 64).astype(F32)
    head = rows_of(128) // 64
    first = (head == lane).astype(F32).astype(BF)
    second = ((head == 0) & (lane == 2)).astype(F32).astype(BF)
    return low.astype(BF), (1.0 - low).astype(BF), first, second


def one_lane(n):
    return (lanes(128) == n).astype(F32).astype(BF)


def stage_keys(meta, lab, own, oth, kaug, other):
    ix, iz, ic, iy = (meta[k] for k in range(4))
    lane = lanes(128)
    row = rows_of(128)
    first, last = lab[0:1, :], lab[1:2, :]
    one = ((lane >= 64) & (lane < 67)).astype(F32)
    low, _, _, _ = lane_masks()

    def place(i, _):
        for j in range(4):
            ki = ((ix - i) & 3) * 4 + ((iz - j) & 3)
            for ref, core in ((own[j], ic), (oth[j], 1 - ic)):
                at = pl.multiple_of(ki * 256 + core * 128, 128)
                k0, k1, v1 = (ref[i, :, 128 * n : 128 * n + 128] for n in range(3))
                place_at = ki * 1024 + core * 512 + iy * 128 + row
                outside = (place_at < first) | (place_at >= last)
                half = k1 * low
                kaug[pl.ds(at, 128), 0:128] = k0
                kaug[pl.ds(at, 128), 128:256] = half + jnp.where(outside, NEG, one).astype(BF)
                other(at, k0, half, k1, v1)
        return 0

    lax.fori_loop(0, 4, place, 0)


def split_two(x):
    hi = x.astype(BF).astype(F32)
    return hi, x - hi


def split_three(x):
    hi, rest = split_two(x)
    return (hi, *split_two(rest))


def fwd_kernel(meta, lab, *refs):
    out_ref, kaug, vbd, qm, acc, q_in, kv_in, sems = refs[12:]
    fetches = [
        pltpu.make_async_copy(ref, q_in.at[n] if n < 4 else kv_in.at[n - 4], sems.at[n])
        for n, ref in enumerate(refs[0:12])
    ]
    for fetch in fetches[4:] + fetches[:4]:
        fetch.start()
    q_refs = [q_in.at[n] for n in range(4)]
    kv_own, kv_oth = ([kv_in.at[n + at] for n in range(4)] for at in (0, 4))
    for fetch in fetches[4:]:
        fetch.wait()
    ix, iz, ic, iy = (meta[k] for k in range(4))
    lane = lanes(128)
    first, last = lab[0:1, :], lab[1:2, :]
    is_label = (lane >= LABEL_LANE) & (lane < LABEL_LANE + LABELS)
    zeros = jnp.zeros((128, 128), BF)
    low, high, by_head0, by_head1 = lane_masks()
    ones = [one_lane(h) for h in range(3)]

    def value_rows(at, k0, half, k1, v1):
        t = at // 256
        inner = pl.multiple_of(at % 256, 128)
        rows = [pl.ds(256 * h + inner, 128) for h in range(3)]
        vbd[t, rows[0], 0:128] = k1 * high + ones[0]
        vbd[t, rows[0], 128:256] = zeros
        vbd[t, rows[1], 0:128] = ones[1]
        vbd[t, rows[1], 128:256] = v1 * low
        vbd[t, rows[2], 0:128] = ones[2]
        vbd[t, rows[2], 128:256] = v1 * high

    stage_keys(meta, lab, kv_own, kv_oth, kaug, value_rows)
    for fetch in fetches[:4]:
        fetch.wait()
    key_norms = query_norms = jnp.zeros((1, 128), F32)
    for n in range(4):
        for ref, at in ((kaug, pl.ds(1024 * n, 1024)), (q_refs[n], slice(None))):
            whole = ref[at].reshape(-1, 256)
            v0, v1 = whole[:, 0:128], whole[:, 128:256] * low[0:1, :]
            norms = mm(v0 * v0, by_head0) + mm(v1 * v1, by_head1)
            norms = jnp.max(norms, axis=0, keepdims=True)
            if ref is kaug:
                key_norms = jnp.maximum(key_norms, norms)
            else:
                query_norms = jnp.maximum(query_norms, norms)
    bound = key_norms * query_norms
    small = jnp.max(bound) < LIMIT * LIMIT

    def one_run(xr, _):
        i = (ix - xr) & 3
        begin = xr * 4096 + iz * 1024 + ic * 512
        for j in range(4):
            yq = (iy - j) & 3
            q0, q1 = q_refs[j][i, :, 0:128], q_refs[j][i, :, 128:256]
            place = begin + yq * 128 + rows_of(128)
            mine = is_label & (place >= first) & (place < last)
            label = jnp.where(mine, 1.0, 0.0).astype(BF)
            at = [pl.ds(pl.multiple_of(512 * h + yq * 128, 128), 128) for h in range(3)]
            qm[at[0], 0:128] = q0 * low
            qm[at[0], 128:256] = label
            qm[at[1], 0:128] = q0 * high
            qm[at[1], 128:256] = label
            qm[at[2], 0:128] = zeros
            qm[at[2], 128:256] = q1 * low + label
        start = meta[4 + xr]
        end = xr * 4 + iz

        def allowed_keys(t):
            key_row = lax.broadcasted_iota(jnp.int32, (256, 512), 0)
            key_place = t * 1024 + iy * 128 + key_row + jnp.where(key_row >= 128, 512 - 128, 0)
            return key_place <= begin + lax.broadcasted_iota(jnp.int32, (256, 512), 1)

        acc[...] = jnp.zeros((512, 256), F32)

        def fast(tiles, diagonal):
            probs = []
            for t in tiles:
                s = mm(qm[...], kaug[pl.ds(pl.multiple_of(t * 256, 256), 256), :], NT)
                if diagonal:
                    key_lane = lax.broadcasted_iota(jnp.int32, (512, 256), 1)
                    key_place = t * 1024 + iy * 128 + key_lane + jnp.where(key_lane >= 128, 512 - 128, 0)
                    allowed = key_place <= begin + lax.broadcasted_iota(jnp.int32, (512, 256), 0)
                for h in range(3):
                    part = s[512 * h : 512 * h + 512]
                    if diagonal:
                        part = jnp.where(allowed, part, NEG)
                    probs.append(jnp.exp(part).astype(BF))
            probs = jnp.concatenate(probs, axis=1)
            values = vbd[pl.ds(tiles[0], len(tiles))].reshape(768 * len(tiles), 256)
            acc[...] += mm(probs, values)

        def finish(highest):
            a0, a1 = acc[:, 0:128], acc[:, 128:256]
            lane5 = lanes(512)
            some = a0 > 0.0
            mass = jnp.where(some, a0, 1.0)
            inverse = jnp.where(some, 1.0 / mass, 0.0)
            log_mass = jnp.where(some, jnp.log(mass) + highest, NEG)
            hi, mid, lo = split_three(log_mass)
            extra = jnp.where(lane5 < 6, pltpu.roll(mid, 3, 1), pltpu.roll(lo, 6, 1))
            extra = jnp.where(lane5 < 3, hi, extra)
            scaled = [inverse[:, h : h + 1] for h in range(3)]
            o0 = jnp.where(lane5 >= 64, a0 * scaled[0], jnp.where(lane5 < 9, extra, 0.0)).astype(BF)
            o1 = (a1 * jnp.where(lane5 < 64, scaled[1], scaled[2])).astype(BF)
            for yq in range(4):
                at = slice(yq * 128, yq * 128 + 128)
                out_ref[xr, yq, :, 0:128] = o0[at]
                out_ref[xr, yq, :, 128:256] = o1[at]

        @pl.when(small)
        def _():
            def step(t, _):
                fast((start + 2 * t, start + 2 * t + 1), False)
                return 0

            lax.fori_loop(0, (end - start) // 2, step, 0)

            @pl.when(((end - start) & 1) == 1)
            def _():
                fast((end - 1,), False)

            fast((end,), True)
            finish(0.0)

        @pl.when(jnp.logical_not(small))
        def _():
            lane5 = lanes(512)

            def step(t, highs):
                at = pl.ds(pl.multiple_of(t * 256, 256), 256)
                keys = kaug[at, :]
                allowed = allowed_keys(t)
                a0, a1 = acc[:, 0:128], acc[:, 128:256]
                total, fresh, scales = None, [], []
                for h in range(3):
                    s = jnp.where(allowed, mm(keys, qm[512 * h : 512 * h + 512, :], NT), NEG)
                    top = jnp.maximum(highs[h], jnp.max(s, axis=0, keepdims=True))
                    scales.append(jnp.exp(highs[h] - top))
                    p = jnp.where(s < 0.5 * NEG, 0.0, jnp.exp(s - top)).astype(BF)
                    part = mm(p, vbd[t, 256 * h : 256 * h + 256, :], TN)
                    total = part if total is None else total + part
                    fresh.append(top)
                rows = jnp.concatenate(scales + [jnp.zeros((125, 512), F32)], axis=0)
                columns = rows.T
                scales = [columns[:, h : h + 1] for h in range(3)]
                factor0 = jnp.where((lane5 >= 64) | (lane5 == 0), scales[0], 1.0)
                factor0 = jnp.where(lane5 == 1, scales[1], jnp.where(lane5 == 2, scales[2], factor0))
                factor1 = jnp.where(lane5 < 64, scales[1], scales[2])
                acc[:, 0:128] = a0 * factor0 + total[:, 0:128]
                acc[:, 128:256] = a1 * factor1 + total[:, 128:256]
                return tuple(fresh)

            lowest = tuple(jnp.full((1, 512), NEG, F32) for _ in range(3))
            highs = lax.fori_loop(start, end + 1, step, lowest)
            rows = jnp.concatenate(list(highs) + [jnp.zeros((125, 512), F32)], axis=0)
            finish(rows.T)

        return 0

    lax.fori_loop(0, 4, one_run, 0)


def bwd_kernel(meta, lab, *refs):
    q_refs, kv_own, kv_oth, do_ref = refs[0:4], refs[4:8], refs[8:12], refs[12]
    dq_refs, dkv_own, dkv_oth = refs[13:17], refs[17], refs[18]
    kaug, vaug, kt, qa, da, dq_acc, dk_acc, dv_acc, dq_rows = refs[19:]
    ix, iz, ic, iy = (meta[k] for k in range(4))
    lane = lanes(128)
    first, last = lab[0:1, :], lab[1:2, :]
    is_label = (lane >= LABEL_LANE) & (lane < LABEL_LANE + LABELS)
    zeros = jnp.zeros((128, 128), BF)

    low, high, _, _ = lane_masks()
    two = ((lane < 2).astype(F32)).astype(BF)
    row = rows_of(128)

    def pick(pairs):
        chosen = [(row == a) & (lane == b) for a, b in pairs]
        return sum(jnp.where(c, 1.0, 0.0) for c in chosen).astype(BF)

    shift_pick = [pick(((h, 64), (h + 3, 65), (h + 12, 66))) for h in range(3)]
    delta_pick = [pick(((h + 6, 0), (h + 9, 1))) for h in range(3)]

    def value_rows(at, k0, half, k1, v1):
        vaug[pl.ds(at, 128), 0:128] = k1 * high + two
        vaug[pl.ds(at, 128), 128:256] = v1

    stage_keys(meta, lab, kv_own, kv_oth, kaug, value_rows)

    def turn(t, _):
        at = pl.ds(pl.multiple_of(t * 256, 256), 256)
        kt[t] = kaug[at, :].T
        return 0

    lax.fori_loop(0, 16, turn, 0)
    dk_acc[...] = jnp.zeros_like(dk_acc)
    dv_acc[...] = jnp.zeros_like(dv_acc)

    def one_run(xr, _):
        i = (ix - xr) & 3
        begin = xr * 4096 + iz * 1024 + ic * 512
        for j in range(4):
            yq = (iy - j) & 3
            q0, q1 = q_refs[j][i, :, 0:128], q_refs[j][i, :, 128:256]
            d0, d1 = do_ref[xr, yq, :, 0:128], do_ref[xr, yq, :, 128:256]
            place = begin + yq * 128 + rows_of(128)
            mine = is_label & (place >= first) & (place < last)
            label = jnp.where(mine, 1.0, 0.0)
            for h in range(3):
                at = pl.ds(pl.multiple_of(512 * h + yq * 128, 128), 128)
                aug = (mm(d0, shift_pick[h]) + label).astype(BF)
                qa[at, 0:128] = q0 * (low, high, low * high)[h]
                qa[at, 128:256] = (q1 * low + aug) if h == 2 else aug
                aug = mm(d0, delta_pick[h]).astype(BF)
                da[at, 0:128] = (d0 * high + aug) if h == 0 else aug
                da[at, 128:256] = d1 * (low * high, low, high)[h]
        start = meta[4 + xr]
        end = xr * 4 + iz
        dq_acc[...] = jnp.zeros_like(dq_acc)

        def tile(t, diagonal):
            at = pl.ds(pl.multiple_of(t * 256, 256), 256)
            keys, values = kaug[at, :], vaug[at, :]
            if diagonal:
                key_row = lax.broadcasted_iota(jnp.int32, (256, 512), 0)
                key_place = t * 1024 + iy * 128 + key_row + jnp.where(key_row >= 128, 512 - 128, 0)
                place = begin + lax.broadcasted_iota(jnp.int32, (256, 512), 1)
                allowed = key_place <= place
            s = mm(keys, qa[...], NT)
            dp = mm(values, da[...], NT)
            probs, grads = [], []
            for h in range(3):
                part = s[:, 512 * h : 512 * h + 512]
                if diagonal:
                    part = jnp.where(allowed, part, NEG)
                p = jnp.exp(part)
                ds = (p * dp[:, 512 * h : 512 * h + 512]).astype(BF)
                probs.append(p.astype(BF))
                grads.append(ds)
                dq_acc[h] += mm(kt[t, 64 * h : 64 * h + 64, :], ds)
            dv_acc[at, :] += mm(jnp.concatenate(probs, axis=1), da[...])
            dk_acc[at, :] += mm(jnp.concatenate(grads, axis=1), qa[...])

        def step(t, _):
            tile(start + 2 * t, False)
            tile(start + 2 * t + 1, False)
            return 0

        lax.fori_loop(0, (end - start) // 2, step, 0)

        @pl.when(((end - start) & 1) == 1)
        def _():
            tile(end - 1, False)

        tile(end, True)
        whole = jnp.concatenate([dq_acc[0], dq_acc[1], dq_acc[2], jnp.zeros((64, 512), F32)], axis=0)
        dq_rows[...] = whole.T.astype(BF)
        for j in range(4):
            yq = (iy - j) & 3
            dq_refs[j][i] = dq_rows[pl.ds(pl.multiple_of(yq * 128, 128), 128), :]
        return 0

    lax.fori_loop(0, 4, one_run, 0)

    def give(i, _):
        for j in range(4):
            ki = ((ix - i) & 3) * 4 + ((iz - j) & 3)
            for ref, core in ((dkv_own, ic), (dkv_oth, 1 - ic)):
                at = pl.ds(pl.multiple_of(ki * 256 + core * 128, 128), 128)
                middle = jnp.where(lane < 64, dk_acc[at, 128:256], dv_acc[at, 0:128])
                ref[j, i, :, 0:128] = dk_acc[at, 0:128].astype(BF)
                ref[j, i, :, 128:256] = middle.astype(BF)
                ref[j, i, :, 256:384] = dv_acc[at, 128:256].astype(BF)
        return 0

    lax.fori_loop(0, 4, give, 0)


def sds(shape, dtype=BF):
    return jax.ShapeDtypeStruct(shape, dtype)


VM = pl.BlockSpec(memory_space=pltpu.VMEM)
SM = pl.BlockSpec(memory_space=pltpu.SMEM)


def attend(meta, lab, q, kv_own, kv_oth):
    return pl.pallas_call(
        fwd_kernel,
        out_shape=sds((4, 4, 128, 256)),
        in_specs=[SM, VM] + [pl.BlockSpec(memory_space=pl.ANY)] * 12,
        out_specs=VM,
        scratch_shapes=[
            pltpu.VMEM((4096, 256), BF),
            pltpu.VMEM((16, 768, 256), BF),
            pltpu.VMEM((1536, 256), BF),
            pltpu.VMEM((512, 256), F32),
            pltpu.VMEM((4, 4, 128, 256), BF),
            pltpu.VMEM((8, 4, 128, 384), BF),
            pltpu.SemaphoreType.DMA((12,)),
        ],
        compiler_params=pltpu.CompilerParams(vmem_limit_bytes=58 * 2**20),
        cost_estimate=pl.CostEstimate(flops=20 * 10**9, bytes_accessed=8 * 2**20, transcendentals=10**7),
        name="attend",
    )(meta, lab, *q, *kv_own, *kv_oth)


def attend_back(meta, lab, q, kv_own, kv_oth, dout):
    outs = pl.pallas_call(
        bwd_kernel,
        out_shape=(sds((4, 128, 256)),) * 4 + (sds((4, 4, 128, 384)),) * 2,
        in_specs=[SM] + [VM] * 14,
        out_specs=(VM,) * 6,
        scratch_shapes=[
            pltpu.VMEM((4096, 256), BF),
            pltpu.VMEM((4096, 256), BF),
            pltpu.VMEM((16, 256, 256), BF),
            pltpu.VMEM((1536, 256), BF),
            pltpu.VMEM((1536, 256), BF),
            pltpu.VMEM((3, 64, 512), F32),
            pltpu.VMEM((4096, 256), F32),
            pltpu.VMEM((4096, 256), F32),
            pltpu.VMEM((512, 256), BF),
        ],
        compiler_params=pltpu.CompilerParams(vmem_limit_bytes=56 * 2**20),
        cost_estimate=pl.CostEstimate(flops=50 * 10**9, bytes_accessed=16 * 2**20, transcendentals=10**7),
        name="attend_back",
    )(meta, lab, *q, *kv_own, *kv_oth, dout)
    return outs[0:4], outs[4], outs[5]


def spread_rows():
    row = lax.broadcasted_iota(jnp.int32, (1024, D), 0)
    column = lax.broadcasted_iota(jnp.int32, (1024, D), 1)
    inner = row % 8
    return jnp.where((inner < 6) & (row // 8 * 6 + inner == column), 1.0, 0.0).astype(BF)


AN = pl.BlockSpec(memory_space=pl.ANY)


def fetch_all(sources, targets, sems):
    copies = [pltpu.make_async_copy(a, b, sems.at[n]) for n, (a, b) in enumerate(zip(sources, targets))]
    for copy in copies:
        copy.start()
    return targets, copies


def documents_kernel(place, seg_ref, meta, lab_ref):
    ix, iz, ic, iy = (place[k] for k in range(4))
    seg = seg_ref[...]
    lane = lax.broadcasted_iota(jnp.int32, (1, 128), 1)
    some = seg != 0
    counted = jnp.sum(some.astype(jnp.int32))
    starts, ends = jnp.zeros((1, 128), jnp.int32), jnp.full((1, 128), 16384, jnp.int32)
    begins = []
    for label in range(LABELS):
        start, end = counted, jnp.int32(16384)
        if label:
            start = jnp.sum((some & (seg < label)).astype(jnp.int32))
            end = jnp.sum((some & (seg <= label)).astype(jnp.int32))
        starts = jnp.where(lane == LABEL_LANE + label, start, starts)
        ends = jnp.where(lane == LABEL_LANE + label, end, ends)
        begins.append(start)
    row = lax.broadcasted_iota(jnp.int32, (8, 128), 0)
    lab_ref[...] = jnp.where(row == 0, starts, ends)
    for k in range(4):
        meta[k] = place[k]
    for xr in range(4):
        at = xr * 32 + iz * 8 + ic * 4
        mine = jnp.sum(jnp.where(lane == 0, seg_ref[pl.ds(at, 1), :], 0))
        first = jnp.int32(0)
        for label in range(LABELS):
            first = jnp.where(mine == label, begins[label], first)
        meta[4 + xr] = lax.shift_right_logical(first, 10)
    meta[8] = counted


def documents(place, segments):
    return pl.pallas_call(
        documents_kernel,
        out_shape=(sds((9,), jnp.int32), sds((8, 128), jnp.int32)),
        in_specs=[SM, VM],
        out_specs=(SM, VM),
        cost_estimate=pl.CostEstimate(flops=10**6, bytes_accessed=10**5, transcendentals=0),
        name="documents",
    )(place, segments)


def prepare_kernel(wq, wk, wv, ga, gm, wg, wu, wo, wd, heads_ref, pack_ref):
    row = lax.broadcasted_iota(jnp.int32, (8, 128), 0)
    lane = lax.broadcasted_iota(jnp.int32, (8, 128), 1)

    def eight(ref, width):
        empty = jnp.zeros((2, width), F32)
        return jnp.concatenate([ref[...].astype(F32), empty], axis=0)

    def column(ref):
        across = jnp.broadcast_to(jnp.pad(ref[...].astype(F32), ((0, 0), (0, 122))), (8, 128))
        return jnp.sum(jnp.where(lane == row, across, 0.0), axis=1, keepdims=True)

    wide = [eight(ref, D) for ref in (wk, wv, wq)]
    gains = jnp.where(lane == 64, column(ga), jnp.where(lane == 65, column(gm), 0.0))
    for g in range(4):
        k, v, q = (pltpu.roll(w, (D - 192 * g) % D, 1)[:, 0:256] if g else w[:, 0:256] for w in wide)
        low = lane < 64
        v = pltpu.roll(v, 64, 1)
        tiles = [
            k[:, 0:128],
            jnp.where(low, k[:, 128:256], v[:, 0:128]),
            v[:, 128:256],
            q[:, 0:128],
            jnp.where(low, q[:, 128:256], gains),
        ]
        block = jnp.concatenate(tiles, axis=1).astype(BF)
        for n in range(16):
            heads_ref[16 * g + n] = block
    pack_ref[:, 0:FF] = eight(wg, FF).astype(BF)
    pack_ref[:, FF : 2 * FF] = eight(wu, FF).astype(BF)
    pack_ref[:, 2 * FF : 2 * FF + D] = eight(wo, D).astype(BF)
    pack_ref[:, 2 * FF + D : 2 * FF + 2 * D] = wd[0:8, :]
    pack_ref[:, 2 * FF + 2 * D : 2 * FF + 3 * D] = wd[8:16, :]


def prepare(wq, wk, wv, ga, gm, wg, wu, wo, wd):
    return pl.pallas_call(
        prepare_kernel,
        out_shape=(sds((64, 8, WIDE)), sds((8, 2 * FF + 3 * D))),
        in_specs=[VM] * 9,
        out_specs=(VM, VM),
        cost_estimate=pl.CostEstimate(flops=10**6, bytes_accessed=2 * 10**6, transcendentals=0),
        name="prepare",
    )(wq, wk, wv, ga.reshape(1, 6), gm.reshape(1, 6), wg, wu, wo, wd)


def close_rows():
    row = lax.broadcasted_iota(jnp.int32, (D, 1024), 0)
    column = lax.broadcasted_iota(jnp.int32, (D, 1024), 1)
    inner = column % 8
    return jnp.where((inner < 6) & (column // 8 * 6 + inner == row), 1.0, 0.0).astype(BF)


def project_kernel(
    meta, w_own, w_oth, t0, t1, t2, t3, cos_ref, sin_ref, q_out, kv_out, w_far, n_far, gain_out,
    w_scr, w_in, t_in, q_ref, kv_ref, w_out, n_out, turn_in, sems,
):
    targets = [w_in.at[0], w_in.at[1]] + [t_in.at[n] for n in range(4)] + [turn_in.at[0], turn_in.at[1]]
    sources = (w_own, w_oth, t0, t1, t2, t3, cos_ref, sin_ref)
    (w_own, w_oth, *_, cos_ref, sin_ref), fetches = fetch_all(sources, targets, sems)
    for fetch in fetches[0:2]:
        fetch.wait()
    sent = []

    def give(source, target):
        sent.append(pltpu.make_async_copy(source, target, sems.at[8 + len(sent)]))
        sent[-1].start()

    for ref, core in ((w_own, meta[2]), (w_oth, 1 - meta[2])):
        for chip in range(16):
            at = pl.multiple_of(64 * chip + 32 * core, 32)
            w_scr[pl.ds(at, 32), :] = ref[32 * chip : 32 * chip + 32, :]
    w = mm(close_rows(), w_scr[...]).astype(BF)
    w_out[...] = w
    give(w_out, w_far)
    tail = w[:, 512:640]
    row, lane = lax.broadcasted_iota(jnp.int32, (8, 128), 0), lax.broadcasted_iota(jnp.int32, (8, 128), 1)
    pick = jnp.where(lane == row + 64, 1.0, 0.0).astype(BF)
    gains = mm(pick, tail, NT)
    gain_out[...] = gains
    for fetch in fetches[2:]:
        fetch.wait()
    for i in range(4):
        wide = t_in[i].astype(F32)
        r1 = lax.rsqrt(jnp.mean(wide * wide, axis=1, keepdims=True) + EPSILON)
        n = (wide * r1 * gains[0:1, :]).astype(BF)
        n_out[i] = n
        y = mm(n, w_out[...])
        turned = turn_heads(y, cos_ref[i], sin_ref[i], 0.125)
        kv_ref[i] = turned[:, 0:384].astype(BF)
        q_ref[i] = turned[:, 384:640].astype(BF)
        give(kv_ref.at[i], kv_out.at[i])
        give(q_ref.at[i], q_out.at[i])
    give(n_out, n_far)
    for copy in sent:
        copy.wait()


def turn_heads(y, cosine, sine, scale):
    lane = lax.broadcasted_iota(jnp.int32, y.shape, 1)
    other = jnp.where(lane % 64 < 32, pltpu.roll(y, WIDE - 32, 1), pltpu.roll(y, 32, 1))
    low = lanes(cosine.shape[0]) < 64
    cosines = [cosine, jnp.where(low, cosine, 1.0), jnp.ones_like(cosine), cosine * scale, cosine * scale]
    none = jnp.zeros_like(sine)
    sines = [sine, jnp.where(low, sine, 0.0), none, sine * scale, sine * scale]
    return y * jnp.concatenate(cosines, axis=1) + other * jnp.concatenate(sines, axis=1)


def project(meta, w, rows, cosine, sine):
    return pl.pallas_call(
        project_kernel,
        out_shape=(
            sds((4, 128, 256)), sds((4, 128, 384)), sds((D, WIDE)), sds((4, 128, D)), sds((8, D), F32),
        ),
        in_specs=[SM] + [AN] * 8,
        out_specs=(AN, AN, AN, AN, VM),
        scratch_shapes=[
            pltpu.VMEM((1024, WIDE), BF),
            pltpu.VMEM((2, 512, WIDE), BF),
            pltpu.VMEM((4, 128, D), BF),
            pltpu.VMEM((4, 128, 256), BF),
            pltpu.VMEM((4, 128, 384), BF),
            pltpu.VMEM((D, WIDE), BF),
            pltpu.VMEM((4, 128, D), BF),
            pltpu.VMEM((2, 4, 128, 128), F32),
            pltpu.SemaphoreType.DMA((18,)),
        ],
        compiler_params=pltpu.CompilerParams(vmem_limit_bytes=58 * 2**20),
        cost_estimate=pl.CostEstimate(flops=2 * 10**9, bytes_accessed=4 * 2**20, transcendentals=0),
        name="project",
    )(meta, *w, *rows, cosine, sine)


def project_back_kernel(
    meta, w_ref, n_ref, cos_ref, sin_ref, loss_ref, *refs
):
    outs, (d_scr, g_scr, a_in, b_in, u_scr, g_out, w_in, n_in, turn_in, sems) = refs[8:14], refs[14:]
    targets = [a_in.at[n] for n in range(4)] + [b_in.at[n] for n in range(4)]
    targets = targets + [turn_in.at[0], turn_in.at[1], w_in, n_in]
    sources = (*refs[0:8], cos_ref, sin_ref, w_ref, n_ref)
    landed, fetches = fetch_all(sources, targets, sems)
    cos_ref, sin_ref, w_ref, n_ref = landed[8:12]
    (a0, a1, a2, a3), (b0, b1, b2, b3) = landed[0:4], landed[4:8]
    for fetch in fetches:
        fetch.wait()
    sent = []

    def give(source, n):
        sent.append(pltpu.make_async_copy(source, outs[n], sems.at[12 + n]))
        sent[-1].start()

    keep = jnp.where(lax.broadcasted_iota(jnp.int32, (D, 128), 1) < 64, 1.0, 0.0)
    tail = (w_ref[:, 512:640].astype(F32) * keep).astype(BF)
    w = jnp.concatenate([w_ref[:, 0:512], tail], axis=1)
    for i in range(4):
        dkv = (b0[i].astype(F32) + b2[i].astype(F32)) + (b1[i].astype(F32) + b3[i].astype(F32))
        dq = (a0[i].astype(F32) + a2[i].astype(F32)) + (a1[i].astype(F32) + a3[i].astype(F32))
        dq1 = jnp.where(lanes(128) < 64, dq[:, 128:256], 0.0)
        y = jnp.concatenate([dkv, dq[:, 0:128], dq1], axis=1).astype(BF).astype(F32)
        d = turn_heads(y, cos_ref[i], -sin_ref[i], 0.125).astype(BF)
        d_scr[i * 128 : i * 128 + 128, :] = d
        u_scr[i] = mm(d, w, NT).astype(BF)
        give(u_scr.at[i], i)
    rows = n_ref[...].reshape(512, D)
    g = mm(rows, d_scr[...], TN)
    last = jnp.where(lanes(D) < 64, g[:, 512:640], loss_ref[0:1, :])
    g = jnp.concatenate([g[:, 0:512], last], axis=1).astype(BF)
    g_scr[...] = mm(spread_rows(), g).astype(BF)
    for n, core in enumerate((1 - meta[2], meta[2])):
        for chip in range(16):
            at = pl.multiple_of(64 * chip + 32 * core, 32)
            g_out[n, 32 * chip : 32 * chip + 32, :] = g_scr[pl.ds(at, 32), :]
        give(g_out.at[n], 5 - n)
    for copy in sent:
        copy.wait()


def project_back(meta, w, n, cosine, sine, loss_row, dq, dkv):
    outs = pl.pallas_call(
        project_back_kernel,
        out_shape=(sds((128, D)),) * 4 + (sds((512, WIDE)),) * 2,
        in_specs=[SM] + [AN] * 4 + [VM] + [AN] * 8,
        out_specs=(AN,) * 6,
        scratch_shapes=[
            pltpu.VMEM((512, WIDE), BF),
            pltpu.VMEM((1024, WIDE), BF),
            pltpu.VMEM((4, 4, 128, 256), BF),
            pltpu.VMEM((4, 4, 128, 384), BF),
            pltpu.VMEM((4, 128, D), BF),
            pltpu.VMEM((2, 512, WIDE), BF),
            pltpu.VMEM((D, WIDE), BF),
            pltpu.VMEM((4, 128, D), BF),
            pltpu.VMEM((2, 4, 128, 128), F32),
            pltpu.SemaphoreType.DMA((18,)),
        ],
        compiler_params=pltpu.CompilerParams(vmem_limit_bytes=58 * 2**20),
        cost_estimate=pl.CostEstimate(flops=2 * 10**9, bytes_accessed=6 * 2**20, transcendentals=0),
        name="project_back",
    )(meta, w, n, cosine, sine, loss_row, *dq, *dkv)
    return outs[0:4], outs[4], outs[5]


PACKED = 2 * FF + FF + 3 * D + 1024


A_ROWS, B_ROWS = 384 + 144, 384 + 384


def weights_back_kernel(meta, own, oth, *refs):
    ix, iz, ic = meta[0], meta[1], meta[2]
    a_refs, b_refs = [refs[0].at[k] for k in range(4)], refs[1:5]
    n_t, m_t, h_t, left, rows, held, sems = refs[5:]
    (own, oth), fetches = fetch_all((own, oth), [held.at[0], held.at[1]], sems)
    for fetch in fetches:
        fetch.wait()
    for k, ref in enumerate((own, oth)):
        at = slice(128 * k, 128 * k + 128)
        n_t[:, at] = ref[:, 3 * FF : 3 * FF + D].astype(F32).T
        h_t[:, at] = ref[:, 2 * FF : 3 * FF].T
        for g in range(4):
            first = 3 * FF + 3 * D + 256 * g
            m_t[192 * g : 192 * g + 192, at] = ref[:, first : first + 256].astype(F32).T[64:256, :]
        rows[at, :] = ref[:, 3 * FF + D : 3 * FF + 3 * D]

    def chips(x_outer):
        for m in range(16):
            yield m, m if x_outer else ((ix - m % 4) & 3) * 4 + ((iz - m // 4) & 3)

    def collect(source, x_outer):
        for m, chip in chips(x_outer):
            left[24 * m : 24 * m + 24, :] = source[pl.ds(pl.multiple_of(48 * chip + 24 * ic, 8), 24), :]
        return left[...].astype(BF)

    def collect_hidden(x_outer):
        picked = [
            h_t[pl.ds(pl.multiple_of(128 * chip + 64 * ic, 64), 64), :] for _, chip in chips(x_outer)
        ]
        return jnp.concatenate(picked, axis=0)

    def put(part, outs, at, height):
        for m in range(16):
            block = part[height * m : height * m + height]
            both = jnp.concatenate([block[:, 0:128], block[:, 128:256]], axis=0)
            outs[m // 4][m % 4, pl.ds(at, 2 * height), :] = both.astype(BF)

    def columns(first, k):
        at = pl.ds(pl.multiple_of(first + 256 * k, 256), 256)
        return jnp.concatenate([own[:, at], oth[:, at]], axis=0)

    for outs, first, x_outer in ((a_refs, 0, True), (b_refs, FF, False)):
        features = collect(n_t, x_outer)

        def gate_or_up(k, _):
            put(mm(features, columns(first, k)), outs, pl.multiple_of(48 * k, 48), 24)
            return 0

        lax.fori_loop(0, 8, gate_or_up, 0)
    outer, down = collect(m_t, True), collect_hidden(False)
    for k in range(3):
        put(mm(outer, rows[:, D + 256 * k : D + 256 * k + 256]), a_refs, 384 + 48 * k, 24)
        put(mm(down, rows[:, 256 * k : 256 * k + 256]), b_refs, 384 + 128 * k, 64)


def weights_back(meta, own, oth):
    outs = pl.pallas_call(
        weights_back_kernel,
        out_shape=(sds((4, 4, A_ROWS, 128)),) + (sds((4, B_ROWS, 128)),) * 4,
        in_specs=[SM, AN, AN],
        out_specs=(VM,) * 5,
        scratch_shapes=[
            pltpu.VMEM((D, 256), F32),
            pltpu.VMEM((D, 256), F32),
            pltpu.VMEM((FF, 256), BF),
            pltpu.VMEM((384, 256), F32),
            pltpu.VMEM((256, 2 * D), BF),
            pltpu.VMEM((2, 128, PACKED), BF),
            pltpu.SemaphoreType.DMA((2,)),
        ],
        compiler_params=pltpu.CompilerParams(vmem_limit_bytes=58 * 2**20),
        cost_estimate=pl.CostEstimate(flops=5 * 10**9, bytes_accessed=10 * 2**20, transcendentals=0),
        name="weights_back",
    )(meta, own, oth)
    return outs[0], outs[1:5]


def middle_kernel(
    meta, pay, tok_ref, teach_ref, gains, w_out, w_pack, w_down,
    out_ref, sq_ref, pack_out, gm_ref, pay_far,
    gu_scr, o_scr, lse_scr, w_gu, pay_in, out_in, down_in, pack_ref, pay_out, sems,
):
    sources = [pay.at[pl.ds(4 * g, 4)] for g in range(4)] + [w_out, w_pack.at[:, 0 : 2 * FF], w_down]
    targets = [pay_in.at[pl.ds(4 * g, 4)] for g in range(4)] + [out_in, w_gu, down_in]
    _, fetches = fetch_all(sources, targets, sems)
    pay, w_out, w_down = pay_in, out_in, down_in
    sent = []

    def give(source, target):
        sent.append(pltpu.make_async_copy(source, target, sems.at[7 + len(sent)]))
        sent[-1].start()

    spread = spread_rows()
    lane = lanes(128)
    middle = tok_ref[...].astype(F32)
    for g in range(4):
        fetches[g].wait()
        if g == 0:
            fetches[4].wait()
        tiles = [pay[g * 4 + y].astype(F32) for y in range(4)]
        logs = [t[:, 0:128] for t in tiles]
        logs = [t + (pltpu.roll(t, 125, 1) + pltpu.roll(t, 122, 1)) for t in logs]
        logs = [jnp.where(lane < 3, v, 0.0) for v in logs]
        top = jnp.maximum(jnp.maximum(logs[0], logs[1]), jnp.maximum(logs[2], logs[3]))
        shares = [jnp.exp(v - top) for v in logs]
        mass = (shares[0] + shares[1]) + (shares[2] + shares[3])
        o0 = o1 = None
        for t, share in zip(tiles, shares):
            w = share / mass
            p0 = t[:, 0:128] * w[:, 0:1]
            p1 = t[:, 128:256] * jnp.where(lane < 64, w[:, 1:2], w[:, 2:3])
            o0 = p0 if o0 is None else o0 + p0
            o1 = p1 if o1 is None else o1 + p1
        o0 = jnp.where(lane < 64, 0.0, o0)
        lse_scr[g] = top + jnp.log(mass)
        o = jnp.concatenate([o0, o1], axis=1)
        o_scr[g] = o
        pack_ref[:, 3 * FF + 3 * D + 256 * g : 3 * FF + 3 * D + 256 * g + 256] = o.astype(BF)
        middle = middle + mm(o.astype(BF), w_out[192 * g : 192 * g + 256, :])
    r2 = lax.rsqrt(jnp.mean(middle * middle, axis=1, keepdims=True) + EPSILON)
    n2 = middle * r2
    n2b = (n2 * gains[1:2, :]).astype(BF)
    pack_ref[:, 3 * FF : 3 * FF + D] = n2b
    n2p = mm(n2b, spread, NT).astype(BF)
    fetches[5].wait()
    for f in range(4):
        at, up_at = slice(512 * f, 512 * f + 512), slice(FF + 512 * f, FF + 512 * f + 512)
        gate = mm(n2p, w_gu[:, at])
        up = mm(n2p, w_gu[:, up_at])
        gu_scr[:, at] = gate
        gu_scr[:, up_at] = up
        hid = (gate / (1.0 + jnp.exp(-gate)) * up).astype(BF)
        pack_ref[:, 2 * FF + 512 * f : 2 * FF + 512 * f + 512] = hid
    fetches[6].wait()
    total = middle + mm(pack_ref[:, 2 * FF : 3 * FF], w_down[...])
    out_ref[...] = total.astype(BF)
    row = lax.broadcasted_iota(jnp.int32, (128, D), 0)
    mine = meta[0] * 4096 + meta[1] * 1024 + meta[2] * 512 + meta[3] * 128
    diff = jnp.where(row < meta[8] - mine, total - teach_ref[...].astype(F32), 0.0)
    square = diff * diff
    square = sum(square[:, 128 * n : 128 * n + 128] for n in range(6))
    square = jnp.sum(square, axis=0, keepdims=True)
    sq_ref[...] = jnp.broadcast_to(square + pltpu.roll(square, 64, 1), (8, 128))
    g = diff * (16384.0 / jnp.full((1, D), meta[8], jnp.int32).astype(F32))
    gb = g.astype(BF)
    pack_ref[:, 3 * FF + D : 3 * FF + 2 * D] = gb
    give(pack_ref.at[:, 2 * FF : 3 * FF + 2 * D], pack_out.at[:, 2 * FF : 3 * FF + 2 * D])
    give(pack_ref.at[:, 3 * FF + 3 * D : PACKED], pack_out.at[:, 3 * FF + 3 * D : PACKED])
    u = jnp.zeros((128, 1024), F32)
    for f in range(4):
        at, up_at = slice(512 * f, 512 * f + 512), slice(FF + 512 * f, FF + 512 * f + 512)
        gate, up = gu_scr[:, at], gu_scr[:, up_at]
        dh = mm(gb, w_down[at, :], NT)
        sig = 1.0 / (1.0 + jnp.exp(-gate))
        dgate = (dh * up * sig * (1.0 + gate * (1.0 - sig))).astype(BF)
        dup = (dh * gate * sig).astype(BF)
        pack_ref[:, at] = dgate
        pack_ref[:, up_at] = dup
        u = u + mm(dgate, w_gu[:, at], NT) + mm(dup, w_gu[:, up_at], NT)
    give(pack_ref.at[:, 0 : 2 * FF], pack_out.at[:, 0 : 2 * FF])
    u_hi, u_rest = split_two(u)
    u_mid, u_low = split_two(u_rest)
    u = mm(u_hi.astype(BF), spread) + (mm(u_mid.astype(BF), spread) + mm(u_low.astype(BF), spread))
    u = u * gains[1:2, :]
    gm = g + r2 * (u - n2 * jnp.mean(u * n2, axis=1, keepdims=True))
    gm_ref[...] = gm
    gmb = gm.astype(BF)
    pack_ref[:, 3 * FF + 2 * D : 3 * FF + 3 * D] = gmb
    give(pack_ref.at[:, 3 * FF + 2 * D : 3 * FF + 3 * D], pack_out.at[:, 3 * FF + 2 * D : 3 * FF + 3 * D])
    for k in range(4):
        dm = mm(gmb, w_out[192 * k : 192 * k + 256, :], NT).astype(BF)
        d0, d1 = dm[:, 0:128].astype(F32), dm[:, 128:256].astype(F32)
        p0, p1 = d0 * o_scr[k, :, 0:128], d1 * o_scr[k, :, 128:256]
        deltas = [
            jnp.sum(p0, axis=1, keepdims=True),
            jnp.sum(jnp.where(lane < 64, p1, 0.0), axis=1, keepdims=True),
            jnp.sum(jnp.where(lane < 64, 0.0, p1), axis=1, keepdims=True),
        ]
        hi, lo, lowest = split_three(-lse_scr[k])
        delta = jnp.where(lane == 0, deltas[0], jnp.where(lane == 1, deltas[1], deltas[2]))
        dhi, dlo = split_two(-delta)
        aug = jnp.where(lane < 3, hi, jnp.where(lane < 6, pltpu.roll(lo, 3, 1), 0.0))
        aug = jnp.where((lane >= 6) & (lane < 9), pltpu.roll(dhi, 6, 1), aug)
        aug = jnp.where((lane >= 9) & (lane < 12), pltpu.roll(dlo, 9, 1), aug)
        aug = jnp.where((lane >= 12) & (lane < 15), pltpu.roll(lowest, 12, 1), aug)
        d0 = jnp.where(lane < 64, aug, d0).astype(BF)
        for y in range(4):
            pay_out[4 * k + y, :, 0:128] = d0
            pay_out[4 * k + y, :, 128:256] = dm[:, 128:256]
        give(pay_out.at[pl.ds(4 * k, 4)], pay_far.at[pl.ds(4 * k, 4)])
    for copy in sent:
        copy.wait()


def middle_part(meta, pay, tokens, teacher, gains, w_out, w_gu, w_down):
    return pl.pallas_call(
        middle_kernel,
        out_shape=(
            sds((128, D)), sds((8, 128), F32), sds((128, PACKED)), sds((128, D), F32), sds((16, 128, 256)),
        ),
        in_specs=[SM, AN] + [VM] * 3 + [AN] * 3,
        out_specs=(VM, VM, AN, VM, AN),
        scratch_shapes=[
            pltpu.VMEM((128, 2 * FF), F32),
            pltpu.VMEM((4, 128, 256), F32),
            pltpu.VMEM((4, 128, 128), F32),
            pltpu.VMEM((1024, 2 * FF), BF),
            pltpu.VMEM((16, 128, 256), BF),
            pltpu.VMEM((832, D), BF),
            pltpu.VMEM((FF, D), BF),
            pltpu.VMEM((128, PACKED), BF),
            pltpu.VMEM((16, 128, 256), BF),
            pltpu.SemaphoreType.DMA((15,)),
        ],
        compiler_params=pltpu.CompilerParams(vmem_limit_bytes=58 * 2**20),
        cost_estimate=pl.CostEstimate(flops=3 * 10**9, bytes_accessed=16 * 2**20, transcendentals=10**6),
        name="middle_part",
    )(meta, pay, tokens, teacher, gains, w_out, w_gu, w_down)


def finish_kernel(meta, g_ref, wq, wk, wv, gain, q_out, k_out, v_out, ga_out, loss_out):
    total, tail = None, None
    for x in range(4):
        part = g_ref[16 * x].astype(F32)
        for n in range(1, 16):
            part = part + g_ref[16 * x + n].astype(F32)
        lane = lax.broadcasted_iota(jnp.int32, (8, 128), 1)
        none = jnp.zeros((8, 512), F32)
        kv1 = part[:, 128:256]
        keys = [part[:, 0:128], jnp.where(lane < 64, kv1, 0.0)]
        values = [jnp.where(lane < 64, 0.0, kv1), part[:, 256:384]]
        last = part[:, 512:640]
        queries = [part[:, 384:512], jnp.where(lane < 64, last, 0.0)]
        wide = [jnp.concatenate(t + [none], axis=1) for t in (keys, values, queries)]
        shifts = (192 * x, (192 * x - 64) % D, 192 * x)
        wide = [pltpu.roll(a, s, 1) if s else a for a, s in zip(wide, shifts)]
        total = wide if total is None else [a + b for a, b in zip(total, wide)]
        tail = last if tail is None else tail + last
    keys, values, queries = total
    q_out[...], k_out[...], v_out[...] = queries[0:6], keys[0:6], values[0:6]
    by_row = keys[0:6] * wk[...].astype(F32) + values[0:6] * wv[...].astype(F32)
    by_row = by_row + queries[0:6] * wq[...].astype(F32)
    rows = jnp.sum(by_row, axis=1, keepdims=True)
    row = lax.broadcasted_iota(jnp.int32, (6, 128), 0)
    lane = lax.broadcasted_iota(jnp.int32, (6, 128), 1)
    across = jnp.sum(jnp.where(row == lane, rows, 0.0), axis=0, keepdims=True)
    ga_out[...] = across[:, 0:6] / gain[...].astype(F32)
    counted = jnp.full((1, 128), meta[8], jnp.int32).astype(F32)
    high = lax.broadcasted_iota(jnp.int32, (1, 128), 1) >= 64
    loss = jnp.sum(jnp.where(high, tail[0:1, :], 0.0), axis=1, keepdims=True)
    loss_out[...] = jnp.broadcast_to(loss / (counted * D), (1, 128))


def finish(meta, g, wq, wk, wv, gain):
    return pl.pallas_call(
        finish_kernel,
        out_shape=(sds((6, D), F32),) * 3 + (sds((1, 6), F32), sds((1, 128), F32)),
        in_specs=[SM] + [VM] * 5,
        out_specs=(VM,) * 5,
        cost_estimate=pl.CostEstimate(flops=10**6, bytes_accessed=10**6, transcendentals=0),
        name="finish",
    )(meta, g, wq, wk, wv, gain.reshape(1, 6))


def from_behind(x, axis, j):
    return lax.ppermute(x, axis, [(s, (s + j) % 4) for s in range(4)])


def from_ahead(x, axis, j):
    return lax.ppermute(x, axis, [(s, (s - j) % 4) for s in range(4)])


def from_core(x):
    return lax.ppermute(x, C, [(0, 1), (1, 0)])


def gather4(x, axis):
    return [x] + [from_behind(x, axis, j) for j in (1, 2, 3)]


def in_order(blocks, index, dim):
    r0, r1, r2, r3 = blocks
    twice = jnp.concatenate([r3, r2, r1, r0, r3, r2, r1], axis=dim)
    size = r0.shape[dim]
    return lax.dynamic_slice_in_dim(twice, (3 - index) * size, 4 * size, dim)


def block_of(x, index):
    return lax.dynamic_index_in_dim(x, index, 0, keepdims=False)


def scatter4(x, axis, index):
    own = block_of(x, index).astype(F32)
    far = [from_ahead(block_of(x, (index - j) & 3), axis, j).astype(F32) for j in (1, 2, 3)]
    return (own + far[1]) + (far[0] + far[2])


def summed(parts):
    a, b, c, d = (p.astype(F32) for p in parts)
    return (a + c) + (b + d)


def per_device(
    tokens, attn_gain, w_query, w_key, w_value, w_out, mlp_gain, w_gate, w_up, w_down, segments, teacher
):
    ix, iz, ic, iy = (lax.axis_index(a) for a in (X, Z, C, Y))
    begin = iz * 1024 + ic * 512

    heads, pack = prepare(
        w_query, w_key, w_value, attn_gain, mlp_gain, w_gate, w_up, w_out, w_down
    )
    pack = lax.all_gather(pack, BLK_HD)
    w_rows = lax.all_to_all(heads, (X, Z, Y), split_axis=0, concat_axis=0, tiled=True)
    w_rows = w_rows.reshape(512, WIDE)
    t_rows = gather4(tokens, X)

    place = jnp.where(
        jnp.arange(4) == 0, ix, jnp.where(jnp.arange(4) == 1, iz, jnp.where(jnp.arange(4) == 2, ic, iy))
    ).astype(jnp.int32)
    meta, lab = documents(place, segments.reshape(128, 128))

    exponents = jnp.arange(32, dtype=jnp.float32) * (-2.0 / HEAD_SIZE)
    frequency = jnp.tile(ROPE_BASE**exponents, 4)
    runs = ((ix - jnp.arange(4, dtype=jnp.int32)) & 3) * 4096
    places = runs[:, None] + begin + iy * 128 + jnp.arange(128, dtype=jnp.int32)[None]
    angles = places.astype(F32)[:, :, None] * frequency[None, None, :]
    cosine = jnp.cos(angles)
    sine = jnp.sin(angles) * jnp.where(jnp.arange(128) % 64 < 32, -1.0, 1.0)

    w_rows, t_rows, cosine, sine, meta, lab = lax.optimization_barrier(
        (w_rows, t_rows, cosine, sine, meta, lab)
    )
    w_rows = [w_rows, from_core(w_rows)]
    q, kv, w_full, n_rows, gain_rows = project(meta, w_rows, t_rows, cosine, sine)
    q_all, kv_own = gather4(q, Y), gather4(kv, Z)
    q_all, kv_own = lax.optimization_barrier((q_all, kv_own))
    kv_oth = [from_core(kv) for kv in kv_own]

    pay = attend(meta, lab, q_all, kv_own, kv_oth).reshape(16, 128, 256)
    pay = lax.all_to_all(pay, (X, Y), split_axis=0, concat_axis=0, tiled=True)
    w_out_all = jnp.pad(pack[:, :6, 4096:4864].reshape(D, D), ((64, 0), (0, 0)))
    w_down_all = pack[:, :, 4864:].reshape(128, 8, 2, D).transpose(0, 2, 1, 3).reshape(FF, D)
    out, squares, packed, grad_middle, dpay = middle_part(
        meta, pay, tokens, teacher, gain_rows, w_out_all, pack.reshape(1024, -1), w_down_all
    )
    dout = lax.all_to_all(dpay, (X, Y), split_axis=0, concat_axis=0, tiled=True)

    part_a, part_b = weights_back(meta, packed, from_core(packed))
    dout, _, _ = lax.optimization_barrier((dout, part_a, part_b))
    part_a = lax.psum_scatter(part_a.reshape(-1, 128), X, scatter_dimension=0, tiled=True)
    part_a = lax.psum_scatter(part_a, Z, scatter_dimension=0, tiled=True)
    far_b = [from_ahead(part_b[j], Z, j) for j in (1, 2, 3)]

    dq, dkv_own, dkv_oth = attend_back(
        meta, lab, q_all, kv_own, kv_oth, dout.reshape(4, 4, 128, 256)
    )
    dq, dkv_own, dkv_oth, far_b = lax.optimization_barrier((dq, dkv_own, dkv_oth, far_b))
    dq = [dq[0]] + [from_ahead(dq[j], Y, j) for j in (1, 2, 3)]
    dkv_oth = from_core(dkv_oth)
    dkv = [(dkv_own[j].astype(F32) + dkv_oth[j].astype(F32)).astype(BF) for j in range(4)]
    dkv, far_b = lax.optimization_barrier((dkv, far_b))
    dkv = [dkv[0]] + [from_ahead(dkv[j], Z, j) for j in (1, 2, 3)]
    part_b = summed([part_b[0]] + far_b).astype(BF)
    far_b = [from_ahead(part_b[j], X, j) for j in (1, 2, 3)]
    dq, dkv, far_b, part_a = lax.optimization_barrier((dq, dkv, far_b, part_a))
    part_b = summed([part_b[0]] + far_b).astype(BF)
    u, keep, send = project_back(meta, w_full, n_rows, cosine, sine, squares, dq, dkv)

    gu = jnp.concatenate([part_a[:384], part_b[:384]]).reshape(32, 4, 6, 128)
    gu = gu.transpose(1, 0, 2, 3).reshape(4, 192, 128)
    down = part_b[384:].reshape(6, 4, 16, 128)
    down = down.transpose(1, 0, 2, 3).reshape(4, 96, 128)
    outer = part_a[384:].reshape(6, 4, 6, 128).transpose(1, 0, 2, 3).reshape(4, 36, 128)
    grads = jnp.concatenate([gu, down, outer], axis=1)
    own_grads = block_of(grads, iy)
    far_grads = [from_ahead(block_of(grads, (iy - j) & 3), Y, j) for j in (1, 2, 3)]
    far_u = [from_ahead(u[j], X, j) for j in (1, 2, 3)]
    g = (keep.astype(F32) + from_core(send).astype(F32)).astype(BF).reshape(64, 8, WIDE)
    g = lax.all_to_all(g, (X, Z, Y), split_axis=0, concat_axis=0, tiled=True)
    g, far_grads, far_u = lax.optimization_barrier((g, far_grads, far_u))
    grads = summed([own_grads] + far_grads)

    u = summed([u[0]] + far_u) * gain_rows[0:1]
    wide = tokens.astype(F32)
    r1 = lax.rsqrt(jnp.mean(wide * wide, axis=1, keepdims=True) + EPSILON)
    n1 = wide * r1
    grad_tokens = grad_middle + r1 * (u - n1 * jnp.mean(u * n1, axis=1, keepdims=True))

    grad_query, grad_key, grad_value, grad_attn_gain, mean_loss = finish(
        meta, g, w_query, w_key, w_value, attn_gain
    )
    mean_loss, grad_attn_gain = mean_loss[0, 0], grad_attn_gain.reshape(6)

    gu = grads[:192].reshape(32, 6, 128).transpose(1, 0, 2).reshape(6, 2 * FF)
    down = grads[192:288].reshape(6, 16, 128).transpose(1, 0, 2).reshape(16, D)
    outer = grads[288:].reshape(6, 6, 128).transpose(1, 0, 2).reshape(6, D)
    grad_gate, grad_up = gu[:, :FF], gu[:, FF:]
    by_row = grad_gate * w_gate.astype(F32) + grad_up * w_up.astype(F32)
    grad_mlp_gain = jnp.sum(by_row, axis=1) / mlp_gain.astype(F32)
    return (
        out,
        grad_tokens.astype(BF),
        mean_loss,
        grad_attn_gain,
        grad_query,
        grad_key,
        grad_value,
        outer,
        grad_mlp_gain,
        grad_gate,
        grad_up,
        down,
    )


def solution(mesh):
    torus = Mesh(mesh.devices.reshape(4, 4, 2, mesh.shape["hd"]), BLK_HD)
    rows, vector = P(BLK_HD, None), P(BLK_HD)
    return jax.shard_map(
        per_device,
        mesh=torus,
        in_specs=(rows, vector, rows, rows, rows, rows, vector, rows, rows, rows, P(), rows),
        out_specs=(rows, rows, P(), vector, rows, rows, rows, rows, vector, rows, rows, rows),
        check_vma=False,
    )
```

```python
import jax
import jax.numpy as jnp
from jax import lax
from jax.experimental import pallas as pl
from jax.experimental.pallas import tpu as pltpu
from jax.sharding import Mesh
from jax.sharding import PartitionSpec as P

HEADS = 12
HEAD_SIZE = 64
D = 768
FF = 2048
EPSILON = 1e-05
ROPE_BASE = 10000.0
X, Z, C, Y = "blk_0", "blk_1", "blk_2", "hd"
BLK = (X, Z, C)
BLK_HD = (X, Z, C, Y)
WIDE = 640

BF = jnp.bfloat16
F32 = jnp.float32
NEG = -1e30
LABEL_LANE = 72
LABELS = 25
NT = (((1,), (1,)), ((), ()))
TN = (((0,), (0,)), ((), ()))
NN = (((1,), (0,)), ((), ()))
LIMIT = 70.0


def mm(a, b, dims=NN):
    return lax.dot_general(a, b, dims, preferred_element_type=F32)


def lanes(rows):
    return lax.broadcasted_iota(jnp.int32, (rows, 128), 1)


def rows_of(rows):
    return lax.broadcasted_iota(jnp.int32, (rows, 128), 0)


def lane_masks():
    lane = lanes(128)
    low = (lane < 64).astype(F32)
    head = rows_of(128) // 64
    first = (head == lane).astype(F32).astype(BF)
    second = ((head == 0) & (lane == 2)).astype(F32).astype(BF)
    return low.astype(BF), (1.0 - low).astype(BF), first, second


def one_lane(n):
    return (lanes(128) == n).astype(F32).astype(BF)


def stage_keys(meta, lab, own, oth, kaug, other):
    ix, iz, ic, iy = (meta[k] for k in range(4))
    lane = lanes(128)
    row = rows_of(128)
    first, last = lab[0:1, :], lab[1:2, :]
    one = ((lane >= 64) & (lane < 67)).astype(F32)
    low, _, _, _ = lane_masks()

    def place(i, _):
        for j in range(4):
            ki = ((ix - i) & 3) * 4 + ((iz - j) & 3)
            for ref, core in ((own[j], ic), (oth[j], 1 - ic)):
                at = pl.multiple_of(ki * 256 + core * 128, 128)
                k0, k1, v1 = (ref[i, :, 128 * n : 128 * n + 128] for n in range(3))
                place_at = ki * 1024 + core * 512 + iy * 128 + row
                outside = (place_at < first) | (place_at >= last)
                half = k1 * low
                kaug[pl.ds(at, 128), 0:128] = k0
                kaug[pl.ds(at, 128), 128:256] = half + jnp.where(outside, NEG, one).astype(BF)
                other(at, k0, half, k1, v1)
        return 0

    lax.fori_loop(0, 4, place, 0)


def split_two(x):
    hi = x.astype(BF).astype(F32)
    return hi, x - hi


def split_three(x):
    hi, rest = split_two(x)
    return (hi, *split_two(rest))


def fwd_kernel(meta, lab, *refs):
    out_ref, kaug, vbd, qm, acc, q_in, kv_in, sems = refs[12:]
    fetches = [
        pltpu.make_async_copy(ref, q_in.at[n] if n < 4 else kv_in.at[n - 4], sems.at[n])
        for n, ref in enumerate(refs[0:12])
    ]
    for fetch in fetches[4:] + fetches[:4]:
        fetch.start()
    q_refs = [q_in.at[n] for n in range(4)]
    kv_own, kv_oth = ([kv_in.at[n + at] for n in range(4)] for at in (0, 4))
    for fetch in fetches[4:]:
        fetch.wait()
    ix, iz, ic, iy = (meta[k] for k in range(4))
    lane = lanes(128)
    first, last = lab[0:1, :], lab[1:2, :]
    is_label = (lane >= LABEL_LANE) & (lane < LABEL_LANE + LABELS)
    zeros = jnp.zeros((128, 128), BF)
    low, high, by_head0, by_head1 = lane_masks()
    ones = [one_lane(h) for h in range(3)]

    def value_rows(at, k0, half, k1, v1):
        t = at // 256
        inner = pl.multiple_of(at % 256, 128)
        rows = [pl.ds(256 * h + inner, 128) for h in range(3)]
        vbd[t, rows[0], 0:128] = k1 * high + ones[0]
        vbd[t, rows[0], 128:256] = zeros
        vbd[t, rows[1], 0:128] = ones[1]
        vbd[t, rows[1], 128:256] = v1 * low
        vbd[t, rows[2], 0:128] = ones[2]
        vbd[t, rows[2], 128:256] = v1 * high

    stage_keys(meta, lab, kv_own, kv_oth, kaug, value_rows)
    for fetch in fetches[:4]:
        fetch.wait()
    key_norms = query_norms = jnp.zeros((1, 128), F32)
    for n in range(4):
        for ref, at in ((kaug, pl.ds(1024 * n, 1024)), (q_refs[n], slice(None))):
            whole = ref[at].reshape(-1, 256)
            v0, v1 = whole[:, 0:128], whole[:, 128:256] * low[0:1, :]
            norms = mm(v0 * v0, by_head0) + mm(v1 * v1, by_head1)
            norms = jnp.max(norms, axis=0, keepdims=True)
            if ref is kaug:
                key_norms = jnp.maximum(key_norms, norms)
            else:
                query_norms = jnp.maximum(query_norms, norms)
    bound = key_norms * query_norms
    small = jnp.max(bound) < LIMIT * LIMIT

    def one_run(xr, _):
        i = (ix - xr) & 3
        begin = xr * 4096 + iz * 1024 + ic * 512
        for j in range(4):
            yq = (iy - j) & 3
            q0, q1 = q_refs[j][i, :, 0:128], q_refs[j][i, :, 128:256]
            place = begin + yq * 128 + rows_of(128)
            mine = is_label & (place >= first) & (place < last)
            label = jnp.where(mine, 1.0, 0.0).astype(BF)
            at = [pl.ds(pl.multiple_of(512 * h + yq * 128, 128), 128) for h in range(3)]
            qm[at[0], 0:128] = q0 * low
            qm[at[0], 128:256] = label
            qm[at[1], 0:128] = q0 * high
            qm[at[1], 128:256] = label
            qm[at[2], 0:128] = zeros
            qm[at[2], 128:256] = q1 * low + label
        start = meta[4 + xr]
        end = xr * 4 + iz

        def allowed_keys(t):
            key_row = lax.broadcasted_iota(jnp.int32, (256, 512), 0)
            key_place = t * 1024 + iy * 128 + key_row + jnp.where(key_row >= 128, 512 - 128, 0)
            return key_place <= begin + lax.broadcasted_iota(jnp.int32, (256, 512), 1)

        acc[...] = jnp.zeros((512, 256), F32)

        def fast(tiles, diagonal):
            probs = []
            for t in tiles:
                s = mm(qm[...], kaug[pl.ds(pl.multiple_of(t * 256, 256), 256), :], NT)
                if diagonal:
                    key_lane = lax.broadcasted_iota(jnp.int32, (512, 256), 1)
                    key_place = t * 1024 + iy * 128 + key_lane + jnp.where(key_lane >= 128, 512 - 128, 0)
                    allowed = key_place <= begin + lax.broadcasted_iota(jnp.int32, (512, 256), 0)
                for h in range(3):
                    part = s[512 * h : 512 * h + 512]
                    if diagonal:
                        part = jnp.where(allowed, part, NEG)
                    probs.append(jnp.exp(part).astype(BF))
            probs = jnp.concatenate(probs, axis=1)
            values = vbd[pl.ds(tiles[0], len(tiles))].reshape(768 * len(tiles), 256)
            acc[...] += mm(probs, values)

        def finish(highest):
            a0, a1 = acc[:, 0:128], acc[:, 128:256]
            lane5 = lanes(512)
            some = a0 > 0.0
            mass = jnp.where(some, a0, 1.0)
            inverse = jnp.where(some, 1.0 / mass, 0.0)
            log_mass = jnp.where(some, jnp.log(mass) + highest, NEG)
            hi, mid, lo = split_three(log_mass)
            extra = jnp.where(lane5 < 6, pltpu.roll(mid, 3, 1), pltpu.roll(lo, 6, 1))
            extra = jnp.where(lane5 < 3, hi, extra)
            scaled = [inverse[:, h : h + 1] for h in range(3)]
            o0 = jnp.where(lane5 >= 64, a0 * scaled[0], jnp.where(lane5 < 9, extra, 0.0)).astype(BF)
            o1 = (a1 * jnp.where(lane5 < 64, scaled[1], scaled[2])).astype(BF)
            for yq in range(4):
                at = slice(yq * 128, yq * 128 + 128)
                out_ref[xr, yq, :, 0:128] = o0[at]
                out_ref[xr, yq, :, 128:256] = o1[at]

        @pl.when(small)
        def _():
            def step(t, _):
                fast((start + 2 * t, start + 2 * t + 1), False)
                return 0

            lax.fori_loop(0, (end - start) // 2, step, 0)

            @pl.when(((end - start) & 1) == 1)
            def _():
                fast((end - 1,), False)

            fast((end,), True)
            finish(0.0)

        @pl.when(jnp.logical_not(small))
        def _():
            lane5 = lanes(512)

            def step(t, highs):
                at = pl.ds(pl.multiple_of(t * 256, 256), 256)
                keys = kaug[at, :]
                allowed = allowed_keys(t)
                a0, a1 = acc[:, 0:128], acc[:, 128:256]
                total, fresh, scales = None, [], []
                for h in range(3):
                    s = jnp.where(allowed, mm(keys, qm[512 * h : 512 * h + 512, :], NT), NEG)
                    top = jnp.maximum(highs[h], jnp.max(s, axis=0, keepdims=True))
                    scales.append(jnp.exp(highs[h] - top))
                    p = jnp.where(s < 0.5 * NEG, 0.0, jnp.exp(s - top)).astype(BF)
                    part = mm(p, vbd[t, 256 * h : 256 * h + 256, :], TN)
                    total = part if total is None else total + part
                    fresh.append(top)
                rows = jnp.concatenate(scales + [jnp.zeros((125, 512), F32)], axis=0)
                columns = rows.T
                scales = [columns[:, h : h + 1] for h in range(3)]
                factor0 = jnp.where((lane5 >= 64) | (lane5 == 0), scales[0], 1.0)
                factor0 = jnp.where(lane5 == 1, scales[1], jnp.where(lane5 == 2, scales[2], factor0))
                factor1 = jnp.where(lane5 < 64, scales[1], scales[2])
                acc[:, 0:128] = a0 * factor0 + total[:, 0:128]
                acc[:, 128:256] = a1 * factor1 + total[:, 128:256]
                return tuple(fresh)

            lowest = tuple(jnp.full((1, 512), NEG, F32) for _ in range(3))
            highs = lax.fori_loop(start, end + 1, step, lowest)
            rows = jnp.concatenate(list(highs) + [jnp.zeros((125, 512), F32)], axis=0)
            finish(rows.T)

        return 0

    lax.fori_loop(0, 4, one_run, 0)


def bwd_kernel(meta, lab, *refs):
    q_refs, kv_own, kv_oth, do_ref = refs[0:4], refs[4:8], refs[8:12], refs[12]
    dq_refs, dkv_own, dkv_oth = refs[13:17], refs[17], refs[18]
    kaug, vaug, kt, qa, da, dq_acc, dk_acc, dv_acc, dq_rows = refs[19:]
    ix, iz, ic, iy = (meta[k] for k in range(4))
    lane = lanes(128)
    first, last = lab[0:1, :], lab[1:2, :]
    is_label = (lane >= LABEL_LANE) & (lane < LABEL_LANE + LABELS)
    zeros = jnp.zeros((128, 128), BF)

    low, high, _, _ = lane_masks()
    two = ((lane < 2).astype(F32)).astype(BF)
    row = rows_of(128)

    def pick(pairs):
        chosen = [(row == a) & (lane == b) for a, b in pairs]
        return sum(jnp.where(c, 1.0, 0.0) for c in chosen).astype(BF)

    shift_pick = [pick(((h, 64), (h + 3, 65), (h + 12, 66))) for h in range(3)]
    delta_pick = [pick(((h + 6, 0), (h + 9, 1))) for h in range(3)]

    def value_rows(at, k0, half, k1, v1):
        vaug[pl.ds(at, 128), 0:128] = k1 * high + two
        vaug[pl.ds(at, 128), 128:256] = v1

    stage_keys(meta, lab, kv_own, kv_oth, kaug, value_rows)

    def turn(t, _):
        at = pl.ds(pl.multiple_of(t * 256, 256), 256)
        kt[t] = kaug[at, :].T
        return 0

    lax.fori_loop(0, 16, turn, 0)
    dk_acc[...] = jnp.zeros_like(dk_acc)
    dv_acc[...] = jnp.zeros_like(dv_acc)

    def one_run(xr, _):
        i = (ix - xr) & 3
        begin = xr * 4096 + iz * 1024 + ic * 512
        for j in range(4):
            yq = (iy - j) & 3
            q0, q1 = q_refs[j][i, :, 0:128], q_refs[j][i, :, 128:256]
            d0, d1 = do_ref[xr, yq, :, 0:128], do_ref[xr, yq, :, 128:256]
            place = begin + yq * 128 + rows_of(128)
            mine = is_label & (place >= first) & (place < last)
            label = jnp.where(mine, 1.0, 0.0)
            for h in range(3):
                at = pl.ds(pl.multiple_of(512 * h + yq * 128, 128), 128)
                aug = (mm(d0, shift_pick[h]) + label).astype(BF)
                qa[at, 0:128] = q0 * (low, high, low * high)[h]
                qa[at, 128:256] = (q1 * low + aug) if h == 2 else aug
                aug = mm(d0, delta_pick[h]).astype(BF)
                da[at, 0:128] = (d0 * high + aug) if h == 0 else aug
                da[at, 128:256] = d1 * (low * high, low, high)[h]
        start = meta[4 + xr]
        end = xr * 4 + iz
        dq_acc[...] = jnp.zeros_like(dq_acc)

        def tile(t, diagonal):
            at = pl.ds(pl.multiple_of(t * 256, 256), 256)
            keys, values = kaug[at, :], vaug[at, :]
            if diagonal:
                key_row = lax.broadcasted_iota(jnp.int32, (256, 512), 0)
                key_place = t * 1024 + iy * 128 + key_row + jnp.where(key_row >= 128, 512 - 128, 0)
                place = begin + lax.broadcasted_iota(jnp.int32, (256, 512), 1)
                allowed = key_place <= place
            s = mm(keys, qa[...], NT)
            dp = mm(values, da[...], NT)
            probs, grads = [], []
            for h in range(3):
                part = s[:, 512 * h : 512 * h + 512]
                if diagonal:
                    part = jnp.where(allowed, part, NEG)
                p = jnp.exp(part)
                ds = (p * dp[:, 512 * h : 512 * h + 512]).astype(BF)
                probs.append(p.astype(BF))
                grads.append(ds)
                dq_acc[h] += mm(kt[t, 64 * h : 64 * h + 64, :], ds)
            dv_acc[at, :] += mm(jnp.concatenate(probs, axis=1), da[...])
            dk_acc[at, :] += mm(jnp.concatenate(grads, axis=1), qa[...])

        def step(t, _):
            tile(start + 2 * t, False)
            tile(start + 2 * t + 1, False)
            return 0

        lax.fori_loop(0, (end - start) // 2, step, 0)

        @pl.when(((end - start) & 1) == 1)
        def _():
            tile(end - 1, False)

        tile(end, True)
        whole = jnp.concatenate([dq_acc[0], dq_acc[1], dq_acc[2], jnp.zeros((64, 512), F32)], axis=0)
        dq_rows[...] = whole.T.astype(BF)
        for j in range(4):
            yq = (iy - j) & 3
            dq_refs[j][i] = dq_rows[pl.ds(pl.multiple_of(yq * 128, 128), 128), :]
        return 0

    lax.fori_loop(0, 4, one_run, 0)

    def give(i, _):
        for j in range(4):
            ki = ((ix - i) & 3) * 4 + ((iz - j) & 3)
            for ref, core in ((dkv_own, ic), (dkv_oth, 1 - ic)):
                at = pl.ds(pl.multiple_of(ki * 256 + core * 128, 128), 128)
                middle = jnp.where(lane < 64, dk_acc[at, 128:256], dv_acc[at, 0:128])
                ref[j, i, :, 0:128] = dk_acc[at, 0:128].astype(BF)
                ref[j, i, :, 128:256] = middle.astype(BF)
                ref[j, i, :, 256:384] = dv_acc[at, 128:256].astype(BF)
        return 0

    lax.fori_loop(0, 4, give, 0)


def sds(shape, dtype=BF):
    return jax.ShapeDtypeStruct(shape, dtype)


VM = pl.BlockSpec(memory_space=pltpu.VMEM)
SM = pl.BlockSpec(memory_space=pltpu.SMEM)


def attend(meta, lab, q, kv_own, kv_oth):
    return pl.pallas_call(
        fwd_kernel,
        out_shape=sds((4, 4, 128, 256)),
        in_specs=[SM, VM] + [pl.BlockSpec(memory_space=pl.ANY)] * 12,
        out_specs=VM,
        scratch_shapes=[
            pltpu.VMEM((4096, 256), BF),
            pltpu.VMEM((16, 768, 256), BF),
            pltpu.VMEM((1536, 256), BF),
            pltpu.VMEM((512, 256), F32),
            pltpu.VMEM((4, 4, 128, 256), BF),
            pltpu.VMEM((8, 4, 128, 384), BF),
            pltpu.SemaphoreType.DMA((12,)),
        ],
        compiler_params=pltpu.CompilerParams(vmem_limit_bytes=58 * 2**20),
        cost_estimate=pl.CostEstimate(flops=20 * 10**9, bytes_accessed=8 * 2**20, transcendentals=10**7),
        name="attend",
    )(meta, lab, *q, *kv_own, *kv_oth)


def attend_back(meta, lab, q, kv_own, kv_oth, dout):
    outs = pl.pallas_call(
        bwd_kernel,
        out_shape=(sds((4, 128, 256)),) * 4 + (sds((4, 4, 128, 384)),) * 2,
        in_specs=[SM] + [VM] * 14,
        out_specs=(VM,) * 6,
        scratch_shapes=[
            pltpu.VMEM((4096, 256), BF),
            pltpu.VMEM((4096, 256), BF),
            pltpu.VMEM((16, 256, 256), BF),
            pltpu.VMEM((1536, 256), BF),
            pltpu.VMEM((1536, 256), BF),
            pltpu.VMEM((3, 64, 512), F32),
            pltpu.VMEM((4096, 256), F32),
            pltpu.VMEM((4096, 256), F32),
            pltpu.VMEM((512, 256), BF),
        ],
        compiler_params=pltpu.CompilerParams(vmem_limit_bytes=56 * 2**20),
        cost_estimate=pl.CostEstimate(flops=50 * 10**9, bytes_accessed=16 * 2**20, transcendentals=10**7),
        name="attend_back",
    )(meta, lab, *q, *kv_own, *kv_oth, dout)
    return outs[0:4], outs[4], outs[5]


def spread_rows():
    row = lax.broadcasted_iota(jnp.int32, (1024, D), 0)
    column = lax.broadcasted_iota(jnp.int32, (1024, D), 1)
    inner = row % 8
    return jnp.where((inner < 6) & (row // 8 * 6 + inner == column), 1.0, 0.0).astype(BF)


AN = pl.BlockSpec(memory_space=pl.ANY)


def fetch_all(sources, targets, sems):
    copies = [pltpu.make_async_copy(a, b, sems.at[n]) for n, (a, b) in enumerate(zip(sources, targets))]
    for copy in copies:
        copy.start()
    return targets, copies


def documents_kernel(place, seg_ref, meta, lab_ref):
    ix, iz, ic, iy = (place[k] for k in range(4))
    seg = seg_ref[...]
    lane = lax.broadcasted_iota(jnp.int32, (1, 128), 1)
    some = seg != 0
    counted = jnp.sum(some.astype(jnp.int32))
    starts, ends = jnp.zeros((1, 128), jnp.int32), jnp.full((1, 128), 16384, jnp.int32)
    begins = []
    for label in range(LABELS):
        start, end = counted, jnp.int32(16384)
        if label:
            start = jnp.sum((some & (seg < label)).astype(jnp.int32))
            end = jnp.sum((some & (seg <= label)).astype(jnp.int32))
        starts = jnp.where(lane == LABEL_LANE + label, start, starts)
        ends = jnp.where(lane == LABEL_LANE + label, end, ends)
        begins.append(start)
    row = lax.broadcasted_iota(jnp.int32, (8, 128), 0)
    lab_ref[...] = jnp.where(row == 0, starts, ends)
    for k in range(4):
        meta[k] = place[k]
    for xr in range(4):
        at = xr * 32 + iz * 8 + ic * 4
        mine = jnp.sum(jnp.where(lane == 0, seg_ref[pl.ds(at, 1), :], 0))
        first = jnp.int32(0)
        for label in range(LABELS):
            first = jnp.where(mine == label, begins[label], first)
        meta[4 + xr] = lax.shift_right_logical(first, 10)
    meta[8] = counted


def documents(place, segments):
    return pl.pallas_call(
        documents_kernel,
        out_shape=(sds((9,), jnp.int32), sds((8, 128), jnp.int32)),
        in_specs=[SM, VM],
        out_specs=(SM, VM),
        cost_estimate=pl.CostEstimate(flops=10**6, bytes_accessed=10**5, transcendentals=0),
        name="documents",
    )(place, segments)


def prepare_kernel(wq, wk, wv, ga, gm, wg, wu, wo, wd, heads_ref, pack_ref):
    row = lax.broadcasted_iota(jnp.int32, (8, 128), 0)
    lane = lax.broadcasted_iota(jnp.int32, (8, 128), 1)

    def eight(ref, width):
        empty = jnp.zeros((2, width), F32)
        return jnp.concatenate([ref[...].astype(F32), empty], axis=0)

    def column(ref):
        across = jnp.broadcast_to(jnp.pad(ref[...].astype(F32), ((0, 0), (0, 122))), (8, 128))
        return jnp.sum(jnp.where(lane == row, across, 0.0), axis=1, keepdims=True)

    wide = [eight(ref, D) for ref in (wk, wv, wq)]
    gains = jnp.where(lane == 64, column(ga), jnp.where(lane == 65, column(gm), 0.0))
    for g in range(4):
        k, v, q = (pltpu.roll(w, (D - 192 * g) % D, 1)[:, 0:256] if g else w[:, 0:256] for w in wide)
        low = lane < 64
        v = pltpu.roll(v, 64, 1)
        tiles = [
            k[:, 0:128],
            jnp.where(low, k[:, 128:256], v[:, 0:128]),
            v[:, 128:256],
            q[:, 0:128],
            jnp.where(low, q[:, 128:256], gains),
        ]
        block = jnp.concatenate(tiles, axis=1).astype(BF)
        for n in range(16):
            heads_ref[16 * g + n] = block
    pack_ref[:, 0:FF] = eight(wg, FF).astype(BF)
    pack_ref[:, FF : 2 * FF] = eight(wu, FF).astype(BF)
    pack_ref[:, 2 * FF : 2 * FF + D] = eight(wo, D).astype(BF)
    pack_ref[:, 2 * FF + D : 2 * FF + 2 * D] = wd[0:8, :]
    pack_ref[:, 2 * FF + 2 * D : 2 * FF + 3 * D] = wd[8:16, :]


def prepare(wq, wk, wv, ga, gm, wg, wu, wo, wd):
    return pl.pallas_call(
        prepare_kernel,
        out_shape=(sds((64, 8, WIDE)), sds((8, 2 * FF + 3 * D))),
        in_specs=[VM] * 9,
        out_specs=(VM, VM),
        cost_estimate=pl.CostEstimate(flops=10**6, bytes_accessed=2 * 10**6, transcendentals=0),
        name="prepare",
    )(wq, wk, wv, ga.reshape(1, 6), gm.reshape(1, 6), wg, wu, wo, wd)


def close_rows():
    row = lax.broadcasted_iota(jnp.int32, (D, 1024), 0)
    column = lax.broadcasted_iota(jnp.int32, (D, 1024), 1)
    inner = column % 8
    return jnp.where((inner < 6) & (column // 8 * 6 + inner == row), 1.0, 0.0).astype(BF)


def project_kernel(
    meta, w_own, w_oth, t0, t1, t2, t3, cos_ref, sin_ref, q_out, kv_out, w_far, n_far, gain_out,
    w_scr, w_in, t_in, q_ref, kv_ref, w_out, n_out, turn_in, sems,
):
    targets = [w_in.at[0], w_in.at[1]] + [t_in.at[n] for n in range(4)] + [turn_in.at[0], turn_in.at[1]]
    sources = (w_own, w_oth, t0, t1, t2, t3, cos_ref, sin_ref)
    (w_own, w_oth, *_, cos_ref, sin_ref), fetches = fetch_all(sources, targets, sems)
    for fetch in fetches[0:2]:
        fetch.wait()
    sent = []

    def give(source, target):
        sent.append(pltpu.make_async_copy(source, target, sems.at[8 + len(sent)]))
        sent[-1].start()

    for ref, core in ((w_own, meta[2]), (w_oth, 1 - meta[2])):
        for chip in range(16):
            at = pl.multiple_of(64 * chip + 32 * core, 32)
            w_scr[pl.ds(at, 32), :] = ref[32 * chip : 32 * chip + 32, :]
    w = mm(close_rows(), w_scr[...]).astype(BF)
    w_out[...] = w
    give(w_out, w_far)
    tail = w[:, 512:640]
    row, lane = lax.broadcasted_iota(jnp.int32, (8, 128), 0), lax.broadcasted_iota(jnp.int32, (8, 128), 1)
    pick = jnp.where(lane == row + 64, 1.0, 0.0).astype(BF)
    gains = mm(pick, tail, NT)
    gain_out[...] = gains
    for fetch in fetches[2:]:
        fetch.wait()
    for i in range(4):
        wide = t_in[i].astype(F32)
        r1 = lax.rsqrt(jnp.mean(wide * wide, axis=1, keepdims=True) + EPSILON)
        n = (wide * r1 * gains[0:1, :]).astype(BF)
        n_out[i] = n
        y = mm(n, w_out[...])
        turned = turn_heads(y, cos_ref[i], sin_ref[i], 0.125)
        kv_ref[i] = turned[:, 0:384].astype(BF)
        q_ref[i] = turned[:, 384:640].astype(BF)
        give(kv_ref.at[i], kv_out.at[i])
        give(q_ref.at[i], q_out.at[i])
    give(n_out, n_far)
    for copy in sent:
        copy.wait()


def turn_heads(y, cosine, sine, scale):
    lane = lax.broadcasted_iota(jnp.int32, y.shape, 1)
    other = jnp.where(lane % 64 < 32, pltpu.roll(y, WIDE - 32, 1), pltpu.roll(y, 32, 1))
    low = lanes(cosine.shape[0]) < 64
    cosines = [cosine, jnp.where(low, cosine, 1.0), jnp.ones_like(cosine), cosine * scale, cosine * scale]
    none = jnp.zeros_like(sine)
    sines = [sine, jnp.where(low, sine, 0.0), none, sine * scale, sine * scale]
    return y * jnp.concatenate(cosines, axis=1) + other * jnp.concatenate(sines, axis=1)


def project(meta, w, rows, cosine, sine):
    return pl.pallas_call(
        project_kernel,
        out_shape=(
            sds((4, 128, 256)), sds((4, 128, 384)), sds((D, WIDE)), sds((4, 128, D)), sds((8, D), F32),
        ),
        in_specs=[SM] + [AN] * 8,
        out_specs=(AN, AN, AN, AN, VM),
        scratch_shapes=[
            pltpu.VMEM((1024, WIDE), BF),
            pltpu.VMEM((2, 512, WIDE), BF),
            pltpu.VMEM((4, 128, D), BF),
            pltpu.VMEM((4, 128, 256), BF),
            pltpu.VMEM((4, 128, 384), BF),
            pltpu.VMEM((D, WIDE), BF),
            pltpu.VMEM((4, 128, D), BF),
            pltpu.VMEM((2, 4, 128, 128), F32),
            pltpu.SemaphoreType.DMA((18,)),
        ],
        compiler_params=pltpu.CompilerParams(vmem_limit_bytes=58 * 2**20),
        cost_estimate=pl.CostEstimate(flops=2 * 10**9, bytes_accessed=4 * 2**20, transcendentals=0),
        name="project",
    )(meta, *w, *rows, cosine, sine)


def project_back_kernel(
    meta, w_ref, n_ref, cos_ref, sin_ref, loss_ref, *refs
):
    outs, (d_scr, g_scr, a_in, b_in, u_scr, g_out, w_in, n_in, turn_in, sems) = refs[8:14], refs[14:]
    targets = [a_in.at[n] for n in range(4)] + [b_in.at[n] for n in range(4)]
    targets = targets + [turn_in.at[0], turn_in.at[1], w_in, n_in]
    sources = (*refs[0:8], cos_ref, sin_ref, w_ref, n_ref)
    landed, fetches = fetch_all(sources, targets, sems)
    cos_ref, sin_ref, w_ref, n_ref = landed[8:12]
    (a0, a1, a2, a3), (b0, b1, b2, b3) = landed[0:4], landed[4:8]
    for fetch in fetches:
        fetch.wait()
    sent = []

    def give(source, n):
        sent.append(pltpu.make_async_copy(source, outs[n], sems.at[12 + n]))
        sent[-1].start()

    keep = jnp.where(lax.broadcasted_iota(jnp.int32, (D, 128), 1) < 64, 1.0, 0.0)
    tail = (w_ref[:, 512:640].astype(F32) * keep).astype(BF)
    w = jnp.concatenate([w_ref[:, 0:512], tail], axis=1)
    for i in range(4):
        dkv = (b0[i].astype(F32) + b2[i].astype(F32)) + (b1[i].astype(F32) + b3[i].astype(F32))
        dq = (a0[i].astype(F32) + a2[i].astype(F32)) + (a1[i].astype(F32) + a3[i].astype(F32))
        dq1 = jnp.where(lanes(128) < 64, dq[:, 128:256], 0.0)
        y = jnp.concatenate([dkv, dq[:, 0:128], dq1], axis=1).astype(BF).astype(F32)
        d = turn_heads(y, cos_ref[i], -sin_ref[i], 0.125).astype(BF)
        d_scr[i * 128 : i * 128 + 128, :] = d
        u_scr[i] = mm(d, w, NT).astype(BF)
        give(u_scr.at[i], i)
    rows = n_ref[...].reshape(512, D)
    g = mm(rows, d_scr[...], TN)
    last = jnp.where(lanes(D) < 64, g[:, 512:640], loss_ref[0:1, :])
    g = jnp.concatenate([g[:, 0:512], last], axis=1).astype(BF)
    g_scr[...] = mm(spread_rows(), g).astype(BF)
    for n, core in enumerate((1 - meta[2], meta[2])):
        for chip in range(16):
            at = pl.multiple_of(64 * chip + 32 * core, 32)
            g_out[n, 32 * chip : 32 * chip + 32, :] = g_scr[pl.ds(at, 32), :]
        give(g_out.at[n], 5 - n)
    for copy in sent:
        copy.wait()


def project_back(meta, w, n, cosine, sine, loss_row, dq, dkv):
    outs = pl.pallas_call(
        project_back_kernel,
        out_shape=(sds((128, D)),) * 4 + (sds((512, WIDE)),) * 2,
        in_specs=[SM] + [AN] * 4 + [VM] + [AN] * 8,
        out_specs=(AN,) * 6,
        scratch_shapes=[
            pltpu.VMEM((512, WIDE), BF),
            pltpu.VMEM((1024, WIDE), BF),
            pltpu.VMEM((4, 4, 128, 256), BF),
            pltpu.VMEM((4, 4, 128, 384), BF),
            pltpu.VMEM((4, 128, D), BF),
            pltpu.VMEM((2, 512, WIDE), BF),
            pltpu.VMEM((D, WIDE), BF),
            pltpu.VMEM((4, 128, D), BF),
            pltpu.VMEM((2, 4, 128, 128), F32),
            pltpu.SemaphoreType.DMA((18,)),
        ],
        compiler_params=pltpu.CompilerParams(vmem_limit_bytes=58 * 2**20),
        cost_estimate=pl.CostEstimate(flops=2 * 10**9, bytes_accessed=6 * 2**20, transcendentals=0),
        name="project_back",
    )(meta, w, n, cosine, sine, loss_row, *dq, *dkv)
    return outs[0:4], outs[4], outs[5]


PACKED = 2 * FF + FF + 3 * D + 1024


A_ROWS, B_ROWS = 384 + 144, 384 + 384


def weights_back_kernel(meta, own, oth, *refs):
    ix, iz, ic = meta[0], meta[1], meta[2]
    a_refs, b_refs = [refs[0].at[k] for k in range(4)], refs[1:5]
    n_t, m_t, h_t, left, rows, held, sems = refs[5:]
    (own, oth), fetches = fetch_all((own, oth), [held.at[0], held.at[1]], sems)
    for fetch in fetches:
        fetch.wait()
    for k, ref in enumerate((own, oth)):
        at = slice(128 * k, 128 * k + 128)
        n_t[:, at] = ref[:, 3 * FF : 3 * FF + D].astype(F32).T
        h_t[:, at] = ref[:, 2 * FF : 3 * FF].T
        for g in range(4):
            first = 3 * FF + 3 * D + 256 * g
            m_t[192 * g : 192 * g + 192, at] = ref[:, first : first + 256].astype(F32).T[64:256, :]
        rows[at, :] = ref[:, 3 * FF + D : 3 * FF + 3 * D]

    def chips(x_outer):
        for m in range(16):
            yield m, m if x_outer else ((ix - m % 4) & 3) * 4 + ((iz - m // 4) & 3)

    def collect(source, x_outer):
        for m, chip in chips(x_outer):
            left[24 * m : 24 * m + 24, :] = source[pl.ds(pl.multiple_of(48 * chip + 24 * ic, 8), 24), :]
        return left[...].astype(BF)

    def collect_hidden(x_outer):
        picked = [
            h_t[pl.ds(pl.multiple_of(128 * chip + 64 * ic, 64), 64), :] for _, chip in chips(x_outer)
        ]
        return jnp.concatenate(picked, axis=0)

    def put(part, outs, at, height):
        for m in range(16):
            block = part[height * m : height * m + height]
            both = jnp.concatenate([block[:, 0:128], block[:, 128:256]], axis=0)
            outs[m // 4][m % 4, pl.ds(at, 2 * height), :] = both.astype(BF)

    def columns(first, k):
        at = pl.ds(pl.multiple_of(first + 256 * k, 256), 256)
        return jnp.concatenate([own[:, at], oth[:, at]], axis=0)

    for outs, first, x_outer in ((a_refs, 0, True), (b_refs, FF, False)):
        features = collect(n_t, x_outer)

        def gate_or_up(k, _):
            put(mm(features, columns(first, k)), outs, pl.multiple_of(48 * k, 48), 24)
            return 0

        lax.fori_loop(0, 8, gate_or_up, 0)
    outer, down = collect(m_t, True), collect_hidden(False)
    for k in range(3):
        put(mm(outer, rows[:, D + 256 * k : D + 256 * k + 256]), a_refs, 384 + 48 * k, 24)
        put(mm(down, rows[:, 256 * k : 256 * k + 256]), b_refs, 384 + 128 * k, 64)


def weights_back(meta, own, oth):
    outs = pl.pallas_call(
        weights_back_kernel,
        out_shape=(sds((4, 4, A_ROWS, 128)),) + (sds((4, B_ROWS, 128)),) * 4,
        in_specs=[SM, AN, AN],
        out_specs=(VM,) * 5,
        scratch_shapes=[
            pltpu.VMEM((D, 256), F32),
            pltpu.VMEM((D, 256), F32),
            pltpu.VMEM((FF, 256), BF),
            pltpu.VMEM((384, 256), F32),
            pltpu.VMEM((256, 2 * D), BF),
            pltpu.VMEM((2, 128, PACKED), BF),
            pltpu.SemaphoreType.DMA((2,)),
        ],
        compiler_params=pltpu.CompilerParams(vmem_limit_bytes=58 * 2**20),
        cost_estimate=pl.CostEstimate(flops=5 * 10**9, bytes_accessed=10 * 2**20, transcendentals=0),
        name="weights_back",
    )(meta, own, oth)
    return outs[0], outs[1:5]


def middle_kernel(
    meta, pay, tok_ref, teach_ref, gains, w_out, w_pack, w_down,
    out_ref, sq_ref, pack_out, gm_ref, pay_far,
    gu_scr, o_scr, lse_scr, w_gu, pay_in, out_in, down_in, pack_ref, pay_out, sems,
):
    sources = [pay.at[pl.ds(4 * g, 4)] for g in range(4)] + [w_out, w_pack.at[:, 0 : 2 * FF], w_down]
    targets = [pay_in.at[pl.ds(4 * g, 4)] for g in range(4)] + [out_in, w_gu, down_in]
    _, fetches = fetch_all(sources, targets, sems)
    pay, w_out, w_down = pay_in, out_in, down_in
    sent = []

    def give(source, target):
        sent.append(pltpu.make_async_copy(source, target, sems.at[7 + len(sent)]))
        sent[-1].start()

    spread = spread_rows()
    lane = lanes(128)
    middle = tok_ref[...].astype(F32)
    for g in range(4):
        fetches[g].wait()
        if g == 0:
            fetches[4].wait()
        tiles = [pay[g * 4 + y].astype(F32) for y in range(4)]
        logs = [t[:, 0:128] for t in tiles]
        logs = [t + (pltpu.roll(t, 125, 1) + pltpu.roll(t, 122, 1)) for t in logs]
        logs = [jnp.where(lane < 3, v, 0.0) for v in logs]
        top = jnp.maximum(jnp.maximum(logs[0], logs[1]), jnp.maximum(logs[2], logs[3]))
        shares = [jnp.exp(v - top) for v in logs]
        mass = (shares[0] + shares[1]) + (shares[2] + shares[3])
        o0 = o1 = None
        for t, share in zip(tiles, shares):
            w = share / mass
            p0 = t[:, 0:128] * w[:, 0:1]
            p1 = t[:, 128:256] * jnp.where(lane < 64, w[:, 1:2], w[:, 2:3])
            o0 = p0 if o0 is None else o0 + p0
            o1 = p1 if o1 is None else o1 + p1
        o0 = jnp.where(lane < 64, 0.0, o0)
        lse_scr[g] = top + jnp.log(mass)
        o = jnp.concatenate([o0, o1], axis=1)
        o_scr[g] = o
        pack_ref[:, 3 * FF + 3 * D + 256 * g : 3 * FF + 3 * D + 256 * g + 256] = o.astype(BF)
        middle = middle + mm(o.astype(BF), w_out[192 * g : 192 * g + 256, :])
    r2 = lax.rsqrt(jnp.mean(middle * middle, axis=1, keepdims=True) + EPSILON)
    n2 = middle * r2
    n2b = (n2 * gains[1:2, :]).astype(BF)
    pack_ref[:, 3 * FF : 3 * FF + D] = n2b
    n2p = mm(n2b, spread, NT).astype(BF)
    fetches[5].wait()
    for f in range(4):
        at, up_at = slice(512 * f, 512 * f + 512), slice(FF + 512 * f, FF + 512 * f + 512)
        gate = mm(n2p, w_gu[:, at])
        up = mm(n2p, w_gu[:, up_at])
        gu_scr[:, at] = gate
        gu_scr[:, up_at] = up
        hid = (gate / (1.0 + jnp.exp(-gate)) * up).astype(BF)
        pack_ref[:, 2 * FF + 512 * f : 2 * FF + 512 * f + 512] = hid
    fetches[6].wait()
    total = middle + mm(pack_ref[:, 2 * FF : 3 * FF], w_down[...])
    out_ref[...] = total.astype(BF)
    row = lax.broadcasted_iota(jnp.int32, (128, D), 0)
    mine = meta[0] * 4096 + meta[1] * 1024 + meta[2] * 512 + meta[3] * 128
    diff = jnp.where(row < meta[8] - mine, total - teach_ref[...].astype(F32), 0.0)
    square = diff * diff
    square = sum(square[:, 128 * n : 128 * n + 128] for n in range(6))
    square = jnp.sum(square, axis=0, keepdims=True)
    sq_ref[...] = jnp.broadcast_to(square + pltpu.roll(square, 64, 1), (8, 128))
    g = diff * (16384.0 / jnp.full((1, D), meta[8], jnp.int32).astype(F32))
    gb = g.astype(BF)
    pack_ref[:, 3 * FF + D : 3 * FF + 2 * D] = gb
    give(pack_ref.at[:, 2 * FF : 3 * FF + 2 * D], pack_out.at[:, 2 * FF : 3 * FF + 2 * D])
    give(pack_ref.at[:, 3 * FF + 3 * D : PACKED], pack_out.at[:, 3 * FF + 3 * D : PACKED])
    u = jnp.zeros((128, 1024), F32)
    for f in range(4):
        at, up_at = slice(512 * f, 512 * f + 512), slice(FF + 512 * f, FF + 512 * f + 512)
        gate, up = gu_scr[:, at], gu_scr[:, up_at]
        dh = mm(gb, w_down[at, :], NT)
        sig = 1.0 / (1.0 + jnp.exp(-gate))
        dgate = (dh * up * sig * (1.0 + gate * (1.0 - sig))).astype(BF)
        dup = (dh * gate * sig).astype(BF)
        pack_ref[:, at] = dgate
        pack_ref[:, up_at] = dup
        u = u + mm(dgate, w_gu[:, at], NT) + mm(dup, w_gu[:, up_at], NT)
    give(pack_ref.at[:, 0 : 2 * FF], pack_out.at[:, 0 : 2 * FF])
    u_hi, u_rest = split_two(u)
    u_mid, u_low = split_two(u_rest)
    u = mm(u_hi.astype(BF), spread) + (mm(u_mid.astype(BF), spread) + mm(u_low.astype(BF), spread))
    u = u * gains[1:2, :]
    gm = g + r2 * (u - n2 * jnp.mean(u * n2, axis=1, keepdims=True))
    gm_ref[...] = gm
    gmb = gm.astype(BF)
    pack_ref[:, 3 * FF + 2 * D : 3 * FF + 3 * D] = gmb
    give(pack_ref.at[:, 3 * FF + 2 * D : 3 * FF + 3 * D], pack_out.at[:, 3 * FF + 2 * D : 3 * FF + 3 * D])
    for k in range(4):
        dm = mm(gmb, w_out[192 * k : 192 * k + 256, :], NT).astype(BF)
        d0, d1 = dm[:, 0:128].astype(F32), dm[:, 128:256].astype(F32)
        p0, p1 = d0 * o_scr[k, :, 0:128], d1 * o_scr[k, :, 128:256]
        deltas = [
            jnp.sum(p0, axis=1, keepdims=True),
            jnp.sum(jnp.where(lane < 64, p1, 0.0), axis=1, keepdims=True),
            jnp.sum(jnp.where(lane < 64, 0.0, p1), axis=1, keepdims=True),
        ]
        hi, lo, lowest = split_three(-lse_scr[k])
        delta = jnp.where(lane == 0, deltas[0], jnp.where(lane == 1, deltas[1], deltas[2]))
        dhi, dlo = split_two(-delta)
        aug = jnp.where(lane < 3, hi, jnp.where(lane < 6, pltpu.roll(lo, 3, 1), 0.0))
        aug = jnp.where((lane >= 6) & (lane < 9), pltpu.roll(dhi, 6, 1), aug)
        aug = jnp.where((lane >= 9) & (lane < 12), pltpu.roll(dlo, 9, 1), aug)
        aug = jnp.where((lane >= 12) & (lane < 15), pltpu.roll(lowest, 12, 1), aug)
        d0 = jnp.where(lane < 64, aug, d0).astype(BF)
        for y in range(4):
            pay_out[4 * k + y, :, 0:128] = d0
            pay_out[4 * k + y, :, 128:256] = dm[:, 128:256]
        give(pay_out.at[pl.ds(4 * k, 4)], pay_far.at[pl.ds(4 * k, 4)])
    for copy in sent:
        copy.wait()


def middle_part(meta, pay, tokens, teacher, gains, w_out, w_gu, w_down):
    return pl.pallas_call(
        middle_kernel,
        out_shape=(
            sds((128, D)), sds((8, 128), F32), sds((128, PACKED)), sds((128, D), F32), sds((16, 128, 256)),
        ),
        in_specs=[SM, AN] + [VM] * 3 + [AN] * 3,
        out_specs=(VM, VM, AN, VM, AN),
        scratch_shapes=[
            pltpu.VMEM((128, 2 * FF), F32),
            pltpu.VMEM((4, 128, 256), F32),
            pltpu.VMEM((4, 128, 128), F32),
            pltpu.VMEM((1024, 2 * FF), BF),
            pltpu.VMEM((16, 128, 256), BF),
            pltpu.VMEM((832, D), BF),
            pltpu.VMEM((FF, D), BF),
            pltpu.VMEM((128, PACKED), BF),
            pltpu.VMEM((16, 128, 256), BF),
            pltpu.SemaphoreType.DMA((15,)),
        ],
        compiler_params=pltpu.CompilerParams(vmem_limit_bytes=58 * 2**20),
        cost_estimate=pl.CostEstimate(flops=3 * 10**9, bytes_accessed=16 * 2**20, transcendentals=10**6),
        name="middle_part",
    )(meta, pay, tokens, teacher, gains, w_out, w_gu, w_down)


def finish_kernel(meta, g_ref, wq, wk, wv, gain, q_out, k_out, v_out, ga_out, loss_out):
    total, tail = None, None
    for x in range(4):
        part = g_ref[16 * x].astype(F32)
        for n in range(1, 16):
            part = part + g_ref[16 * x + n].astype(F32)
        lane = lax.broadcasted_iota(jnp.int32, (8, 128), 1)
        none = jnp.zeros((8, 512), F32)
        kv1 = part[:, 128:256]
        keys = [part[:, 0:128], jnp.where(lane < 64, kv1, 0.0)]
        values = [jnp.where(lane < 64, 0.0, kv1), part[:, 256:384]]
        last = part[:, 512:640]
        queries = [part[:, 384:512], jnp.where(lane < 64, last, 0.0)]
        wide = [jnp.concatenate(t + [none], axis=1) for t in (keys, values, queries)]
        shifts = (192 * x, (192 * x - 64) % D, 192 * x)
        wide = [pltpu.roll(a, s, 1) if s else a for a, s in zip(wide, shifts)]
        total = wide if total is None else [a + b for a, b in zip(total, wide)]
        tail = last if tail is None else tail + last
    keys, values, queries = total
    q_out[...], k_out[...], v_out[...] = queries[0:6], keys[0:6], values[0:6]
    by_row = keys[0:6] * wk[...].astype(F32) + values[0:6] * wv[...].astype(F32)
    by_row = by_row + queries[0:6] * wq[...].astype(F32)
    rows = jnp.sum(by_row, axis=1, keepdims=True)
    row = lax.broadcasted_iota(jnp.int32, (6, 128), 0)
    lane = lax.broadcasted_iota(jnp.int32, (6, 128), 1)
    across = jnp.sum(jnp.where(row == lane, rows, 0.0), axis=0, keepdims=True)
    ga_out[...] = across[:, 0:6] / gain[...].astype(F32)
    counted = jnp.full((1, 128), meta[8], jnp.int32).astype(F32)
    high = lax.broadcasted_iota(jnp.int32, (1, 128), 1) >= 64
    loss = jnp.sum(jnp.where(high, tail[0:1, :], 0.0), axis=1, keepdims=True)
    loss_out[...] = jnp.broadcast_to(loss / (counted * D), (1, 128))


def finish(meta, g, wq, wk, wv, gain):
    return pl.pallas_call(
        finish_kernel,
        out_shape=(sds((6, D), F32),) * 3 + (sds((1, 6), F32), sds((1, 128), F32)),
        in_specs=[SM] + [VM] * 5,
        out_specs=(VM,) * 5,
        cost_estimate=pl.CostEstimate(flops=10**6, bytes_accessed=10**6, transcendentals=0),
        name="finish",
    )(meta, g, wq, wk, wv, gain.reshape(1, 6))


def from_behind(x, axis, j):
    return lax.ppermute(x, axis, [(s, (s + j) % 4) for s in range(4)])


def from_ahead(x, axis, j):
    return lax.ppermute(x, axis, [(s, (s - j) % 4) for s in range(4)])


def from_core(x):
    return lax.ppermute(x, C, [(0, 1), (1, 0)])


def gather4(x, axis):
    return [x] + [from_behind(x, axis, j) for j in (1, 2, 3)]


def in_order(blocks, index, dim):
    r0, r1, r2, r3 = blocks
    twice = jnp.concatenate([r3, r2, r1, r0, r3, r2, r1], axis=dim)
    size = r0.shape[dim]
    return lax.dynamic_slice_in_dim(twice, (3 - index) * size, 4 * size, dim)


def block_of(x, index):
    return lax.dynamic_index_in_dim(x, index, 0, keepdims=False)


def scatter4(x, axis, index):
    own = block_of(x, index).astype(F32)
    far = [from_ahead(block_of(x, (index - j) & 3), axis, j).astype(F32) for j in (1, 2, 3)]
    return (own + far[1]) + (far[0] + far[2])


def summed(parts):
    a, b, c, d = (p.astype(F32) for p in parts)
    return (a + c) + (b + d)


def per_device(
    tokens, attn_gain, w_query, w_key, w_value, w_out, mlp_gain, w_gate, w_up, w_down, segments, teacher
):
    ix, iz, ic, iy = (lax.axis_index(a) for a in (X, Z, C, Y))
    begin = iz * 1024 + ic * 512

    heads, pack = prepare(
        w_query, w_key, w_value, attn_gain, mlp_gain, w_gate, w_up, w_out, w_down
    )
    pack = lax.all_gather(pack, BLK_HD)
    w_rows = lax.all_to_all(heads, (X, Z, Y), split_axis=0, concat_axis=0, tiled=True)
    w_rows = w_rows.reshape(512, WIDE)
    t_rows = gather4(tokens, X)

    place = jnp.where(
        jnp.arange(4) == 0, ix, jnp.where(jnp.arange(4) == 1, iz, jnp.where(jnp.arange(4) == 2, ic, iy))
    ).astype(jnp.int32)
    meta, lab = documents(place, segments.reshape(128, 128))

    exponents = jnp.arange(32, dtype=jnp.float32) * (-2.0 / HEAD_SIZE)
    frequency = jnp.tile(ROPE_BASE**exponents, 4)
    runs = ((ix - jnp.arange(4, dtype=jnp.int32)) & 3) * 4096
    places = runs[:, None] + begin + iy * 128 + jnp.arange(128, dtype=jnp.int32)[None]
    angles = places.astype(F32)[:, :, None] * frequency[None, None, :]
    cosine = jnp.cos(angles)
    sine = jnp.sin(angles) * jnp.where(jnp.arange(128) % 64 < 32, -1.0, 1.0)

    w_rows, t_rows, cosine, sine, meta, lab = lax.optimization_barrier(
        (w_rows, t_rows, cosine, sine, meta, lab)
    )
    w_rows = [w_rows, from_core(w_rows)]
    q, kv, w_full, n_rows, gain_rows = project(meta, w_rows, t_rows, cosine, sine)
    q_all, kv_own = gather4(q, Y), gather4(kv, Z)
    q_all, kv_own = lax.optimization_barrier((q_all, kv_own))
    kv_oth = [from_core(kv) for kv in kv_own]

    pay = attend(meta, lab, q_all, kv_own, kv_oth).reshape(16, 128, 256)
    pay = lax.all_to_all(pay, (X, Y), split_axis=0, concat_axis=0, tiled=True)
    w_out_all = jnp.pad(pack[:, :6, 4096:4864].reshape(D, D), ((64, 0), (0, 0)))
    w_down_all = pack[:, :, 4864:].reshape(128, 8, 2, D).transpose(0, 2, 1, 3).reshape(FF, D)
    out, squares, packed, grad_middle, dpay = middle_part(
        meta, pay, tokens, teacher, gain_rows, w_out_all, pack.reshape(1024, -1), w_down_all
    )
    dout = lax.all_to_all(dpay, (X, Y), split_axis=0, concat_axis=0, tiled=True)

    part_a, part_b = weights_back(meta, packed, from_core(packed))
    dout, _, _ = lax.optimization_barrier((dout, part_a, part_b))
    part_a = lax.psum_scatter(part_a.reshape(-1, 128), X, scatter_dimension=0, tiled=True)
    part_a = lax.psum_scatter(part_a, Z, scatter_dimension=0, tiled=True)
    far_b = [from_ahead(part_b[j], Z, j) for j in (1, 2, 3)]

    dq, dkv_own, dkv_oth = attend_back(
        meta, lab, q_all, kv_own, kv_oth, dout.reshape(4, 4, 128, 256)
    )
    dq, dkv_own, dkv_oth, far_b = lax.optimization_barrier((dq, dkv_own, dkv_oth, far_b))
    dq = [dq[0]] + [from_ahead(dq[j], Y, j) for j in (1, 2, 3)]
    dkv_oth = from_core(dkv_oth)
    dkv = [(dkv_own[j].astype(F32) + dkv_oth[j].astype(F32)).astype(BF) for j in range(4)]
    dkv, far_b = lax.optimization_barrier((dkv, far_b))
    dkv = [dkv[0]] + [from_ahead(dkv[j], Z, j) for j in (1, 2, 3)]
    part_b = summed([part_b[0]] + far_b).astype(BF)
    far_b = [from_ahead(part_b[j], X, j) for j in (1, 2, 3)]
    dq, dkv, far_b, part_a = lax.optimization_barrier((dq, dkv, far_b, part_a))
    part_b = summed([part_b[0]] + far_b).astype(BF)
    u, keep, send = project_back(meta, w_full, n_rows, cosine, sine, squares, dq, dkv)

    gu = jnp.concatenate([part_a[:384], part_b[:384]]).reshape(32, 4, 6, 128)
    gu = gu.transpose(1, 0, 2, 3).reshape(4, 192, 128)
    down = part_b[384:].reshape(6, 4, 16, 128)
    down = down.transpose(1, 0, 2, 3).reshape(4, 96, 128)
    outer = part_a[384:].reshape(6, 4, 6, 128).transpose(1, 0, 2, 3).reshape(4, 36, 128)
    grads = jnp.concatenate([gu, down, outer], axis=1)
    own_grads = block_of(grads, iy)
    far_grads = [from_ahead(block_of(grads, (iy - j) & 3), Y, j) for j in (1, 2, 3)]
    far_u = [from_ahead(u[j], X, j) for j in (1, 2, 3)]
    g = (keep.astype(F32) + from_core(send).astype(F32)).astype(BF).reshape(64, 8, WIDE)
    g = lax.all_to_all(g, (X, Z, Y), split_axis=0, concat_axis=0, tiled=True)
    g, far_grads = lax.optimization_barrier((g, far_grads))
    grads = summed([own_grads] + far_grads)

    u = summed([u[0]] + far_u) * gain_rows[0:1]
    wide = tokens.astype(F32)
    r1 = lax.rsqrt(jnp.mean(wide * wide, axis=1, keepdims=True) + EPSILON)
    n1 = wide * r1
    grad_tokens = grad_middle + r1 * (u - n1 * jnp.mean(u * n1, axis=1, keepdims=True))

    grad_query, grad_key, grad_value, grad_attn_gain, mean_loss = finish(
        meta, g, w_query, w_key, w_value, attn_gain
    )
    mean_loss, grad_attn_gain = mean_loss[0, 0], grad_attn_gain.reshape(6)

    gu = grads[:192].reshape(32, 6, 128).transpose(1, 0, 2).reshape(6, 2 * FF)
    down = grads[192:288].reshape(6, 16, 128).transpose(1, 0, 2).reshape(16, D)
    outer = grads[288:].reshape(6, 6, 128).transpose(1, 0, 2).reshape(6, D)
    grad_gate, grad_up = gu[:, :FF], gu[:, FF:]
    by_row = grad_gate * w_gate.astype(F32) + grad_up * w_up.astype(F32)
    grad_mlp_gain = jnp.sum(by_row, axis=1) / mlp_gain.astype(F32)
    return (
        out,
        grad_tokens.astype(BF),
        mean_loss,
        grad_attn_gain,
        grad_query,
        grad_key,
        grad_value,
        outer,
        grad_mlp_gain,
        grad_gate,
        grad_up,
        down,
    )


def solution(mesh):
    torus = Mesh(mesh.devices.reshape(4, 4, 2, mesh.shape["hd"]), BLK_HD)
    rows, vector = P(BLK_HD, None), P(BLK_HD)
    return jax.shard_map(
        per_device,
        mesh=torus,
        in_specs=(rows, vector, rows, rows, rows, rows, vector, rows, rows, rows, P(), rows),
        out_specs=(rows, rows, P(), vector, rows, rows, rows, rows, vector, rows, rows, rows),
        check_vma=False,
    )
```
